32 devices in a mesh: dp: 4 (over z), tr: 4 (over x, core), tc: 2 (over y).
Axes of the slice: x: 2, y: 2, z: 4, core: 2. Of those that a mesh axis runs over, the one named last changes fastest.
Arguments:
- layer_input: bfloat16 [8192, 1152], P(('dp', 'tr'), 'tc'), may hold values from -6 to 6
- picture: int32 [8192], P('dp'), may hold values from 0 to 7, as said below
- token_kept: int32 [8192], P('dp'), may hold values from 0 to 1, as said below
- ln1_gain: float32 [1152], P('tc'), may hold values from 0.5 to 1.5
- ln1_bias: float32 [1152], P('tc'), may hold values from -1.75 to 1.75
- w_query: bfloat16 [1152, 1152], P('tc', 'tr'), may hold values from -0.1875 to 0.1875
- b_query: float32 [1152], P(('tr', 'tc')), may hold values from -3 to 3
- w_key: bfloat16 [1152, 1152], P('tc', 'tr'), may hold values from -0.1875 to 0.1875
- w_value: bfloat16 [1152, 1152], P('tc', 'tr'), may hold values from -0.1875 to 0.1875
- b_value: float32 [1152], P(('tr', 'tc')), may hold values from -0.3125 to 0.3125
- w_out: bfloat16 [1152, 1152], P('tr', 'tc'), may hold values from -3 to 3
- b_out: float32 [1152], P('tc'), may hold values from -1.75 to 1.75
- ln2_gain: float32 [1152], P('tc'), may hold values from 0.5 to 1.5
- ln2_bias: float32 [1152], P('tc'), may hold values from -1.75 to 1.75
- w_up: bfloat16 [1152, 4304], P('tc', 'tr'), may hold values from -0.1875 to 0.1875
- b_up: float32 [4304], P(('tr', 'tc')), may hold values from -3 to 3
- w_down: bfloat16 [4304, 1152], P('tr', 'tc'), may hold values from -0.09375 to 0.09375
- b_down: float32 [1152], P('tc'), may hold values from -1.75 to 1.75
- grad_out: bfloat16 [8192, 1152], P(('dp', 'tr'), 'tc'), may hold values from -6 to 6
Outputs:
- result: bfloat16 [8192, 1152], P(('dp', 'tr'), 'tc')
- grad_layer_input: bfloat16 [8192, 1152], P(('dp', 'tr'), 'tc')
- grad_ln1_gain: float32 [1152], P('tc')
- grad_ln1_bias: float32 [1152], P('tc')
- grad_w_query: float32 [1152, 1152], P('tc', 'tr')
- grad_b_query: float32 [1152], P(('tr', 'tc'))
- grad_w_key: float32 [1152, 1152], P('tc', 'tr')
- grad_w_value: float32 [1152, 1152], P('tc', 'tr')
- grad_b_value: float32 [1152], P(('tr', 'tc'))
- grad_w_out: float32 [1152, 1152], P('tr', 'tc')
- grad_b_out: float32 [1152], P('tc')
- grad_ln2_gain: float32 [1152], P('tc')
- grad_ln2_bias: float32 [1152], P('tc')
- grad_w_up: float32 [1152, 4304], P('tc', 'tr')
- grad_b_up: float32 [4304], P(('tr', 'tc'))
- grad_w_down: float32 [4304, 1152], P('tr', 'tc')
- grad_b_down: float32 [1152], P('tc')
The draws below stay inside these ranges and needn't reach their ends.
Inputs may be any that keep to these rules, and one draw needn't show every extreme that they name: Within each packed row of 2048 tokens the picture numbers run 0 to 7 in order, each picture a contiguous run. `token_kept`: padding stands at the end of each packed row, at least one token and at most 128 of them, inside the row's last picture.
All inputs are finite; a program needn't handle non-finite values.
Results may differ from the reference program's by a relative error of at most 0.015.
Values may be sent and summed in bfloat16 or wider, within the bound.
No kernel may reach another device: no remote copies, remote signals or barrier semaphores. Data moves between devices by JAX's collectives and lax.ppermute only.
A program may use at most 128 MiB of HBM per device.

```python
import jax
import jax.numpy as jnp
from jax import lax

D = 1152
H = 16
DH = 72
FF = 4304
SEQ = 2048
PICS = 8
HD = 1152
BLOCK = 512
TOKENS = 8192


def draw_picture(key, part):
    key = jax.random.fold_in(key, 11)
    row_count = TOKENS // SEQ
    jitter = SEQ // (4 * PICS)
    cuts = jnp.arange(1, PICS, dtype=jnp.int32) * (SEQ // PICS)
    cuts = cuts[None, :] + jax.random.randint(key, (row_count, PICS - 1), -jitter, jitter + 1)
    places = jnp.arange(SEQ, dtype=jnp.int32)
    labels = jnp.sum((places[None, :, None] >= cuts[:, None, :]).astype(jnp.int32), axis=2)
    return labels.reshape(TOKENS).astype(jnp.int32)


def draw_token_kept(key, part):
    key = jax.random.fold_in(key, 23)
    row_count = TOKENS // SEQ
    padded = jax.random.randint(key, (row_count, 1), 1, SEQ // (2 * PICS) + 1)
    places = jnp.arange(SEQ, dtype=jnp.int32)
    return (places[None, :] < SEQ - padded).astype(jnp.int32).reshape(TOKENS)


def shard_levels(key, dims, shards, smallest, high):
    gain = 1.0
    for position, blocks in shards:
        steps = jax.random.uniform(jax.random.fold_in(jax.random.fold_in(key, 6), position), (blocks,), jnp.float32, smallest / len(shards), high / len(shards))
        gain = gain * jnp.repeat(jnp.exp(steps), dims[position] // blocks).reshape((-1,) + (1,) * (len(dims) - 1 - position))
    return gain


def normal_values(key, extent, scale, limit, split=(), kind=jnp.bfloat16):
    values = scale * jax.random.normal(key, extent, jnp.float32)
    if split:
        values = values * shard_levels(key, extent, split, -0.22, 0.18)
    return jnp.clip(values, -limit, limit).astype(kind)


def setup_inputs(seed: int = 0) -> dict:
    arg_keys = jax.random.split(jax.random.key(seed), 20)
    return {
        "layer_input": normal_values(arg_keys[0], (TOKENS, D), 1.0, 6.0, ((0, 16), (1, 2))),
        "picture": draw_picture(jax.random.fold_in(arg_keys[19], 71), 0),
        "token_kept": draw_token_kept(jax.random.fold_in(arg_keys[19], 71), 0),
        "ln1_gain": jnp.clip(1.0 + 0.1 * jax.random.normal(arg_keys[3], (D,), jnp.float32), 0.5, 1.5),
        "ln1_bias": normal_values(arg_keys[4], (D,), 0.3, 1.75, ((0, 2),), jnp.float32),
        "w_query": normal_values(arg_keys[5], (D, HD), D ** -0.5, 0.1875, ((0, 2), (1, 4))),
        "b_query": normal_values(arg_keys[6], (HD,), 0.5, 3.0, ((0, 8),), jnp.float32),
        "w_key": normal_values(arg_keys[7], (D, HD), D ** -0.5, 0.1875, ((0, 2), (1, 4))),
        "w_value": normal_values(arg_keys[8], (D, HD), D ** -0.5, 0.1875, ((0, 2), (1, 4))),
        "b_value": normal_values(arg_keys[9], (HD,), 0.05, 0.3125, ((0, 8),), jnp.float32),
        "w_out": normal_values(arg_keys[10], (HD, D), (max(HD * PICS // SEQ, 1)) ** -0.5, 3.0, ((0, 4), (1, 2))),
        "b_out": normal_values(arg_keys[11], (D,), 0.3, 1.75, ((0, 2),), jnp.float32),
        "ln2_gain": jnp.clip(1.0 + 0.1 * jax.random.normal(arg_keys[12], (D,), jnp.float32), 0.5, 1.5),
        "ln2_bias": normal_values(arg_keys[13], (D,), 0.3, 1.75, ((0, 2),), jnp.float32),
        "w_up": normal_values(arg_keys[14], (D, FF), D ** -0.5, 0.1875, ((0, 2), (1, 4))),
        "b_up": normal_values(arg_keys[15], (FF,), 0.5, 3.0, ((0, 8),), jnp.float32),
        "w_down": normal_values(arg_keys[16], (FF, D), FF ** -0.5, 0.09375, ((0, 4), (1, 2))),
        "b_down": normal_values(arg_keys[17], (D,), 0.3, 1.75, ((0, 2),), jnp.float32),
        "grad_out": normal_values(arg_keys[18], (TOKENS, D), 1.0, 6.0, ((0, 16), (1, 2))),
    }


@jax.custom_vjp
def low(v):
    return lax.optimization_barrier(v.astype(jnp.bfloat16)).astype(jnp.float32)

@jax.custom_vjp
def low_back(v):
    return v

def low_keep(v):
    return (low(v), None)

def low_pass(kept, grad):
    return (grad,)

def back_keep(v):
    return (v, None)

def back_low(kept, grad):
    return (low(grad),)
low.defvjp(low_keep, low_pass)
low_back.defvjp(back_keep, back_low)
EPSILON = 1e-06
GELU_C = 0.7978845608028654
GELU_A = 0.044715
MASKED = -1e+30

def product(left, right):
    return jnp.dot(left, right, precision=lax.Precision.HIGHEST, preferred_element_type=jnp.float32)

def norm_rows(values, gains, biases):
    means = lax.optimization_barrier(jnp.mean(values, axis=1, keepdims=True))
    spread = lax.optimization_barrier(jnp.mean(values * values, axis=1, keepdims=True)) - means * means
    return (values - means) * lax.rsqrt(spread + EPSILON) * gains + biases

def gelu_tanh(upper):
    return 0.5 * upper * (1.0 + jnp.tanh(GELU_C * (upper + GELU_A * upper * upper * upper)))

def attend_block(query_block, key_rows, value_rows, picture_query, picture_row, kept_row, query_offset):
    raw = jnp.einsum('qhd,khd->hqk', query_block, key_rows, precision=lax.Precision.HIGHEST)
    scores = low_back(raw * DH ** (-0.5))
    query_places = query_offset + jnp.arange(BLOCK, dtype=jnp.int32)
    key_places = jnp.arange(SEQ, dtype=jnp.int32)
    same = (picture_query[:, None] == picture_row[None, :]) & (kept_row[None, :] == 1)
    allowed = same | (query_places[:, None] == key_places[None, :])
    scores = jnp.where(allowed[None], scores, MASKED)
    highest = lax.optimization_barrier(jnp.max(scores, axis=2, keepdims=True))
    weights = jnp.exp(scores - highest)
    probs = low(weights / lax.optimization_barrier(jnp.sum(weights, axis=2, keepdims=True)))
    return jnp.einsum('hqk,khd->qhd', probs, value_rows, precision=lax.Precision.HIGHEST)

def attend_row(row_items):
    queries, keys, values, picture_row, kept_row = row_items
    block_count = SEQ // BLOCK
    query_blocks = queries.reshape(block_count, BLOCK, H, DH)
    picture_blocks = picture_row.reshape(block_count, BLOCK)
    offsets = jnp.arange(block_count, dtype=jnp.int32) * BLOCK

    def one_block(block_items):
        return attend_block(block_items[0], keys, values, block_items[1], picture_row, kept_row, block_items[2])
    attended = lax.map(jax.checkpoint(one_block), (query_blocks, picture_blocks, offsets))
    return attended.reshape(SEQ, H * DH)

def forward(input_rows, ln1_gain, ln1_bias, w_query, b_query, w_key, w_value, b_value, w_out, b_out, ln2_gain, ln2_bias, w_up, b_up, w_down, b_down, picture, token_kept):
    token_count = input_rows.shape[0]
    row_count = token_count // SEQ
    hidden1 = low(norm_rows(input_rows, ln1_gain, ln1_bias))
    queries = low(low_back(product(hidden1, w_query) + b_query))
    keys = low(low_back(product(hidden1, w_key)))
    values = low(low_back(product(hidden1, w_value) + b_value))
    attended = lax.map(attend_row, (queries.reshape(row_count, SEQ, H, DH), keys.reshape(row_count, SEQ, H, DH), values.reshape(row_count, SEQ, H, DH), picture.reshape(row_count, SEQ), token_kept.reshape(row_count, SEQ)))
    heads = low(low_back(attended.reshape(token_count, H * DH)))
    mixed = input_rows + low_back(product(heads, w_out)) + b_out
    hidden2 = low(norm_rows(mixed, ln2_gain, ln2_bias))
    upper = low_back(product(hidden2, w_up) + b_up)
    activated = low(gelu_tanh(upper))
    return mixed + low_back(product(activated, w_down)) + b_down

def reference(layer_input, picture, token_kept, ln1_gain, ln1_bias, w_query, b_query, w_key, w_value, b_value, w_out, b_out, ln2_gain, ln2_bias, w_up, b_up, w_down, b_down, grad_out):
    floats = tuple((array.astype(jnp.float32) for array in (layer_input, ln1_gain, ln1_bias, w_query, b_query, w_key, w_value, b_value, w_out, b_out, ln2_gain, ln2_bias, w_up, b_up, w_down, b_down)))

    def layer(*params):
        return forward(*params, picture, token_kept)
    result, pullback = jax.vjp(layer, *floats)
    grads = pullback(grad_out.astype(jnp.float32))
    return (result.astype(jnp.bfloat16), grads[0].astype(jnp.bfloat16), grads[1], grads[2], grads[3], grads[4], grads[5], grads[6], grads[7], grads[8], grads[9], grads[10], grads[11], grads[12], grads[13], grads[14], grads[15])
```

```python
import functools

import jax
import jax.numpy as jnp
from jax import lax
from jax.experimental import pallas as pl
from jax.experimental.pallas import tpu as pltpu
from jax.sharding import PartitionSpec as P

DH = 72
SUB = 256
EPSILON = 1e-06
GELU_C = 0.7978845608028654
GELU_A = 0.044715
MASKED = -1e30
SCALE = DH**-0.5
SCALE2 = SCALE * 1.4426950408889634
BF = jnp.bfloat16
F32 = jnp.float32
VMEM_BYTES = 56 * 1024 * 1024


def swap_perm(axis, bit):
    return [(i, i ^ bit) for i in range(lax.axis_size(axis))]


def px(v):
    return lax.ppermute(v, "tr", swap_perm("tr", 2))


def pc(v):
    return lax.ppermute(v, "tr", swap_perm("tr", 1))


def py(v):
    return lax.ppermute(v, "tc", swap_perm("tc", 1))


def dot(a, b):
    return jnp.dot(a, b, preferred_element_type=F32)


def dot_tn(a, b):
    return lax.dot_general(a, b, (((0,), (0,)), ((), ())), preferred_element_type=F32)


def dot_nt(a, b):
    return lax.dot_general(a, b, (((1,), (1,)), ((), ())), preferred_element_type=F32)


def rows_at(v, first, count):
    return lax.dynamic_slice_in_dim(v, first, count, 0)


def cols_at(v, first, count):
    return lax.dynamic_slice_in_dim(v, first, count, 1)


def rel_rows(v, ypos):
    half = v.shape[0] // 2
    return jnp.concatenate((rows_at(v, ypos * half, half), rows_at(v, (1 - ypos) * half, half)), 0)


def whole_vmem(n):
    return [pl.BlockSpec(memory_space=pltpu.VMEM)] * n


SMEM_SPEC = pl.BlockSpec(memory_space=pltpu.SMEM)


def params(**kw):
    return pltpu.CompilerParams(vmem_limit_bytes=VMEM_BYTES, **kw)


def norm_qkv_kernel(scal, a00, b00, a01, b01, a10, b10, a11, b11, wa, wb, bias, gain, shift, h_ref, qkv_ref, res_ref):
    ypos = scal[0]
    width = a00.shape[1]
    weights = jnp.concatenate((wa[...], wb[...]), 0)
    sources = {(0, 0): (a00, b00), (1, 0): (a01, b01), (0, 1): (a10, b10), (1, 1): (a11, b11)}
    for rc in range(2):
        for ry in range(2):
            for rx in range(2):
                place = (rc * 4 + ry * 2 + rx) * SUB
                first = pl.multiple_of((ypos ^ ry) * SUB, SUB)
                sa, sb = sources[(rc, rx)]
                raw_a, raw_b = sa[pl.ds(first, SUB), :], sb[pl.ds(first, SUB), :]
                raw = jnp.concatenate((raw_a, raw_b), 1)
                if rc == 0 and ry == 0:
                    res_ref[rx * SUB : (rx + 1) * SUB, :] = raw
                v = raw.astype(F32)
                mean = jnp.sum(v, axis=1, keepdims=True) / (2 * width)
                square = jnp.sum(v * v, axis=1, keepdims=True) / (2 * width)
                root = lax.rsqrt(square - mean * mean + EPSILON)
                hidden = ((v - mean) * root * gain[...] + shift[...]).astype(BF)
                h_ref[place : place + SUB, :] = hidden
                qkv_ref[place : place + SUB, :] = (dot(hidden, weights) + bias[...]).astype(BF)


def spots():
    return [(rc, ry, rx) for rc in range(2) for ry in range(2) for rx in range(2)]


def block_of(me, rc, ry, rx):
    return me ^ (rx * 4 + rc * 2 + ry)


def span(block):
    return pl.ds(pl.multiple_of(block * SUB, SUB), SUB)


def attend_kernel(scal, klo, khi, qkv, lo, hi, o00, o01, o10, o11, lse, ks, qt, vt):
    me = scal[1]
    outs = {(0, 0): o00, (0, 1): o01, (1, 0): o10, (1, 1): o11}
    tail = lax.broadcasted_iota(jnp.int32, (8, vt.shape[2]), 0)
    for h in range(2):
        vt[h, DH:, :] = jnp.where(tail == 0, 1.0, 0.0).astype(BF)
    for p, (rc, ry, rx) in enumerate(spots()):
        rows = span(block_of(me, rc, ry, rx))
        here = slice(p * SUB, (p + 1) * SUB)
        for h in range(2):
            ks[h, rows, :] = qkv[here, 144 + DH * h : 144 + DH * (h + 1)]
        qtile = qkv[here, 0:144].T
        vtile = qkv[here, 288:432].T
        for h in range(2):
            qt[h, :, rows] = qtile[DH * h : DH * (h + 1)]
            vt[h, :DH, rows] = vtile[DH * h : DH * (h + 1)]
    places = lax.broadcasted_iota(jnp.int32, (SUB, SUB), 0)
    lanes = lax.broadcasted_iota(jnp.int32, (1, SUB), 1)
    for rc, ry, rx in spots():
        block = block_of(me, rc, ry, rx)
        cols = span(block)
        low, high = lo[:, cols], hi[:, cols]
        own = lanes + block * SUB

        def body(kb, carry):
            base = kb * SUB
            allowed = ((places >= low - base) & (places < high - base)) | (places == own - base)
            new = []
            for h in range(2):
                top, acc = carry[h]
                s = dot(ks[h, span(kb), :], qt[h, :, cols])
                s = jnp.where(allowed, s, MASKED)
                newtop = jnp.maximum(top, jnp.max(s, axis=0, keepdims=True))
                alpha = jnp.exp2((top - newtop) * SCALE2)
                weights = jnp.exp2((s - newtop) * SCALE2).astype(BF)
                acc = acc * alpha + dot(vt[h, :, span(kb)], weights)
                new.append((newtop, acc))
            return tuple(new)

        start = (jnp.full((1, SUB), MASKED, F32), jnp.zeros((DH + 8, SUB), F32))
        done = lax.fori_loop(klo[block], khi[block], body, (start, start))
        heads = []
        for h in range(2):
            top, acc = done[h]
            total = acc[DH : DH + 1, :]
            heads.append(acc[:DH, :] / total)
            lse[h : h + 1, cols] = top * SCALE2 + jnp.log2(total)
        outs[(rc, ry)][:, rx * SUB : (rx + 1) * SUB] = jnp.concatenate(heads, 0).astype(BF)


def attend_back_kernel(
    scal, qlo, qhi, qkv, lo, hi, lse, o00, o01, o10, o11, g00, g01, g10, g11, gs, out,
    ks, kt, vs, qt, gt, delta, dqt, dk, dv,
):
    me = scal[1]
    outs = {(0, 0): o00, (0, 1): o01, (1, 0): o10, (1, 1): o11}
    grads = {(0, 0): g00, (0, 1): g01, (1, 0): g10, (1, 1): g11}
    for p, (rc, ry, rx) in enumerate(spots()):
        rows = span(block_of(me, rc, ry, rx))
        here = slice(p * SUB, (p + 1) * SUB)
        for h in range(2):
            ks[h, rows, :] = qkv[here, 144 + DH * h : 144 + DH * (h + 1)]
            vs[h, rows, :] = qkv[here, 288 + DH * h : 288 + DH * (h + 1)]
        qtile = qkv[here, 0:144].T
        ktile = qkv[here, 144:288].T
        if rc == 0:
            gtile = grads[(rx, ry)][0:144, :]
        else:
            gtile = gs[:, (ry * 2 + rx) * SUB : (ry * 2 + rx + 1) * SUB]
        otile = outs[(rc, ry)][:, rx * SUB : (rx + 1) * SUB]
        both = gtile.astype(F32) * otile.astype(F32)
        for h in range(2):
            part = slice(DH * h, DH * (h + 1))
            qt[h, :, rows] = qtile[part]
            kt[h, :, rows] = ktile[part]
            gt[h, :, rows] = gtile[part]
            delta[h : h + 1, rows] = jnp.sum(both[part], axis=0, keepdims=True)
    dqt[...] = jnp.zeros_like(dqt)
    dk[...] = jnp.zeros_like(dk)
    dv[...] = jnp.zeros_like(dv)
    places = lax.broadcasted_iota(jnp.int32, (SUB, SUB), 0)
    lanes = lax.broadcasted_iota(jnp.int32, (1, SUB), 1)

    @pl.loop(0, 8)
    def _(kb):
        keys = span(kb)
        base = kb * SUB

        def body(qb, carry):
            cols = span(qb)
            low, high = lo[:, cols] - base, hi[:, cols] - base
            own = lanes + (qb * SUB - base)
            allowed = ((places >= low) & (places < high)) | (places == own)
            for h in range(2):
                s = dot(ks[h, keys, :], qt[h, :, cols])
                probs = jnp.where(allowed, jnp.exp2(s * SCALE2 - lse[h : h + 1, cols]), 0.0)
                gprobs = dot(vs[h, keys, :], gt[h, :, cols])
                gscores = (probs * (gprobs - delta[h : h + 1, cols])).astype(BF)
                dv[h, keys, :] += dot_nt(probs.astype(BF), gt[h, :, cols])
                dk[h, keys, :] += dot_nt(gscores, qt[h, :, cols])
                dqt[h, :, cols] += dot(kt[h, :, keys], gscores)
            return carry

        lax.fori_loop(qlo[kb], qhi[kb], body, 0)

    for p, (rc, ry, rx) in enumerate(spots()):
        rows = span(block_of(me, rc, ry, rx))
        parts = [dqt[h, :, rows].T * SCALE for h in range(2)]
        parts += [dk[h, rows, :] * SCALE for h in range(2)]
        parts += [dv[h, rows, :] for h in range(2)]
        out[p * SUB : (p + 1) * SUB, :] = jnp.concatenate(parts, 1).astype(BF)


def gelu_tangent(u):
    return jnp.tanh(GELU_C * (u + GELU_A * u * u * u))


def dp_sum(v):
    return lax.psum(v, "dp")


def local(
    layer_input, picture, token_kept, ln1_gain, ln1_bias, w_query, b_query, w_key, w_value, b_value,
    w_out, b_out, ln2_gain, ln2_bias, w_up, b_up, w_down, b_down, grad_out,
):
    ypos = lax.axis_index("tc").astype(jnp.int32)
    trpos = lax.axis_index("tr").astype(jnp.int32)
    me = trpos * 2 + ypos
    half = layer_input.shape[1]
    width = 2 * half
    seq = picture.shape[0]
    heads2 = b_query.shape[0]
    units = w_up.shape[1]

    numbers = jnp.arange(8, dtype=jnp.int32)[:, None]
    hot = (picture[None, :] == numbers).astype(jnp.int32)
    counts = jnp.sum(hot, axis=1)
    kept = jnp.sum(hot * token_kept[None, :], axis=1)
    starts = jnp.cumsum(counts) - counts
    lo = jnp.sum(hot * starts[:, None], axis=0)
    hi = jnp.sum(hot * (starts + kept)[:, None], axis=0)
    end = jnp.sum(hot * (starts + counts)[:, None], axis=0)
    blocks = seq // SUB
    firsts = lo.reshape(blocks, SUB)[:, 0]
    klo = qlo = firsts // SUB
    lasts = jnp.arange(1, blocks + 1, dtype=jnp.int32) * SUB
    khi = (jnp.maximum(lasts, hi.reshape(blocks, SUB)[:, -1]) + SUB - 1) // SUB
    qhi = (jnp.maximum(lasts, end.reshape(blocks, SUB)[:, -1]) + SUB - 1) // SUB
    lo, hi = lo[None, :], hi[None, :]
    scal = jnp.stack((ypos, me))

    small = jnp.stack((ln1_gain, ln1_bias, ln2_gain, ln2_bias, b_out, b_down))
    both = jnp.concatenate((small, py(small)), 1)
    gain1, shift1, gain2, shift2, bias_out, bias_down = [both[i : i + 1] for i in range(6)]
    up_y = py(b_up)
    up_own = jnp.where(ypos == 0, jnp.concatenate((b_up, up_y)), jnp.concatenate((up_y, b_up)))
    bias_up = jnp.concatenate((up_own, pc(up_own)))[None, :]

    a00 = layer_input
    a10 = px(a00)
    b00 = py(a00)
    b10 = px(b00)
    a01, b01, a11, b11 = pc(a00), pc(b00), pc(a10), pc(b10)

    def heads_of(w, pos):
        return cols_at(w, pos * heads2, heads2)

    wa = jnp.concatenate([heads_of(w, ypos) for w in (w_query, w_key, w_value)], 1)
    wb = py(jnp.concatenate([heads_of(w, 1 - ypos) for w in (w_query, w_key, w_value)], 1))
    qkv_bias = jnp.concatenate((b_query, jnp.zeros_like(b_query), b_value))[None, :]

    h1, qkv, resid = pl.pallas_call(
        norm_qkv_kernel,
        out_shape=(
            jax.ShapeDtypeStruct((seq, width), BF),
            jax.ShapeDtypeStruct((seq, 3 * heads2), BF),
            jax.ShapeDtypeStruct((2 * SUB, width), BF),
        ),
        in_specs=[SMEM_SPEC] + whole_vmem(13),
        out_specs=tuple(whole_vmem(3)),
        compiler_params=params(),
        name="norm_qkv",
    )(scal, a00, b00, a01, b01, a10, b10, a11, b11, wa, wb, qkv_bias, gain1, shift1)

    wo_a = rel_rows(w_out, ypos)
    wo_b = rel_rows(py(wo_a), 1)
    wo_x0 = jnp.concatenate((wo_a, wo_b), 1)
    wo_c = pc(wo_x0)
    n2 = heads2
    wo_half = jnp.concatenate((wo_x0[:n2], wo_c[:n2], wo_x0[n2:], wo_c[n2:]), 0)
    wo = jnp.concatenate((wo_half, px(wo_half)), 0)
    up_a, up_b = w_up, py(w_up)
    up_a2, up_b2 = pc(up_a), pc(up_b)
    wup = jnp.concatenate((jnp.concatenate((up_a, up_a2), 1), jnp.concatenate((up_b, up_b2), 1)), 0)
    down_a, down_b = w_down, py(w_down)
    down_a2, down_b2 = pc(down_a), pc(down_b)
    wdown = jnp.concatenate((jnp.concatenate((down_a, down_b), 1), jnp.concatenate((down_a2, down_b2), 1)), 0)
    go_own = rows_at(grad_out, ypos * SUB, SUB)
    go = jnp.concatenate((go_own, py(rows_at(grad_out, (1 - ypos) * SUB, SUB))), 1)
    go_all = jnp.concatenate((go, px(go)), 0)

    scratch_t = pltpu.VMEM((2, DH, seq), BF)
    scratch_k = pltpu.VMEM((2, seq, DH), BF)
    o_shape = jax.ShapeDtypeStruct((heads2, 2 * SUB), BF)
    o00, o01, o10, o11, lse = pl.pallas_call(
        attend_kernel,
        out_shape=(o_shape,) * 4 + (jax.ShapeDtypeStruct((2, seq), F32),),
        in_specs=[SMEM_SPEC] * 3 + whole_vmem(3),
        out_specs=tuple(whole_vmem(5)),
        scratch_shapes=[scratch_k, scratch_t, pltpu.VMEM((2, DH + 8, seq), BF)],
        compiler_params=params(),
        name="attend",
    )(scal, klo, khi, qkv, lo, hi)

    c0, c1 = pc(o10), pc(o11)
    y0, y1 = py(o01), py(c1)
    x0, x1, xy0, xy1 = px(o00), px(c0), px(y0), px(y1)

    def turned(v):
        return jnp.concatenate((v[:, SUB:], v[:, :SUB]), 1)

    att = jnp.concatenate((o00, c0, y0, y1) + tuple(turned(v) for v in (x0, x1, xy0, xy1)), 0)
    mixed = resid.astype(F32) + dot_tn(att, wo) + bias_out
    mean2 = jnp.mean(mixed, axis=1, keepdims=True)
    root2 = lax.rsqrt(jnp.mean(mixed * mixed, axis=1, keepdims=True) - mean2 * mean2 + EPSILON)
    normed2 = (mixed - mean2) * root2
    h2 = (normed2 * gain2 + shift2).astype(BF)

    upper = dot(h2, wup) + bias_up
    tangent = gelu_tangent(upper)
    activated = (0.5 * upper * (1.0 + tangent)).astype(BF)
    slope = 0.5 * (1.0 + tangent) + 0.5 * upper * (1.0 - tangent * tangent) * GELU_C * (
        1.0 + 3.0 * GELU_A * upper * upper
    )
    grad_upper = (dot_nt(go_all, wdown) * slope).astype(BF)
    part_h2 = dot_nt(grad_upper, wup)
    grad_h2 = part_h2[:SUB] + px(part_h2[SUB:].astype(BF)).astype(F32)
    part_res = dot(activated, wdown)
    result = mixed[:SUB] + part_res[:SUB] + px(part_res[SUB:].astype(BF)).astype(F32) + bias_down
    result = result.astype(BF)
    result_y = py(result[:, half:])
    result = jnp.where(
        ypos == 0,
        jnp.concatenate((result[:, :half], result_y), 0),
        jnp.concatenate((result_y, result[:, :half]), 0),
    )

    weighted = grad_h2 * gain2
    n_own = normed2[:SUB]
    grad_mixed = go.astype(F32) + root2[:SUB] * (
        weighted
        - jnp.mean(weighted, axis=1, keepdims=True)
        - n_own * jnp.mean(weighted * n_own, axis=1, keepdims=True)
    )
    sums2 = jnp.stack((jnp.sum(grad_h2 * n_own, 0), jnp.sum(grad_h2, 0), jnp.sum(grad_mixed, 0)))
    gm_low = grad_mixed.astype(BF)
    gm_x = px(gm_low)
    gm_y = py(gm_low[:, half:])

    gatt = dot_nt(wo, gm_low).astype(BF)
    gx = px(gatt[4 * n2 :])
    gy = py(gatt[2 * n2 : 4 * n2])
    gxy = py(gx[2 * n2 :])
    gs = pc(jnp.concatenate((gatt[n2 : 2 * n2], gx[n2 : 2 * n2], gy[n2:], gxy[n2:]), 1))

    dqkv = pl.pallas_call(
        attend_back_kernel,
        out_shape=jax.ShapeDtypeStruct((seq, 3 * heads2), BF),
        in_specs=[SMEM_SPEC] * 3 + whole_vmem(13),
        out_specs=pl.BlockSpec(memory_space=pltpu.VMEM),
        scratch_shapes=[
            scratch_k, scratch_t, scratch_k, scratch_t, scratch_t,
            pltpu.VMEM((2, seq), F32),
            pltpu.VMEM((2, DH, seq), F32),
            pltpu.VMEM((2, seq, DH), F32),
            pltpu.VMEM((2, seq, DH), F32),
        ],
        compiler_params=params(),
        name="attend_back",
    )(scal, qlo, qhi, qkv, lo, hi, lse, o00, o01, o10, o11, gatt, gy, gx, gxy, gs)

    dwd = dot_tn(activated, go_all)
    dwd = dwd[:units] + pc(dwd[units:].astype(BF)).astype(F32)
    dwd = dwd[:, :half] + py(dwd[:, half:].astype(BF)).astype(F32)
    dwu = dot_tn(h2, grad_upper)
    dwu = dwu[:, :units] + pc(dwu[:, units:].astype(BF)).astype(F32)
    dwu = dwu[:half] + py(dwu[half:].astype(BF)).astype(F32)
    gm_all = jnp.concatenate((gm_low, gm_x), 0)
    dwo = dot(att[: 4 * n2], gm_all)
    dwo_own = jnp.concatenate((dwo[:n2], dwo[2 * n2 : 3 * n2]), 0)
    dwo_sib = jnp.concatenate((dwo[n2 : 2 * n2], dwo[3 * n2 :]), 0)
    dwo = dwo_own + pc(dwo_sib.astype(BF)).astype(F32)
    dwo = dwo[:, :half] + rel_rows(py(dwo[:, half:].astype(BF)), 1).astype(F32)

    wqkv = jnp.concatenate((wa, wb), 0)
    dwqkv = dot_tn(h1, dqkv)
    dwq_y = py(dwqkv[half:].astype(BF))
    dwq_a = dwqkv[:half].astype(BF)

    dwd_t = dp_sum(dwd.astype(BF))
    dwu_t = dp_sum(dwu.astype(BF))
    dwo_t = dp_sum(dwo.astype(BF))
    dwq_t = dp_sum(jnp.concatenate((dwq_a, dwq_y), 1)).astype(F32)
    own_q, other_q = dwq_t[:, : 3 * n2], dwq_t[:, 3 * n2 :]
    first_q = jnp.where(ypos == 0, own_q, other_q)
    second_q = jnp.where(ypos == 0, other_q, own_q)
    gw = [
        jnp.concatenate((first_q[:, i * n2 : (i + 1) * n2], second_q[:, i * n2 : (i + 1) * n2]), 1)
        for i in range(3)
    ]

    q4 = 4 * SUB
    low_part = dot_nt(dqkv[q4:], wqkv).astype(BF)
    part = dot_nt(dqkv[:q4], wqkv) + pc(low_part).astype(F32)
    top, bottom = part[: 2 * SUB], part[2 * SUB :]
    top = top[:SUB] + px(top[SUB:].astype(BF)).astype(F32)
    top_send = top[:, half:].astype(BF)
    return_top = top[:, :half]
    bottom_y = py(bottom[:, half:].astype(BF)).astype(F32)
    bottom_a = bottom[:, :half]
    top_recv = py(top_send).astype(F32)
    extra = px(bottom_a[SUB:].astype(BF)).astype(F32)
    extra_y = px(bottom_y[SUB:].astype(BF)).astype(F32)
    grad_h1_0 = return_top + bottom_y[:SUB] + extra_y
    grad_h1_1 = bottom_a[:SUB] + extra + top_recv
    grad_h1 = jnp.concatenate((grad_h1_0, grad_h1_1), 0)

    own_rel = rel_rows(a00, ypos).astype(F32)
    oth_rel = rel_rows(b00, ypos).astype(F32)
    mean1 = (jnp.sum(own_rel, 1, keepdims=True) + jnp.sum(oth_rel, 1, keepdims=True)) / width
    sq1 = (jnp.sum(own_rel * own_rel, 1, keepdims=True) + jnp.sum(oth_rel * oth_rel, 1, keepdims=True)) / width
    root1 = lax.rsqrt(sq1 - mean1 * mean1 + EPSILON)
    n1 = (own_rel - mean1) * root1
    weighted1 = grad_h1 * ln1_gain[None, :]
    stats = jnp.stack((jnp.sum(weighted1, 1), jnp.sum(weighted1 * n1, 1)))
    stats = stats + rel_rows(py(stats).T, 1).T
    gm_blk = jnp.concatenate((grad_mixed[:, :half], gm_y.astype(F32)), 0)
    gin = gm_blk + root1 * (weighted1 - stats[0][:, None] / width - n1 * (stats[1][:, None] / width))
    gin = rel_rows(gin, ypos).astype(BF)

    sums2 = sums2[:, :half] + py(sums2[:, half:])
    sums1 = jnp.stack((jnp.sum(grad_h1 * n1, 0), jnp.sum(grad_h1, 0)))
    sum_down = jnp.sum(grad_out.astype(F32), 0)
    totals = lax.psum((sums1, sums2, sum_down), ("dp", "tr"))
    gbu = jnp.sum(grad_upper, 0, dtype=F32)
    gbu = gbu[:units] + pc(gbu[units:])
    sums_q = jnp.sum(dqkv, 0, dtype=F32)
    gbu = lax.psum(gbu, ("dp", "tc"))
    n_up = b_up.shape[0]
    gbu = lax.dynamic_slice_in_dim(gbu, ypos * n_up, n_up, 0)
    gbq, gbv = lax.psum((sums_q[:n2], sums_q[2 * n2 :]), "dp")
    return (
        result, gin, totals[0][0], totals[0][1], gw[0], gbq, gw[1], gw[2], gbv,
        rel_rows(dwo_t.astype(F32), ypos), totals[1][2], totals[1][0], totals[1][1],
        dwu_t.astype(F32), gbu, dwd_t.astype(F32), totals[2],
    )


def solution(mesh):
    rows = P(("dp", "tr"), "tc")
    placed = (
        rows, P("dp"), P("dp"), P("tc"), P("tc"), P("tc", "tr"), P(("tr", "tc")), P("tc", "tr"),
        P("tc", "tr"), P(("tr", "tc")), P("tr", "tc"), P("tc"), P("tc"), P("tc"), P("tc", "tr"),
        P(("tr", "tc")), P("tr", "tc"), P("tc"), rows,
    )
    outs = (
        rows, rows, P("tc"), P("tc"), P("tc", "tr"), P(("tr", "tc")), P("tc", "tr"), P("tc", "tr"),
        P(("tr", "tc")), P("tr", "tc"), P("tc"), P("tc"), P("tc"), P("tc", "tr"), P(("tr", "tc")),
        P("tr", "tc"), P("tc"),
    )
    return jax.shard_map(local, mesh=mesh, in_specs=placed, out_specs=outs, check_vma=False)
```

```python
import jax
import jax.numpy as jnp
from jax import lax
from jax.experimental import pallas as pl
from jax.experimental.pallas import tpu as pltpu
from jax.sharding import PartitionSpec as P

DH = 72
PITCH = 80
SUB = 256
EPSILON = 1e-06
GELU_C = 0.7978845608028654
GELU_A = 0.044715
MASKED = -1e30
SCALE = DH**-0.5
SCALE2 = SCALE * 1.4426950408889634
BF = jnp.bfloat16
F32 = jnp.float32
MIB = 1024 * 1024


def swap_perm(axis, bit):
    return [(i, i ^ bit) for i in range(lax.axis_size(axis))]


def px(v):
    return lax.ppermute(v, "tr", swap_perm("tr", 2))


def pc(v):
    return lax.ppermute(v, "tr", swap_perm("tr", 1))


def py(v):
    return lax.ppermute(v, "tc", swap_perm("tc", 1))


def after(v, *earlier):
    return lax.optimization_barrier((v,) + earlier)[0]


def dot(a, b):
    return jnp.dot(a, b, preferred_element_type=F32)


def dot_tn(a, b):
    return lax.dot_general(a, b, (((0,), (0,)), ((), ())), preferred_element_type=F32)


def dot_nt(a, b):
    return lax.dot_general(a, b, (((1,), (1,)), ((), ())), preferred_element_type=F32)


def rows_at(v, first, count):
    return lax.dynamic_slice_in_dim(v, first, count, 0)


def cols_at(v, first, count):
    return lax.dynamic_slice_in_dim(v, first, count, 1)


def rel_rows(v, ypos):
    half = v.shape[0] // 2
    return jnp.concatenate((rows_at(v, ypos * half, half), rows_at(v, (1 - ypos) * half, half)), 0)


VM = pl.BlockSpec(memory_space=pltpu.VMEM)
SM = pl.BlockSpec(memory_space=pltpu.SMEM)


def shape(*dims, dtype=BF):
    return jax.ShapeDtypeStruct(dims, dtype)


def call(body, name, scalars, arrays, outs, us, scratch=(), vmem=24):
    return pl.pallas_call(
        body,
        out_shape=tuple(outs),
        in_specs=[SM] * len(scalars) + [VM] * len(arrays),
        out_specs=tuple([VM] * len(outs)),
        scratch_shapes=list(scratch),
        compiler_params=pltpu.CompilerParams(vmem_limit_bytes=vmem * MIB),
        cost_estimate=pl.CostEstimate(
            flops=int(us * 600e6), bytes_accessed=int(us * 3e6), transcendentals=0
        ),
        name=name,
    )(*scalars, *arrays)


def spots():
    return [(rc, ry, rx) for rc in range(2) for ry in range(2) for rx in range(2)]


def block_of(me, rc, ry, rx):
    return me ^ (rx * 4 + rc * 2 + ry)


def span(block):
    return pl.ds(pl.multiple_of(block * SUB, SUB), SUB)


def norm_qkv_kernel(
    scal, a00, b00, a01, b01, a10, b10, a11, b11, wa, wb, bias, gain, shift,
    h_ref, qkv_ref, kv_ref, res_ref, w_ref, gain_s, shift_s, bias_s,
):
    ypos, me = scal[0], scal[1]
    half = a00.shape[0]
    weights = jnp.concatenate((wa[...], wb[...]), 1)
    w_ref[...] = weights.T
    gain_s[...] = jnp.broadcast_to(gain[...], gain_s.shape)
    shift_s[...] = jnp.broadcast_to(shift[...], shift_s.shape)
    bias_s[...] = jnp.broadcast_to(bias[...], bias_s.shape)
    sources = {(0, 0): (a00, b00), (1, 0): (a01, b01), (0, 1): (a10, b10), (1, 1): (a11, b11)}
    for p, (rc, ry, rx) in enumerate(spots()):
        here = slice(p * SUB, (p + 1) * SUB)
        there = span(block_of(me, rc, ry, rx))
        cols = span(ypos ^ ry)
        sa, sb = sources[(rc, rx)]
        raw = jnp.concatenate((sa[:, cols], sb[:, cols]), 0)
        if rc == 0 and ry == 0:
            res_ref[:, rx * SUB : (rx + 1) * SUB] = raw
        v = raw.astype(F32)
        mean = jnp.sum(v, axis=0, keepdims=True) / (2 * half)
        square = jnp.sum(v * v, axis=0, keepdims=True) / (2 * half)
        root = lax.rsqrt(square - mean * mean + EPSILON)
        hidden = ((v - mean) * root * gain_s[...] + shift_s[...]).astype(BF)
        h_ref[:, here] = hidden
        qkv = (dot(weights, hidden) + bias_s[...]).astype(BF)
        qkv_ref[:, there] = qkv
        for i in range(4):
            kv_ref[there, 128 * i : 128 * i + PITCH] = qkv[PITCH * (2 + i) : PITCH * (3 + i), :].T


def attend_kernel(scal, klo, khi, qkv, kv, lo, hi, o00, o01, o10, o11, lse):
    me = scal[1]
    outs = {(0, 0): o00, (0, 1): o01, (1, 0): o10, (1, 1): o11}
    places = lax.broadcasted_iota(jnp.int32, (SUB, SUB), 0)
    lanes = lax.broadcasted_iota(jnp.int32, (1, SUB), 1)
    for rc, ry, rx in sorted(spots(), reverse=True):
        block = block_of(me, rc, ry, rx)
        cols = span(block)
        low, high = lo[:, cols], hi[:, cols]
        own = lanes + block * SUB

        def body(kb, carry):
            base = kb * SUB
            allowed = ((places >= low - base) & (places < high - base)) | (places == own - base)
            new = []
            for h in range(2):
                top, acc = carry[h]
                s = dot(kv[span(kb), 128 * h : 128 * h + PITCH], qkv[PITCH * h : PITCH * (h + 1), cols])
                s = jnp.where(allowed, s, MASKED)
                newtop = jnp.maximum(top, jnp.max(s, axis=0, keepdims=True))
                alpha = jnp.exp2((top - newtop) * SCALE2)
                weights = jnp.exp2((s - newtop) * SCALE2).astype(BF)
                acc = acc * alpha + dot(qkv[PITCH * (4 + h) : PITCH * (5 + h), span(kb)], weights)
                new.append((newtop, acc))
            return tuple(new)

        start = (jnp.full((1, SUB), MASKED, F32), jnp.zeros((PITCH, SUB), F32))
        done = lax.fori_loop(klo[block], khi[block], body, (start, start))
        heads = []
        for h in range(2):
            top, acc = done[h]
            total = acc[DH : DH + 1, :]
            heads.append(acc[:DH, :] / total)
            lse[h : h + 1, cols] = top * SCALE2 + jnp.log2(total)
        outs[(rc, ry)][:, rx * SUB : (rx + 1) * SUB] = jnp.concatenate(heads, 0).astype(BF)


def attend_back_kernel(
    scal, qlo, qhi, qkv, kv, lo, hi, lse, o00, o01, o10, o11, g00, g10, g01, g11, gs, out,
    gt, delta, dqt, dk, dv,
):
    me = scal[1]
    outs = {(0, 0): o00, (0, 1): o01, (1, 0): o10, (1, 1): o11}
    grads = {(0, 0): g00, (0, 1): g01, (1, 0): g10, (1, 1): g11}
    for rc, ry, rx in spots():
        cols = span(block_of(me, rc, ry, rx))
        if rc == 0:
            gtile = grads[(rx, ry)][0 : 2 * DH, :].astype(F32)
        else:
            gtile = gs[:, (ry * 2 + rx) * SUB : (ry * 2 + rx + 1) * SUB].astype(F32)
        both = gtile * outs[(rc, ry)][:, rx * SUB : (rx + 1) * SUB].astype(F32)
        for h in range(2):
            part = slice(DH * h, DH * (h + 1))
            padded = jnp.concatenate((gtile[part], jnp.zeros((PITCH - DH, SUB), F32)), 0)
            gt[PITCH * h : PITCH * (h + 1), cols] = padded.astype(BF)
            delta[h : h + 1, cols] = jnp.sum(both[part], axis=0, keepdims=True)
    dqt[...] = jnp.zeros_like(dqt)
    dk[...] = jnp.zeros_like(dk)
    dv[...] = jnp.zeros_like(dv)
    places = lax.broadcasted_iota(jnp.int32, (SUB, SUB), 0)
    lanes = lax.broadcasted_iota(jnp.int32, (1, SUB), 1)

    @pl.loop(0, 8)
    def _(kb):
        keys = span(kb)
        base = kb * SUB

        def body(qb, carry):
            cols = span(qb)
            low, high = lo[:, cols] - base, hi[:, cols] - base
            own = lanes + (qb * SUB - base)
            allowed = ((places >= low) & (places < high)) | (places == own)
            for h in range(2):
                head = slice(PITCH * h, PITCH * (h + 1))
                s = dot(kv[keys, 128 * h : 128 * h + PITCH], qkv[head, cols])
                probs = jnp.where(allowed, jnp.exp2(s * SCALE2 - lse[h : h + 1, cols]), 0.0)
                gprobs = dot(kv[keys, 256 + 128 * h : 256 + 128 * h + PITCH], gt[head, cols])
                gscores = (probs * (gprobs - delta[h : h + 1, cols])).astype(BF)
                dv[h, keys, :] += dot_nt(probs.astype(BF), gt[head, cols])
                dk[h, keys, :] += dot_nt(gscores, qkv[head, cols])
                dqt[head, cols] += dot(qkv[PITCH * (2 + h) : PITCH * (3 + h), keys], gscores)
            return carry

        lax.fori_loop(qlo[kb], qhi[kb], body, 0)

    for p, (rc, ry, rx) in enumerate(spots()):
        here = slice(p * SUB, (p + 1) * SUB)
        rows = span(block_of(me, rc, ry, rx))
        out[: 2 * PITCH, here] = (dqt[:, rows] * SCALE).astype(BF)
        for h in range(2):
            out[PITCH * (2 + h) : PITCH * (3 + h), here] = (dk[h, rows, :].T * SCALE).astype(BF)
            out[PITCH * (4 + h) : PITCH * (5 + h), here] = dv[h, rows, :].T.astype(BF)


def mix_kernel(o0, o1, o2, o3, x0, x1, x2, x3, woa, wob, res, bias, gain, shift, mixed, h2t, h2):
    weights = jnp.concatenate((woa[...], wob[...]), 1)
    for rx in range(2):
        here = slice(rx * SUB, (rx + 1) * SUB)
        turned = slice((1 - rx) * SUB, (2 - rx) * SUB)
        att = jnp.concatenate([o[:, here] for o in (o0, o1, o2, o3)] + [x[:, turned] for x in (x0, x1, x2, x3)], 0)
        v = res[:, here].astype(F32) + dot_tn(weights, att) + bias[...]
        mixed[:, here] = v
        mean = jnp.mean(v, axis=0, keepdims=True)
        root = lax.rsqrt(jnp.mean(v * v, axis=0, keepdims=True) - mean * mean + EPSILON)
        hidden = ((v - mean) * root * gain[...] + shift[...]).astype(BF)
        h2t[:, here] = hidden
        h2[here, :] = hidden.T


def gelu_both(u):
    square = u * u
    tangent = jnp.tanh(GELU_C * (u + GELU_A * square * u))
    plus = 0.5 * (1.0 + tangent)
    slope = plus + 0.5 * u * (1.0 - tangent * tangent) * GELU_C * (1.0 + 3.0 * GELU_A * square)
    return u * plus, slope


def feed_kernel(h2, go, uaa, uba, uas, ubs, daa, dba, das, dbs, bias, act0, act1, gu0, gu1, send):
    for k, (ua, ub, da, db, act, gu) in enumerate(
        ((uaa, uba, daa, dba, act0, gu0), (uas, ubs, das, dbs, act1, gu1))
    ):
        upper = dot(h2[...], jnp.concatenate((ua[...], ub[...]), 0)) + bias[k : k + 1, :]
        value, slope = gelu_both(upper)
        act[...] = value.astype(BF)
        gact = dot(go[...], jnp.concatenate((da[...], db[...]), 0))
        gu[...] = (gact * slope).astype(BF)
    half = uaa.shape[0]
    other = slice(SUB, 2 * SUB)
    for first, u0, u1 in ((0, uaa, uas), (half, uba, ubs)):
        part = dot_nt(u0[...], gu0[other, :]) + dot_nt(u1[...], gu1[other, :])
        send[first : first + half, :] = part.astype(BF)


def feed_back_kernel(uaa, uba, uas, ubs, gu0, gu1, own):
    half = uaa.shape[0]
    here = slice(0, SUB)
    for first, u0, u1 in ((0, uaa, uas), (half, uba, ubs)):
        own[first : first + half, :] = dot_nt(u0[...], gu0[here, :]) + dot_nt(u1[...], gu1[here, :])


def norm2_back_kernel(own, recv, mixed, go, gain, woa, wob, gm, low, g_own, g_y, g_x, sums):
    e = own[...] + recv[...].astype(F32)
    v = mixed[:, :SUB]
    mean = jnp.mean(v, axis=0, keepdims=True)
    root = lax.rsqrt(jnp.mean(v * v, axis=0, keepdims=True) - mean * mean + EPSILON)
    n = (v - mean) * root
    w = e * gain[...]
    grad = go[...].astype(F32) + root * (
        w - jnp.mean(w, axis=0, keepdims=True) - n * jnp.mean(w * n, axis=0, keepdims=True)
    )
    gm[...] = grad
    rounded = grad.astype(BF)
    low[...] = rounded
    half = woa.shape[1]
    gatt = (dot(woa[...], rounded[:half]) + dot(wob[...], rounded[half:])).astype(BF)
    n2 = 2 * DH
    g_own[...] = gatt[: 2 * n2]
    g_y[...] = gatt[2 * n2 : 4 * n2]
    g_x[...] = gatt[4 * n2 :]
    sums[:, 0:1] = jnp.sum(e * n, axis=1, keepdims=True)
    sums[:, 1:2] = jnp.sum(e, axis=1, keepdims=True)
    sums[:, 2:3] = jnp.sum(grad, axis=1, keepdims=True)


def part_kernel(w, dqkv, send):
    send[...] = dot(w[...], dqkv[:, 4 * SUB :]).astype(BF)


HALF = SUB // 2


def spread_kernel(w, dqkv, recv, to_x, to_y, keep_p, keep_q):
    half = w.shape[0] // 2
    total = dot(w[...], dqkv[:, : 4 * SUB]) + recv[...].astype(F32)
    for ry in range(2):
        at = slice(ry * HALF, (ry + 1) * HALF)
        for rx in range(2):
            first = (ry * 2 + rx) * SUB
            p = total[:, first : first + HALF]
            q = total[:, first + HALF : first + SUB]
            if rx == 0:
                keep_p[:, at] = p
            else:
                to_x[:, at] = p.astype(BF)
            where = slice((ry * 2 + rx) * HALF, (ry * 2 + rx + 1) * HALF)
            keep_q[:, where] = q[:half]
            to_y[:, where] = q[half:].astype(BF)


def spread2_kernel(keep_p, keep_q, from_x, from_y, to_x, to_y, own_p, own_q):
    half = own_p.shape[0]
    p = keep_p[...] + from_x[...].astype(F32)
    own_p[...] = p[:half]
    to_y[...] = p[half:].astype(BF)
    for ry in range(2):
        at = slice(ry * HALF, (ry + 1) * HALF)
        for rx in range(2):
            mine = slice((ry * 2 + rx) * HALF, (ry * 2 + rx + 1) * HALF)
            theirs = slice(((1 - ry) * 2 + rx) * HALF, ((1 - ry) * 2 + rx + 1) * HALF)
            q = keep_q[:, mine] + from_y[:, theirs].astype(F32)
            if rx == 0:
                own_q[:, at] = q
            else:
                to_x[:, at] = q.astype(BF)


def norm1_stats_kernel(scal, own_p, own_q, from_x, from_y, a, b, gain, grad, normed, stats, sums):
    ypos = scal[0]
    half = a.shape[0]
    for ry in range(2):
        at = slice(ry * HALF, (ry + 1) * HALF)
        other = slice((1 - ry) * HALF, (2 - ry) * HALF)
        e = jnp.concatenate(
            (own_p[:, at] + from_y[:, other].astype(F32), own_q[:, at] + from_x[:, at].astype(F32)), 1
        )
        here = slice(ry * SUB, (ry + 1) * SUB)
        cols = span(ypos ^ ry)
        va, vb = a[:, cols].astype(F32), b[:, cols].astype(F32)
        mean = (jnp.sum(va, 0, keepdims=True) + jnp.sum(vb, 0, keepdims=True)) / (2 * half)
        square = (jnp.sum(va * va, 0, keepdims=True) + jnp.sum(vb * vb, 0, keepdims=True)) / (2 * half)
        root = lax.rsqrt(square - mean * mean + EPSILON)
        n = (va - mean) * root
        w = e * gain[...]
        grad[:, here] = w
        normed[:, here] = n
        stats[0:1, here] = jnp.sum(w, 0, keepdims=True)
        stats[1:2, here] = jnp.sum(w * n, 0, keepdims=True)
        stats[2:3, here] = root
        more = (jnp.sum(e * n, 1, keepdims=True), jnp.sum(e, 1, keepdims=True))
        for i in range(2):
            if ry == 0:
                sums[:, i : i + 1] = more[i]
            else:
                sums[:, i : i + 1] += more[i]


def norm1_back_kernel(scal, grad, normed, stats, recv, gm_own, gm_y, out):
    ypos = scal[0]
    width = 2 * grad.shape[0]
    for ry in range(2):
        here = slice(ry * SUB, (ry + 1) * SUB)
        other = slice((1 - ry) * SUB, (2 - ry) * SUB)
        total = (stats[0:1, here] + recv[0:1, other]) / width
        along = (stats[1:2, here] + recv[1:2, other]) / width
        gm = gm_own[: grad.shape[0], :] if ry == 0 else gm_y[...].astype(F32)
        whole = gm + stats[2:3, here] * (grad[:, here] - total - normed[:, here] * along)
        out[:, span(ypos ^ ry)] = whole.astype(BF)


def local(
    layer_input, picture, token_kept, ln1_gain, ln1_bias, w_query, b_query, w_key, w_value, b_value,
    w_out, b_out, ln2_gain, ln2_bias, w_up, b_up, w_down, b_down, grad_out,
):
    ypos = lax.axis_index("tc").astype(jnp.int32)
    trpos = lax.axis_index("tr").astype(jnp.int32)
    me = trpos * 2 + ypos
    half = layer_input.shape[1]
    width = 2 * half
    seq = picture.shape[0]
    n2 = b_query.shape[0]
    units = w_up.shape[1]
    scal = jnp.stack((ypos, me))

    a00 = layer_input.T
    a10, b00 = px(a00), py(a00)
    weights = (w_query.T, w_key.T, w_value.T)
    wa = jnp.concatenate([rows_at(w, ypos * n2, n2) for w in weights], 0)
    wb = py(after(jnp.concatenate([rows_at(w, (1 - ypos) * n2, n2) for w in weights], 0), b00))
    b10 = px(b00)
    a01, b01, a11, b11 = pc(a00), pc(b00), pc(a10), pc(b10)

    small = jnp.stack((ln1_gain, ln1_bias, ln2_gain, ln2_bias, b_out, b_down))
    both = jnp.concatenate((small, py(small)), 1)[:, :, None]
    gain1, shift1, gain2, shift2, bias_out, bias_down = [both[i] for i in range(6)]
    up_y = py(b_up)
    up_own = jnp.where(ypos == 0, jnp.concatenate((b_up, up_y)), jnp.concatenate((up_y, b_up)))
    bias_up = jnp.stack((up_own, pc(up_own)))

    def padded(w):
        w = w.reshape(6, DH, w.shape[1])
        return jnp.pad(w, ((0, 0), (0, PITCH - DH), (0, 0))).reshape(6 * PITCH, -1)

    qkv_bias = jnp.concatenate((b_query, jnp.zeros_like(b_query), b_value)).reshape(6, DH)
    ones = (jnp.arange(6) >= 4).astype(F32)[:, None]
    qkv_bias = jnp.concatenate((qkv_bias, ones, jnp.zeros((6, PITCH - DH - 1), F32)), 1).reshape(-1, 1)

    numbers = jnp.arange(8, dtype=jnp.int32)[:, None]
    hot = (picture[None, :] == numbers).astype(jnp.int32)
    counts = jnp.sum(hot, axis=1)
    kept = jnp.sum(hot * token_kept[None, :], axis=1)
    starts = jnp.cumsum(counts) - counts
    lo = jnp.sum(hot * starts[:, None], axis=0)
    hi = jnp.sum(hot * (starts + kept)[:, None], axis=0)
    end = jnp.sum(hot * (starts + counts)[:, None], axis=0)
    blocks = seq // SUB
    klo = qlo = lo.reshape(blocks, SUB)[:, 0] // SUB
    lasts = jnp.arange(1, blocks + 1, dtype=jnp.int32) * SUB
    khi = (jnp.maximum(lasts, hi.reshape(blocks, SUB)[:, -1]) + SUB - 1) // SUB
    qhi = (jnp.maximum(lasts, end.reshape(blocks, SUB)[:, -1]) + SUB - 1) // SUB
    lo, hi = lo[None, :], hi[None, :]

    h1, qkv, kv, resid, w_all = call(
        norm_qkv_kernel, "norm_qkv", (scal,),
        (a00, b00, a01, b01, a10, b10, a11, b11, padded(wa), padded(wb), qkv_bias, gain1, shift1),
        (shape(width, seq), shape(6 * PITCH, seq), shape(seq, 512), shape(width, 2 * SUB), shape(width, 6 * PITCH)),
        8,
        scratch=[pltpu.VMEM((width, SUB), F32)] * 2 + [pltpu.VMEM((6 * PITCH, SUB), F32)],
        vmem=32,
    )

    wo_own = rel_rows(w_out, ypos)
    wo_y = rel_rows(py(after(wo_own, wb)), 1)
    wo_sib, wo_ysib = pc(wo_own), pc(wo_y)

    def by_heads(own, sib):
        return jnp.concatenate((own[:n2], sib[:n2], own[n2:], sib[n2:]), 0)

    wo_a, wo_b = by_heads(wo_own, wo_sib), by_heads(wo_y, wo_ysib)
    wo_a = jnp.concatenate((wo_a, px(after(wo_a, b10))), 0)
    wo_b = jnp.concatenate((wo_b, px(wo_b)), 0)
    u_aa = w_up
    u_ba = py(after(w_up, wo_y))
    u_as, u_bs = pc(u_aa), pc(u_ba)
    go_t = grad_out.T
    go_own = cols_at(go_t, ypos * SUB, SUB)
    go_send = cols_at(go_t, (1 - ypos) * SUB, SUB)
    go_b = py(after(go_send, wo_y))
    go_mine = jnp.concatenate((go_own, go_b), 0)
    go_both = jnp.concatenate((go_mine, px(after(go_mine, b10))), 1)
    go = go_both.T
    d_aa = w_down.T
    d_ba = py(after(d_aa, u_ba))
    d_as, d_bs = pc(d_aa), pc(d_ba)

    o00, o01, o10, o11, lse = call(
        attend_kernel, "attend", (scal, klo, khi), (qkv, kv, lo, hi),
        (shape(n2, 2 * SUB),) * 4 + (shape(2, seq, dtype=F32),), 18,
    )
    c0, c1 = pc(o10), pc(o11)
    y0, y1 = py(o01), py(c1)
    x0, x1, xy0, xy1 = px(o00), px(c0), px(y0), px(y1)
    mixed, h2t, h2 = call(
        mix_kernel, "mix", (),
        (o00, c0, y0, y1, x0, x1, xy0, xy1, wo_a, wo_b, resid, bias_out, gain2, shift2),
        (shape(width, 2 * SUB, dtype=F32), shape(width, 2 * SUB), shape(2 * SUB, width)), 6,
    )

    act0, act1, gu0, gu1, gh_send = call(
        feed_kernel, "feed", (),
        (h2, go, u_aa, u_ba, u_as, u_bs, d_aa, d_ba, d_as, d_bs, bias_up),
        (shape(2 * SUB, units),) * 4 + (shape(width, SUB),), 12, vmem=40,
    )
    gh_recv = px(gh_send)
    (gh_own,) = call(
        feed_back_kernel, "feed_back", (), (u_aa, u_ba, u_as, u_bs, gu0, gu1),
        (shape(width, SUB, dtype=F32),), 3,
    )
    gm, gm_low, g_own, g_y, g_x, sums2 = call(
        norm2_back_kernel, "norm2_back", (),
        (gh_own, gh_recv, mixed, go_mine, gain2, wo_a, wo_b),
        (
            shape(width, SUB, dtype=F32), shape(width, SUB), shape(2 * n2, SUB), shape(2 * n2, SUB),
            shape(4 * n2, SUB), shape(width, 3, dtype=F32),
        ),
        4,
    )
    gx = px(g_x)
    gy = py(g_y)
    gxy = py(gx[2 * n2 :])
    gs = pc(jnp.concatenate((g_own[n2:], gx[n2 : 2 * n2], gy[n2:], gxy[n2:]), 1))
    (dqkv,) = call(
        attend_back_kernel, "attend_back", (scal, qlo, qhi),
        (qkv, kv, lo, hi, lse, o00, o01, o10, o11, g_own, gx, gy, gxy, gs),
        (shape(6 * PITCH, seq),), 22,
        scratch=[
            pltpu.VMEM((2 * PITCH, seq), BF), pltpu.VMEM((2, seq), F32), pltpu.VMEM((2 * PITCH, seq), F32),
            pltpu.VMEM((2, seq, PITCH), F32), pltpu.VMEM((2, seq, PITCH), F32),
        ],
    )

    part_d = [dot(go_both, act).astype(BF) for act in (act0, act1)]
    dwd = part_d[0].astype(F32) + pc(part_d[1]).astype(F32)
    dwd = dwd[:half] + py(dwd[half:].astype(BF)).astype(F32)
    part_u = [dot(h2t, gu).astype(BF) for gu in (gu0, gu1)]
    dwu = part_u[0].astype(F32) + pc(part_u[1]).astype(F32)
    dwu = dwu[:half] + py(dwu[half:].astype(BF)).astype(F32)
    gm_x, gm_y = px(gm_low), py(gm_low[half:])
    gm_both = jnp.concatenate((gm_low, gm_x), 1)
    dwo_own = dot_nt(jnp.concatenate((o00, y0), 0), gm_both)
    dwo_sib = dot_nt(jnp.concatenate((c0, y1), 0), gm_both).astype(BF)
    dwo = dwo_own + pc(dwo_sib).astype(F32)
    dwo = dwo[:, :half] + rel_rows(py(dwo[:, half:].astype(BF)), 1).astype(F32)

    part_r = dot_nt(jnp.concatenate((jnp.concatenate((d_aa, d_as), 1), jnp.concatenate((d_ba, d_bs), 1)), 0),
                    jnp.concatenate((act0, act1), 1))
    result = mixed[:, :SUB] + part_r[:, :SUB] + px(part_r[:, SUB:].astype(BF)).astype(F32) + bias_down
    result = result.astype(BF)

    def by_place(own, other):
        return jnp.where(ypos == 0, jnp.concatenate((own, other), 1), jnp.concatenate((other, own), 1))

    result = by_place(result[:half], py(result[half:])).T

    (p_send,) = call(part_kernel, "part", (), (w_all, dqkv), (shape(width, 4 * SUB),), 3)
    p_recv = pc(p_send)
    to_x, to_y, keep_p, keep_q = call(
        spread_kernel, "spread", (), (w_all, dqkv, p_recv),
        (shape(width, SUB), shape(half, 2 * SUB), shape(width, SUB, dtype=F32), shape(half, 2 * SUB, dtype=F32)), 4,
    )
    to_x2, to_y2, own_p, own_q = call(
        spread2_kernel, "spread2", (), (keep_p, keep_q, px(to_x), py(to_y)),
        (shape(half, SUB), shape(half, SUB), shape(half, SUB, dtype=F32), shape(half, SUB, dtype=F32)), 2,
    )
    grad, normed, stats, sums1 = call(
        norm1_stats_kernel, "norm1_stats", (scal,),
        (own_p, own_q, px(to_x2), py(to_y2), a00, b00, ln1_gain[:, None]),
        (
            shape(half, 2 * SUB, dtype=F32), shape(half, 2 * SUB, dtype=F32),
            shape(8, 2 * SUB, dtype=F32), shape(half, 2, dtype=F32),
        ),
        2,
    )
    (gin,) = call(
        norm1_back_kernel, "norm1_back", (scal,), (grad, normed, stats, py(stats), gm, gm_y),
        (shape(half, 2 * SUB),), 1,
    )

    dwq = dot_nt(dqkv, h1).astype(BF).reshape(6, PITCH, width)[:, :DH].reshape(3, n2, width)
    dwq_y = py(dwq[:, :, half:])
    dwq = jnp.stack((dwq[:, :, :half], dwq_y), 1)
    dwq = lax.psum(dwq, "dp").astype(F32)
    dwq = jnp.where(ypos == 0, dwq, dwq[:, ::-1]).reshape(3, 2 * n2, half)

    dwd, dwu, dwo = lax.psum((dwd.astype(BF), dwu.astype(BF), dwo.astype(BF)), "dp")

    sums2 = sums2[:half] + py(sums2[half:])
    sum_down = jnp.sum(go_t.astype(F32), 1, keepdims=True)
    totals = lax.psum(jnp.concatenate((sums1, sums2, sum_down), 1), ("dp", "tr"))
    gbu = jnp.stack((jnp.sum(gu0, 0, dtype=F32), jnp.sum(gu1, 0, dtype=F32)))
    gbu = gbu[0] + pc(gbu[1])
    sums_q = jnp.sum(dqkv, 1, dtype=F32).reshape(3, 2, PITCH)[:, :, :DH].reshape(3, n2)
    gbu = lax.psum(gbu, ("dp", "tc"))
    n_up = b_up.shape[0]
    gbu = lax.dynamic_slice_in_dim(gbu, ypos * n_up, n_up, 0)
    sums_q = lax.psum(sums_q, "dp")
    return (
        result, gin.T, totals[:, 0], totals[:, 1], dwq[0].T, sums_q[0], dwq[1].T, dwq[2].T, sums_q[2],
        rel_rows(dwo.astype(F32), ypos), totals[:, 4], totals[:, 2], totals[:, 3],
        dwu.astype(F32), gbu, dwd.astype(F32).T, totals[:, 5],
    )


def solution(mesh):
    rows = P(("dp", "tr"), "tc")
    placed = (
        rows, P("dp"), P("dp"), P("tc"), P("tc"), P("tc", "tr"), P(("tr", "tc")), P("tc", "tr"),
        P("tc", "tr"), P(("tr", "tc")), P("tr", "tc"), P("tc"), P("tc"), P("tc"), P("tc", "tr"),
        P(("tr", "tc")), P("tr", "tc"), P("tc"), rows,
    )
    outs = (
        rows, rows, P("tc"), P("tc"), P("tc", "tr"), P(("tr", "tc")), P("tc", "tr"), P("tc", "tr"),
        P(("tr", "tc")), P("tr", "tc"), P("tc"), P("tc"), P("tc"), P("tc", "tr"), P(("tr", "tc")),
        P("tr", "tc"), P("tc"),
    )
    return jax.shard_map(local, mesh=mesh, in_specs=placed, out_specs=outs, check_vma=False)
```

```python
import jax
import jax.numpy as jnp
from jax import lax
from jax.experimental import pallas as pl
from jax.experimental.pallas import tpu as pltpu
from jax.sharding import PartitionSpec as P

DH = 72
PITCH = 80
SUB = 256
EPSILON = 1e-06
GELU_C = 0.7978845608028654
GELU_A = 0.044715
MASKED = -1e30
SCALE = DH**-0.5
SCALE2 = SCALE * 1.4426950408889634
BF = jnp.bfloat16
F32 = jnp.float32
MIB = 1024 * 1024


def swap_perm(axis, bit):
    return [(i, i ^ bit) for i in range(lax.axis_size(axis))]


def px(v):
    return lax.ppermute(v, "tr", swap_perm("tr", 2))


def pc(v):
    return lax.ppermute(v, "tr", swap_perm("tr", 1))


def py(v):
    return lax.ppermute(v, "tc", swap_perm("tc", 1))


def phase(*values):
    return lax.optimization_barrier(values)


def after(v, *earlier):
    return phase(v, *earlier)[0]


def dot(a, b):
    return jnp.dot(a, b, preferred_element_type=F32)


def dot_tn(a, b):
    return lax.dot_general(a, b, (((0,), (0,)), ((), ())), preferred_element_type=F32)


def dot_nt(a, b):
    return lax.dot_general(a, b, (((1,), (1,)), ((), ())), preferred_element_type=F32)


def rows_at(v, first, count):
    return lax.dynamic_slice_in_dim(v, first, count, 0)


def cols_at(v, first, count):
    return lax.dynamic_slice_in_dim(v, first, count, 1)


def dp_swap(v, bit):
    return lax.ppermute(v, "dp", swap_perm("dp", bit))


def line(step, v):
    if lax.axis_size("dp") != 4:
        return v
    return lax.ppermute(v, "dp", ([(0, 1), (3, 2)], [(1, 2), (2, 1)], [(1, 0), (2, 3)])[step])


def line_sum(v, received):
    if lax.axis_size("dp") != 4:
        return v
    return (v.astype(F32) + received.astype(F32)).astype(BF)


def line_end(v, received):
    if lax.axis_size("dp") != 4:
        return lax.psum(v, "dp").astype(F32)
    place = lax.axis_index("dp")
    return jnp.where((place == 1) | (place == 2), v, received).astype(F32)


def dp_step(v, bit):
    return dp_swap(v, bit) if lax.axis_size("dp") == 4 else jnp.zeros_like(v)


def dp_last(v):
    return v if lax.axis_size("dp") == 4 else lax.psum(v, "dp")


VM = pl.BlockSpec(memory_space=pltpu.VMEM)
SM = pl.BlockSpec(memory_space=pltpu.SMEM)


def shape(*dims, dtype=BF):
    return jax.ShapeDtypeStruct(dims, dtype)


ANY = pl.BlockSpec(memory_space=pl.ANY)


def call(body, name, scalars, arrays, outs, us, scratch=(), vmem=14, far=()):
    return pl.pallas_call(
        body,
        out_shape=tuple(outs),
        in_specs=[SM] * len(scalars) + [VM] * len(arrays) + [ANY] * len(far),
        out_specs=tuple([VM] * len(outs)),
        scratch_shapes=list(scratch),
        compiler_params=pltpu.CompilerParams(vmem_limit_bytes=vmem * MIB),
        cost_estimate=pl.CostEstimate(
            flops=int(us * 600e6), bytes_accessed=int(us * 3e6), transcendentals=0
        ),
        name=name,
    )(*scalars, *arrays, *far)


def spots():
    return [(rc, ry, rx) for rc in range(2) for ry in range(2) for rx in range(2)]


def block_of(me, rc, ry, rx):
    return me ^ (rx * 4 + rc * 2 + ry)


def span(block):
    return pl.ds(pl.multiple_of(block * SUB, SUB), SUB)


def head_rows(pos):
    return pl.ds(pl.multiple_of(pos * 2 * DH, 16), 2 * DH)


def row_of(col):
    return jnp.broadcast_to(col, (col.shape[0], 128)).T[0:1]


def column(i, *parts):
    return jnp.concatenate([p[...].T[:, i : i + 1] for p in parts], 0)


def pack_kernel(scal, q, k, v, out):
    rows = head_rows(1 - scal[0])
    for i, w in enumerate((q, k, v)):
        out[2 * DH * i : 2 * DH * (i + 1), :] = w[rows, :]


def unpack_kernel(scal, q, k, v, other, wt, w):
    rows = head_rows(scal[0])
    parts = []
    for i, own in enumerate((q, k, v)):
        there = slice(2 * DH * i, 2 * DH * (i + 1))
        both = jnp.concatenate((own[rows, :].astype(F32), other[there, :].astype(F32)), 1)
        gap = jnp.zeros((PITCH - DH, both.shape[1]), F32)
        parts += [both[:DH], gap, both[DH:], gap]
    whole = jnp.concatenate(parts, 0).astype(BF)
    wt[...] = whole
    w[...] = whole.T


def norm_qkv_kernel(
    scal, a00, b00, a01, b01, a10, b10, a11, b11, weights, bias, small, small_y,
    h_ref, qkv_ref, kv_ref, res_ref, gain_s, shift_s, bias_s,
):
    ypos, me = scal[0], scal[1]
    half = a00.shape[0]
    gain_s[...] = jnp.broadcast_to(column(0, small, small_y), gain_s.shape)
    shift_s[...] = jnp.broadcast_to(column(1, small, small_y), shift_s.shape)
    bias_s[...] = jnp.broadcast_to(column(0, bias), bias_s.shape)
    sources = {(0, 0): (a00, b00), (1, 0): (a01, b01), (0, 1): (a10, b10), (1, 1): (a11, b11)}
    for p, (rc, ry, rx) in enumerate(spots()):
        here = slice(p * SUB, (p + 1) * SUB)
        there = span(block_of(me, rc, ry, rx))
        cols = span(ypos ^ ry)
        sa, sb = sources[(rc, rx)]
        raw = jnp.concatenate((sa[:, cols], sb[:, cols]), 0)
        if rc == 0 and ry == 0:
            res_ref[:, rx * SUB : (rx + 1) * SUB] = raw
        v = raw.astype(F32)
        mean = jnp.sum(v, axis=0, keepdims=True) / (2 * half)
        square = jnp.sum(v * v, axis=0, keepdims=True) / (2 * half)
        root = lax.rsqrt(square - mean * mean + EPSILON)
        hidden = ((v - mean) * root * gain_s[...] + shift_s[...]).astype(BF)
        h_ref[:, here] = hidden
        qkv = (dot(weights[...], hidden) + bias_s[...]).astype(BF)
        qkv_ref[:, there] = qkv
        for i in range(4):
            kv_ref[there, 128 * i : 128 * i + PITCH] = qkv[PITCH * (2 + i) : PITCH * (3 + i), :].T


def attend_kernel(scal, klo, khi, qkv, kv, lo, hi, o0, o1, lse, s_ref, acc_ref):
    me = scal[1]
    outs = (o0, o1)
    places = lax.broadcasted_iota(jnp.int32, (SUB, SUB), 0)
    lanes = lax.broadcasted_iota(jnp.int32, (1, SUB), 1)
    for rc, ry, rx in sorted(spots(), reverse=True):
        block = block_of(me, rc, ry, rx)
        cols = span(block)
        low, high = lo[:, cols], hi[:, cols]
        own = lanes + block * SUB

        def score(kb, tops):
            base = kb * SUB
            allowed = ((places >= low - base) & (places < high - base)) | (places == own - base)
            new = []
            for h in range(2):
                s = dot(kv[span(kb), 128 * h : 128 * h + PITCH], qkv[PITCH * h : PITCH * (h + 1), cols])
                s = jnp.where(allowed, s, MASKED)
                s_ref[h, span(kb), :] = s
                new.append(jnp.maximum(tops[h], jnp.max(s.reshape(SUB // 8, 8, SUB), axis=0)))
            return tuple(new)

        start = jnp.full((8, SUB), MASKED, F32)
        tops = lax.fori_loop(klo[block], khi[block], score, (start, start))
        tops = [jnp.max(t, axis=0, keepdims=True) * SCALE2 for t in tops]
        acc_ref[...] = jnp.zeros_like(acc_ref)

        def weigh(kb, carry):
            for h in range(2):
                weights = jnp.exp2(s_ref[h, span(kb), :] * SCALE2 - tops[h]).astype(BF)
                acc_ref[h] += dot(qkv[PITCH * (4 + h) : PITCH * (5 + h), span(kb)], weights)
            return carry

        lax.fori_loop(klo[block], khi[block], weigh, 0)
        heads = []
        for h in range(2):
            total = acc_ref[h, DH : DH + 1, :]
            heads.append(acc_ref[h, :DH, :] / total)
            lse[h : h + 1, cols] = tops[h] + jnp.log2(total)
        rows = slice(rc * 2 * DH, (rc + 1) * 2 * DH)
        outs[ry][rows, rx * SUB : (rx + 1) * SUB] = jnp.concatenate(heads, 0).astype(BF)


def attend_back_kernel(
    scal, qlo, qhi, qkv, kv, lo, hi, lse, o0, o1, g0, gx, gy, gxy, s0, sx, sy, sxy,
    out, gt, delta, dqt, dk, dv,
):
    me = scal[1]
    outs = (o0, o1)
    n2 = 2 * DH
    grads = (g0, gx, gy, gxy, s0, sx, sy, sxy)
    for p, (rc, ry, rx) in enumerate(spots()):
        cols = span(block_of(me, rc, ry, rx))
        rows = slice(rc * n2, (rc + 1) * n2)
        gtile = (grads[p][...] if p in (0, 4) else grads[p][rows, :]).astype(F32)
        both = gtile * outs[ry][rows, rx * SUB : (rx + 1) * SUB].astype(F32)
        for h in range(2):
            part = slice(DH * h, DH * (h + 1))
            padded = jnp.concatenate((gtile[part], jnp.zeros((PITCH - DH, SUB), F32)), 0)
            gt[PITCH * h : PITCH * (h + 1), cols] = padded.astype(BF)
            delta[h : h + 1, cols] = jnp.sum(both[part], axis=0, keepdims=True)
    dqt[...] = jnp.zeros_like(dqt)
    dk[...] = jnp.zeros_like(dk)
    dv[...] = jnp.zeros_like(dv)
    places = lax.broadcasted_iota(jnp.int32, (SUB, SUB), 0)
    lanes = lax.broadcasted_iota(jnp.int32, (1, SUB), 1)

    @pl.loop(0, 8)
    def _(kb):
        keys = span(kb)
        base = kb * SUB

        def body(qb, carry):
            cols = span(qb)
            low, high = lo[:, cols] - base, hi[:, cols] - base
            own = lanes + (qb * SUB - base)
            allowed = ((places >= low) & (places < high)) | (places == own)
            for h in range(2):
                head = slice(PITCH * h, PITCH * (h + 1))
                s = dot(kv[keys, 128 * h : 128 * h + PITCH], qkv[head, cols])
                probs = jnp.where(allowed, jnp.exp2(s * SCALE2 - lse[h : h + 1, cols]), 0.0)
                gprobs = dot(kv[keys, 256 + 128 * h : 256 + 128 * h + PITCH], gt[head, cols])
                gscores = (probs * (gprobs - delta[h : h + 1, cols])).astype(BF)
                dv[h, keys, :] += dot_nt(probs.astype(BF), gt[head, cols])
                dk[h, keys, :] += dot_nt(gscores, qkv[head, cols])
                dqt[head, cols] += dot(qkv[PITCH * (2 + h) : PITCH * (3 + h), keys], gscores)
            return carry

        lax.fori_loop(qlo[kb], qhi[kb], body, 0)

    for p, (rc, ry, rx) in enumerate(spots()):
        here = slice(p * SUB, (p + 1) * SUB)
        rows = span(block_of(me, rc, ry, rx))
        out[: 2 * PITCH, here] = (dqt[:, rows] * SCALE).astype(BF)
        for h in range(2):
            out[PITCH * (2 + h) : PITCH * (3 + h), here] = (dk[h, rows, :].T * SCALE).astype(BF)
            out[PITCH * (4 + h) : PITCH * (5 + h), here] = dv[h, rows, :].T.astype(BF)


def own_and_y(ypos, w):
    return [w[head_rows(ypos), :], w[head_rows(1 - ypos), :]]


def out_weights_kernel(scal, own_a, own_b, x_a, x_b, w):
    parts = []
    for a, b in ((own_a, own_b), (x_a, x_b)):
        for wa, wb in zip(own_and_y(scal[0], a), own_and_y(scal[0], b)):
            parts.append(jnp.concatenate((wa, wb), 1))
    w[...] = jnp.concatenate(parts, 0)


def mix_kernel(own, y, x, xy, sib, ysib, xsib, xysib, w, w_sib, res, small, small_y, mixed, h2t, h2):
    n2 = 2 * DH
    gain, shift, bias = [column(i, small, small_y) for i in (2, 3, 4)]
    parts = []
    for rows, group in ((slice(0, n2), (own, y, x, xy)), (slice(n2, 2 * n2), (sib, ysib, xsib, xysib))):
        for i, o in enumerate(group):
            if i < 2:
                parts.append(o[rows, :])
            else:
                parts.append(jnp.concatenate((o[rows, SUB:], o[rows, :SUB]), 1))
    att = jnp.concatenate(parts, 0)
    weights = jnp.concatenate((w[...], w_sib[...]), 0)
    v = res[...].astype(F32) + dot_tn(weights, att) + bias
    mixed[...] = v
    mean = jnp.mean(v, axis=0, keepdims=True)
    root = lax.rsqrt(jnp.mean(v * v, axis=0, keepdims=True) - mean * mean + EPSILON)
    hidden = ((v - mean) * root * gain + shift).astype(BF)
    h2t[...] = hidden
    h2[...] = hidden.T


def turn_kernel(oa, ob, xa, xb, gof, go):
    half = oa.shape[0]
    for rx, (a, b) in enumerate(((oa, ob), (xa, xb))):
        here = slice(rx * SUB, (rx + 1) * SUB)
        gof[:half, here] = a[...]
        gof[half:, here] = b[...]
        go[here, :] = jnp.concatenate((a[...], b[...]), 0).T


def gelu_both(u):
    square = u * u
    tangent = jnp.tanh(GELU_C * (u + GELU_A * square * u))
    plus = 0.5 * (1.0 + tangent)
    slope = plus + 0.5 * u * (1.0 - tangent * tangent) * GELU_C * (1.0 + 3.0 * GELU_A * square)
    return u * plus, slope


def fetch(sources, buffers, sems):
    half = sources[0].shape[0]
    copies = []
    for i, src in enumerate(sources):
        dst = buffers[i // 2].at[pl.ds((i % 2) * half, half), :]
        copies.append(pltpu.make_async_copy(src, dst, sems.at[i]))
        copies[-1].start()
    return copies


def feed_half(h2, go, bias, u, d, copies, act, gu, sums):
    for c in copies[:2]:
        c.wait()
    upper = dot(h2[...], u[...]) + bias
    value, slope = gelu_both(upper)
    act[...] = value.astype(BF)
    for c in copies[2:]:
        c.wait()
    rounded = (dot(go[...], d[...]) * slope).astype(BF)
    gu[...] = rounded
    sums[...] = jnp.broadcast_to(jnp.sum(rounded.astype(F32), axis=0, keepdims=True), sums.shape)
    return dot_nt(u[...], gu[...])


def feed_own_kernel(h2, go, bias, ua, ub, da, db, act, gu, sums, part, u, d, sems):
    copies = fetch((ua, ub, da, db), (u, d), sems)
    part[...] = feed_half(h2, go, bias[0:1, :], u, d, copies, act, gu, sums)


def feed_sib_kernel(h2, go, bias, part, ua, ub, da, db, act, gu, sums, send, own, u, d, sems):
    copies = fetch((ua, ub, da, db), (u, d), sems)
    total = feed_half(h2, go, bias[1:2, :], u, d, copies, act, gu, sums) + part[...]
    send[...] = total[:, SUB:].astype(BF)
    own[...] = total[:, :SUB]


def padded_units(v, width):
    return jnp.concatenate((v, jnp.zeros((v.shape[0], width - v.shape[1]), v.dtype)), 1)


def outers_kernel(gof, act, h2t, gu, sums, down, up):
    width, rows = down.shape[1], h2t.shape[0]
    down[...] = padded_units(dot(gof[...], act[...]).astype(BF), width)
    up[:rows, :] = padded_units(dot(h2t[...], gu[...]).astype(BF), width)
    up[rows:, :] = padded_units(jnp.concatenate((sums[...], sums[...]), 0).astype(BF), width)


def down_own_kernel(gof, act, recv, keep, send):
    half, width = keep.shape
    total = padded_units(dot(gof[...], act[...]), width) + recv[...].astype(F32)
    keep[...] = total[:half]
    send[...] = total[half:].astype(BF)


def up_own_kernel(h2t, gu, sums, recv, keep, send):
    half = h2t.shape[0] // 2
    width = keep.shape[1]
    total = padded_units(dot(h2t[...], gu[...]), width) + recv[: 2 * half, :].astype(F32)
    more = padded_units(jnp.concatenate((sums[...], sums[...]), 0), width) + recv[2 * half :, :].astype(F32)
    keep[:half, :] = total[:half]
    keep[half:, :] = more
    send[:half, :] = total[half:].astype(BF)
    send[half:, :] = more.astype(BF)


def result_kernel(act0, act1, mixed, small, small_y, daa, dba, das, dbs, send, own, d0, d1, sems):
    copies = fetch((daa, dba, das, dbs), (d0, d1), sems)
    for c in copies:
        c.wait()
    part = dot_nt(d0[...], act0[...]) + dot_nt(d1[...], act1[...])
    send[...] = part[:, SUB:].astype(BF)
    own[...] = part[:, :SUB] + mixed[:, :SUB] + column(5, small, small_y)


def result_sum_kernel(own, recv, out_a, out_b):
    half = out_a.shape[0]
    total = (own[...] + recv[...].astype(F32)).astype(BF)
    out_a[...] = total[:half]
    out_b[...] = total[half:]


def place_kernel(scal, own, other, out):
    out[:, span(scal[0])] = own[...]
    out[:, span(1 - scal[0])] = other[...]


def norm2_back_kernel(
    own, recv, mixed, goa, gob, small, small_y, w, w_sib, gm, low, low_b, g_own, g_sib, g_y, g_x, g_xy, sums
):
    e = own[...] + recv[...].astype(F32)
    v = mixed[:, :SUB]
    mean = jnp.mean(v, axis=0, keepdims=True)
    root = lax.rsqrt(jnp.mean(v * v, axis=0, keepdims=True) - mean * mean + EPSILON)
    n = (v - mean) * root
    weighted = e * column(2, small, small_y)
    go = jnp.concatenate((goa[...], gob[...]), 0).astype(F32)
    grad = go + root * (
        weighted
        - jnp.mean(weighted, axis=0, keepdims=True)
        - n * jnp.mean(weighted * n, axis=0, keepdims=True)
    )
    gm[...] = grad
    rounded = grad.astype(BF)
    low[...] = rounded
    low_b[...] = rounded[low_b.shape[0] :]
    n2 = 2 * DH
    mine = dot(w[...], rounded).astype(BF)
    sibs = dot(w_sib[...], rounded).astype(BF)
    g_own[...] = mine[:n2]
    g_sib[...] = sibs[:n2]
    for i, out in enumerate((g_y, g_x, g_xy)):
        rows = slice(n2 * (i + 1), n2 * (i + 2))
        out[:n2, :] = mine[rows]
        out[n2:, :] = sibs[rows]
    for i, q in enumerate((e * n, e, grad, go)):
        sums[i : i + 1, :] = row_of(jnp.sum(q, axis=1, keepdims=True))
    sums[4:, :] = jnp.zeros_like(sums[4:, :])


def heads_outer_kernel(scal, own, y, sib, ysib, low, low_x, sums, sums_x, keep, send):
    right = jnp.concatenate((low[...], low_x[...]), 1)
    n2 = 2 * DH
    for rows, a, b, out in ((slice(0, n2), own, y, keep), (slice(n2, 2 * n2), sib, ysib, send)):
        out[head_rows(scal[0]), :] = dot_nt(a[rows, :], right).astype(out.dtype)
        out[head_rows(1 - scal[0]), :] = dot_nt(b[rows, :], right).astype(out.dtype)
        total = sums[...] + sums_x[...]
        out[2 * n2 :, :] = jnp.concatenate((total, total), 0).astype(out.dtype)


def qkv_outer_kernel(dqkv, h1, keep_o, recv_o, own, send):
    total = dot_nt(dqkv[...], h1[...])
    half = h1.shape[0] // 2
    lanes = own.shape[1]
    rows = jnp.concatenate([total[PITCH * i : PITCH * i + DH] for i in range(6)], 0)
    n = 6 * DH
    own[:n, :] = padded_units(rows[:, :half].astype(BF), lanes)
    send[:n, :] = padded_units(rows[:, half:].astype(BF), lanes)
    col = jnp.sum(dqkv[...].astype(F32), axis=1, keepdims=True)
    cols = [col[PITCH * i : PITCH * i + DH] for i in (0, 1, 4, 5)]
    cols.append(jnp.zeros((lanes - 4 * DH, 1), F32))
    own[n : n + 16, :] = jnp.broadcast_to(row_of(jnp.concatenate(cols, 0)), (16, lanes)).astype(BF)
    outs = keep_o[...] + recv_o[...].astype(F32)
    own[n + 16 :, :] = padded_units(outs[:, :half].astype(BF), lanes)
    send[n:, :] = padded_units(outs[:, half:].astype(BF), lanes)


def gather_kernel(own, recv, out):
    n = 6 * DH
    out[: n + 16, :] = own[: n + 16, :]
    out[n + 16 : 2 * n + 16, :] = recv[:n, :]
    out[2 * n + 16 :, :] = (own[n + 16 :, :].astype(F32) + recv[n:, :].astype(F32)).astype(BF)


def part_kernel(w, dqkv, send):
    send[...] = dot(w[...], dqkv[:, 4 * SUB :]).astype(BF)


HALF = SUB // 2


def spread_kernel(w, dqkv, recv, to_x, to_y, keep_p, keep_q):
    half = w.shape[0] // 2
    total = dot(w[...], dqkv[:, : 4 * SUB]) + recv[...].astype(F32)
    for ry in range(2):
        at = slice(ry * HALF, (ry + 1) * HALF)
        for rx in range(2):
            first = (ry * 2 + rx) * SUB
            p = total[:, first : first + HALF]
            q = total[:, first + HALF : first + SUB]
            if rx == 0:
                keep_p[:, at] = p
            else:
                to_x[:, at] = p.astype(BF)
            where = slice((ry * 2 + rx) * HALF, (ry * 2 + rx + 1) * HALF)
            keep_q[:, where] = q[:half]
            to_y[:, where] = q[half:].astype(BF)


def spread2_kernel(keep_p, keep_q, from_x, from_y, to_x, to_y, own_p, own_q):
    half = own_p.shape[0]
    p = keep_p[...] + from_x[...].astype(F32)
    own_p[...] = p[:half]
    to_y[...] = p[half:].astype(BF)
    for ry in range(2):
        at = slice(ry * HALF, (ry + 1) * HALF)
        for rx in range(2):
            mine = slice((ry * 2 + rx) * HALF, (ry * 2 + rx + 1) * HALF)
            theirs = slice(((1 - ry) * 2 + rx) * HALF, ((1 - ry) * 2 + rx + 1) * HALF)
            q = keep_q[:, mine] + from_y[:, theirs].astype(F32)
            if rx == 0:
                own_q[:, at] = q
            else:
                to_x[:, at] = q.astype(BF)


def norm1_stats_kernel(scal, own_p, own_q, from_x, from_y, a, b, small, grad, normed, stats, sums):
    ypos = scal[0]
    half = a.shape[0]
    gain = column(0, small)
    cols_sums = [0.0, 0.0]
    for ry in range(2):
        at = slice(ry * HALF, (ry + 1) * HALF)
        other = slice((1 - ry) * HALF, (2 - ry) * HALF)
        e = jnp.concatenate(
            (own_p[:, at] + from_y[:, other].astype(F32), own_q[:, at] + from_x[:, at].astype(F32)), 1
        )
        here = slice(ry * SUB, (ry + 1) * SUB)
        cols = span(ypos ^ ry)
        va, vb = a[:, cols].astype(F32), b[:, cols].astype(F32)
        mean = (jnp.sum(va, 0, keepdims=True) + jnp.sum(vb, 0, keepdims=True)) / (2 * half)
        square = (jnp.sum(va * va, 0, keepdims=True) + jnp.sum(vb * vb, 0, keepdims=True)) / (2 * half)
        root = lax.rsqrt(square - mean * mean + EPSILON)
        n = (va - mean) * root
        w = e * gain
        grad[:, here] = w
        normed[:, here] = n
        stats[0:1, here] = jnp.sum(w, 0, keepdims=True)
        stats[1:2, here] = jnp.sum(w * n, 0, keepdims=True)
        stats[2:3, here] = root
        cols_sums[0] += jnp.sum(e * n, 1, keepdims=True)
        cols_sums[1] += jnp.sum(e, 1, keepdims=True)
    stats[3:, :] = jnp.zeros_like(stats[3:, :])
    for i in range(2):
        sums[i : i + 1, :] = row_of(cols_sums[i])
    sums[2:, :] = jnp.zeros_like(sums[2:, :])


def norm1_back_kernel(scal, grad, normed, stats, recv, gm_own, gm_y, out):
    ypos = scal[0]
    width = 2 * grad.shape[0]
    for ry in range(2):
        here = slice(ry * SUB, (ry + 1) * SUB)
        other = slice((1 - ry) * SUB, (2 - ry) * SUB)
        total = (stats[0:1, here] + recv[0:1, other]) / width
        along = (stats[1:2, here] + recv[1:2, other]) / width
        gm = gm_own[: grad.shape[0], :] if ry == 0 else gm_y[...].astype(F32)
        whole = gm + stats[2:3, here] * (grad[:, here] - total - normed[:, here] * along)
        out[:, span(ypos ^ ry)] = whole.astype(BF)


def local(
    layer_input, picture, token_kept, ln1_gain, ln1_bias, w_query, b_query, w_key, w_value, b_value,
    w_out, b_out, ln2_gain, ln2_bias, w_up, b_up, w_down, b_down, grad_out,
):
    ypos = lax.axis_index("tc").astype(jnp.int32)
    trpos = lax.axis_index("tr").astype(jnp.int32)
    me = trpos * 2 + ypos
    half = layer_input.shape[1]
    width = 2 * half
    seq = picture.shape[0]
    n2 = b_query.shape[0]
    units = w_up.shape[1]
    n_up = b_up.shape[0]
    scal = jnp.stack((ypos, me))
    two = 2 * SUB

    a00 = layer_input.T
    qkv_weights = (w_query.T, w_key.T, w_value.T)
    go_t = grad_out.T
    u_aa, d_aa = w_up, w_down.T
    small = jnp.stack(
        (ln1_gain, ln1_bias, ln2_gain, ln2_bias, b_out, b_down, jnp.pad(b_up, (0, half - n_up)), ln1_gain)
    )
    (w_send,) = call(pack_kernel, "pack", (scal,), qkv_weights, (shape(3 * n2, half),), 1)
    b00, a10, a01, small_y, d_as = py(a00), px(a00), pc(a00), py(small), pc(d_aa)
    go_a = cols_at(go_t, ypos * SUB, SUB)
    go_send = cols_at(go_t, (1 - ypos) * SUB, SUB)
    quarter = half // lax.axis_size("dp")
    first = lax.axis_index("dp") * quarter
    u_part, d_part = rows_at(u_aa, first, quarter), rows_at(d_aa, first, quarter)
    qkv_bias = jnp.concatenate((b_query, jnp.zeros_like(b_query), b_value)).reshape(6, DH)
    ones = (jnp.arange(6) >= 4).astype(F32)[:, None]
    qkv_bias = jnp.concatenate((qkv_bias, ones, jnp.zeros((6, PITCH - DH - 1), F32)), 1).reshape(1, -1)
    qkv_bias = jnp.broadcast_to(qkv_bias, (8, 6 * PITCH))

    numbers = jnp.arange(8, dtype=jnp.int32)[:, None]
    hot = (picture[None, :] == numbers).astype(jnp.int32)
    counts = jnp.sum(hot, axis=1)
    kept = jnp.sum(hot * token_kept[None, :], axis=1)
    starts = jnp.cumsum(counts) - counts
    lo = jnp.sum(hot * starts[:, None], axis=0)
    hi = jnp.sum(hot * (starts + kept)[:, None], axis=0)
    end = jnp.sum(hot * (starts + counts)[:, None], axis=0)
    blocks = seq // SUB
    klo = qlo = lo.reshape(blocks, SUB)[:, 0] // SUB
    lasts = jnp.arange(1, blocks + 1, dtype=jnp.int32) * SUB
    khi = (jnp.maximum(lasts, hi.reshape(blocks, SUB)[:, -1]) + SUB - 1) // SUB
    qhi = (jnp.maximum(lasts, end.reshape(blocks, SUB)[:, -1]) + SUB - 1) // SUB
    lo, hi = lo[None, :], hi[None, :]

    b00, a10, a01, small_y, d_as, w_send, u_part = phase(b00, a10, a01, small_y, d_as, w_send, u_part)
    b10, w_other, b01, a11, u_part = px(b00), py(w_send), pc(b00), pc(a10), py(u_part)
    b10, w_other, b01, a11, u_part, w_out1, go_send, go_a, d_part = phase(
        b10, w_other, b01, a11, u_part, w_out, go_send, go_a, d_part
    )
    u_ba = lax.all_gather(u_part, "dp", axis=0, tiled=True)
    b11, w0b, w2a, go_b, d_part = pc(b10), py(w_out1), px(w_out1), py(go_send), py(d_part)
    go_xa = px(after(go_a, b11))
    wt_all, w_all = call(
        unpack_kernel, "unpack", (scal,), qkv_weights + (w_other,),
        (shape(6 * PITCH, width), shape(width, 6 * PITCH)), 2,
    )
    h1, qkv, kv, resid = call(
        norm_qkv_kernel, "norm_qkv", (scal,),
        (a00, b00, a01, b01, a10, b10, a11, b11, wt_all, qkv_bias, small, small_y),
        (shape(width, seq), shape(6 * PITCH, seq), shape(seq, 512), shape(width, two)),
        8,
        scratch=[pltpu.VMEM((width, SUB), F32)] * 2 + [pltpu.VMEM((6 * PITCH, SUB), F32)],
    )

    o0, o1, lse = call(
        attend_kernel, "attend", (scal, klo, khi), (qkv, kv, lo, hi),
        (shape(2 * n2, two),) * 2 + (shape(2, seq, dtype=F32),), 12,
        scratch=[pltpu.VMEM((2, seq, SUB), F32), pltpu.VMEM((2, PITCH, SUB), F32)],
    )
    o0, o1, w0b, w2a, go_b, go_xa, d_part, u_ba = phase(o0, o1, w0b, w2a, go_b, go_xa, d_part, u_ba)
    d_ba = lax.all_gather(d_part, "dp", axis=0, tiled=True)
    att_y, att_x, att_s, w2b, go_xb = py(o1), px(o0), pc(o0), py(w2a), px(go_b)
    up_y = small_y[6, :n_up]
    up_own = jnp.where(ypos == 0, jnp.concatenate((b_up, up_y)), jnp.concatenate((up_y, b_up)))
    att_y, att_x, att_s, w2b, go_xb, up_own, u_aa1 = phase(att_y, att_x, att_s, w2b, go_xb, up_own, u_aa)
    att_xy, att_sy, att_sx, u_as, up_sib = px(att_y), pc(att_y), pc(att_x), pc(u_aa1), pc(up_own)
    (wo,) = call(out_weights_kernel, "out_weights", (scal,), (w_out, w0b, w2a, w2b), (shape(4 * n2, width),), 1)
    gof, go = call(
        turn_kernel, "turn", (), (go_a, go_b, go_xa, go_xb), (shape(width, two), shape(two, width)), 2
    )
    att_xy, att_sy, att_sx, wo1, u_as, up_sib, u_ba, d_ba = phase(
        att_xy, att_sy, att_sx, wo, u_as, up_sib, u_ba, d_ba
    )
    att_sxy, wo_sib, u_bs, d_bs = pc(att_xy), pc(wo1), pc(u_ba), pc(d_ba)
    bias_up = jnp.stack((up_own, up_sib))
    mixed, h2t, h2 = call(
        mix_kernel, "mix", (),
        (o0, att_y, att_x, att_xy, att_s, att_sy, att_sx, att_sxy, wo, wo_sib, resid, small, small_y),
        (shape(width, two, dtype=F32), shape(width, two), shape(two, width)), 5,
    )
    held = pltpu.VMEM((width, units), BF)
    four = pltpu.SemaphoreType.DMA((4,))
    u_shape = shape(two, units)
    sum_shape = shape(8, units, dtype=F32)
    act0, gu0, gu_sums0, gh_part = call(
        feed_own_kernel, "feed_own", (), (h2, go, bias_up),
        (u_shape, u_shape, sum_shape, shape(width, two, dtype=F32)), 7, vmem=24,
        scratch=[held, held, four], far=(u_aa, u_ba, d_aa, d_ba),
    )
    act1, gu1, gu_sums1, gh_send, gh_own = call(
        feed_sib_kernel, "feed_sib", (), (h2, go, bias_up, gh_part),
        (u_shape, u_shape, sum_shape, shape(width, SUB), shape(width, SUB, dtype=F32)), 7, vmem=24,
        scratch=[held, held, four], far=(u_as, u_bs, d_as, d_bs),
    )
    gh_recv = px(gh_send)
    wide = (units + 127) // 128 * 128
    d_send, u_send = call(
        outers_kernel, "outers", (), (gof, act1, h2t, gu1, gu_sums1), (shape(width, wide), shape(width + 16, wide)), 4
    )
    d_recv, u_recv = pc(d_send), pc(u_send)
    keep_d, d_send = call(
        down_own_kernel, "down_own", (), (gof, act0, d_recv), (shape(half, wide, dtype=F32), shape(half, wide)), 2,
    )
    d_recv = py(d_send)
    keep_u, u_send = call(
        up_own_kernel, "up_own", (), (h2t, after(gu0, d_send), gu_sums0, u_recv),
        (shape(half + 16, wide, dtype=F32), shape(half + 16, wide)), 2,
    )
    r_send, r_own = call(
        result_kernel, "result", (), (act0, act1, after(mixed, u_send), small, small_y),
        (shape(width, SUB), shape(width, SUB, dtype=F32)), 6, vmem=20,
        scratch=[held, held, four], far=(d_aa, d_ba, d_as, d_bs),
    )
    gm, low, low_b, g_own, g_sib, g_y, g_x, g_xy, sums2 = call(
        norm2_back_kernel, "norm2_back", (),
        (gh_own, gh_recv, mixed, go_a, go_b, after(small, r_send), small_y, wo, wo_sib),
        (shape(width, SUB, dtype=F32), shape(width, SUB), shape(half, SUB))
        + (shape(n2, SUB),) * 2
        + (shape(2 * n2, SUB),) * 3
        + (shape(8, width, dtype=F32),),
        4,
    )
    g_x, g_xy, g_y, g_s = px(g_x), px(g_xy), py(g_y), pc(g_sib)
    g_x, g_xy, g_y, g_s, low1, r_send, u_send = phase(g_x, g_xy, g_y, g_s, low, r_send, u_send)
    g_xy, g_sx, g_sy = py(g_xy), pc(g_x), pc(g_y)
    g_xy, g_sx, g_sy, d_recv = phase(g_xy, g_sx, g_sy, d_recv)
    g_sxy = pc(g_xy)
    d_sum = (keep_d + d_recv.astype(F32)).astype(BF)
    low_x, u_recv, d_in, r_recv, sums2_x = px(low1), py(after(u_send, d_recv)), line(0, d_sum), px(r_send), px(sums2)
    heads = phase(qkv, kv, lo, hi, lse, o0, o1, g_own, g_x, g_y, g_xy, g_s, g_sx, g_sy, g_sxy, d_sum)[:-1]
    (dqkv,) = call(
        attend_back_kernel, "attend_back", (scal, qlo, qhi), heads, (shape(6 * PITCH, seq),), 19,
        scratch=[
            pltpu.VMEM((2 * PITCH, seq), BF), pltpu.VMEM((2, seq), F32), pltpu.VMEM((2 * PITCH, seq), F32),
            pltpu.VMEM((2, seq, PITCH), F32), pltpu.VMEM((2, seq, PITCH), F32),
        ],
    )
    dqkv, low_x, u_recv, d_in, r_recv, sums2_x = phase(dqkv, low_x, u_recv, d_in, r_recv, sums2_x)
    d_sum = line_sum(d_sum, d_in)
    u_sum = (keep_u + u_recv.astype(F32)).astype(BF)

    (p_send,) = call(part_kernel, "part", (), (w_all, dqkv), (shape(width, 4 * SUB),), 3)
    d_in, u_in, p_recv = line(1, d_sum), line(0, u_sum), pc(p_send)
    keep_o, o_send = call(
        heads_outer_kernel, "heads_outer", (scal,), (o0, att_y, att_s, att_sy, after(low, p_send), low_x, sums2, sums2_x),
        (shape(2 * n2 + 16, width, dtype=F32), shape(2 * n2 + 16, width)), 2,
    )
    o_recv = pc(o_send)
    r_a, r_b = call(
        result_sum_kernel, "result_sum", (), (r_own, after(r_recv, o_send)), (shape(half, SUB), shape(half, SUB)), 1
    )
    lanes = (half + 127) // 128 * 128
    q_own, q_send = call(
        qkv_outer_kernel, "qkv_outer", (), (after(dqkv, r_b), h1, keep_o, o_recv),
        (shape(5 * n2 + 32, lanes), shape(5 * n2 + 16, lanes)), 4,
    )
    to_x, to_y, keep_p, keep_q = call(
        spread_kernel, "spread", (), (w_all, after(dqkv, q_send), p_recv),
        (shape(width, SUB), shape(half, two), shape(width, SUB, dtype=F32), shape(half, two, dtype=F32)), 4,
    )
    q_y, from_x, from_y = py(q_send), px(to_x), py(to_y)
    from_x, from_y, q_y, d_in, u_in = phase(from_x, from_y, q_y, d_in, u_in)
    d_sum, u_sum = line_sum(d_sum, d_in), line_sum(u_sum, u_in)
    to_x2, to_y2, own_p, own_q = call(
        spread2_kernel, "spread2", (), (keep_p, keep_q, from_x, from_y),
        (shape(half, SUB), shape(half, SUB), shape(half, SUB, dtype=F32), shape(half, SUB, dtype=F32)), 2,
    )
    (qo_sum,) = call(gather_kernel, "gather", (), (q_own, q_y), (shape(8 * n2 + 32, lanes),), 1)
    from_x2, from_y2 = px(to_x2), py(to_y2)
    d_in, u_in, qo_in = line(2, d_sum), line(1, u_sum), line(0, qo_sum)
    from_x2, from_y2, low_b, r_b = phase(from_x2, from_y2, low_b, r_b)
    grad, normed, stats, sums1 = call(
        norm1_stats_kernel, "norm1_stats", (scal,), (own_p, own_q, from_x2, from_y2, a00, b00, small),
        (shape(half, two, dtype=F32), shape(half, two, dtype=F32), shape(8, two, dtype=F32), shape(8, half, dtype=F32)),
        2,
    )
    stats_y, sums1_c = py(stats), pc(sums1)
    stats_y, sums1_c, low_b, r_b = phase(stats_y, sums1_c, low_b, r_b)
    sums1 = sums1 + sums1_c
    sums1_x, low_y = px(sums1), py(low_b)
    d_in, u_in, qo_in, sums1_x, low_y, r_b = phase(d_in, u_in, qo_in, sums1_x, low_y, r_b)
    u_sum, qo_sum = line_sum(u_sum, u_in), line_sum(qo_sum, qo_in)
    sums1 = sums1 + sums1_x
    u_in, qo_in, sums1_z, r_y = line(2, u_sum), line(1, qo_sum), dp_step(sums1, 1), py(r_b)
    dwd = line_end(d_sum, d_in)
    (gin,) = call(
        norm1_back_kernel, "norm1_back", (scal,), (grad, normed, stats, stats_y, gm, low_y), (shape(half, two),), 1,
    )
    u_in, qo_in, sums1_z, gin, r_y, dwd = phase(u_in, qo_in, sums1_z, gin, r_y, dwd)
    sums1 = sums1 + sums1_z
    qo_sum = line_sum(qo_sum, qo_in)
    qo_in, sums1_z = line(2, qo_sum), dp_step(sums1, 2)
    dwu = line_end(u_sum, u_in)
    (result,) = call(place_kernel, "place", (scal,), (r_a, r_y), (shape(half, two),), 1)
    qo_in, sums1_z, dwu, result = phase(qo_in, sums1_z, dwu, result)
    sums1 = dp_last(sums1 + sums1_z)
    qo = line_end(qo_sum, qo_in)[:, :half]
    dwq_own, dwq_y, dwo = qo[: 3 * n2 + 16], qo[3 * n2 + 16 : 6 * n2 + 16], qo[6 * n2 + 16 :]

    bias_q = dwq_own[3 * n2]
    dwq_own = dwq_own[: 3 * n2]
    first = jnp.where(ypos == 0, dwq_own, dwq_y).reshape(3, n2, half)
    second = jnp.where(ypos == 0, dwq_y, dwq_own).reshape(3, n2, half)
    dwq = jnp.concatenate((first, second), 1)
    gbu = lax.dynamic_slice_in_dim(dwu[half], ypos * n_up, n_up, 0)
    sums2 = dwo[2 * n2 :]
    return (
        result.T, gin.T, sums1[0], sums1[1], dwq[0].T, bias_q[:n2], dwq[1].T, dwq[2].T, bias_q[n2 : 2 * n2],
        dwo[: 2 * n2], sums2[2], sums2[0], sums2[1], dwu[:half, :units], gbu, dwd[:, :units].T, sums2[3],
    )


def solution(mesh):
    rows = P(("dp", "tr"), "tc")
    placed = (
        rows, P("dp"), P("dp"), P("tc"), P("tc"), P("tc", "tr"), P(("tr", "tc")), P("tc", "tr"),
        P("tc", "tr"), P(("tr", "tc")), P("tr", "tc"), P("tc"), P("tc"), P("tc"), P("tc", "tr"),
        P(("tr", "tc")), P("tr", "tc"), P("tc"), rows,
    )
    outs = (
        rows, rows, P("tc"), P("tc"), P("tc", "tr"), P(("tr", "tc")), P("tc", "tr"), P("tc", "tr"),
        P(("tr", "tc")), P("tr", "tc"), P("tc"), P("tc"), P("tc"), P("tc", "tr"), P(("tr", "tc")),
        P("tr", "tc"), P("tc"),
    )
    return jax.shard_map(local, mesh=mesh, in_specs=placed, out_specs=outs, check_vma=False)
```

```python
import jax
import jax.numpy as jnp
from jax import lax
from jax.experimental import pallas as pl
from jax.experimental.pallas import tpu as pltpu
from jax.sharding import PartitionSpec as P

DH = 72
PITCH = 80
SUB = 256
HALF = SUB // 2
EPSILON = 1e-06
GELU_C = 0.7978845608028654
GELU_A = 0.044715
MASKED = -1e30
SCALE = DH**-0.5
SCALE2 = SCALE * 1.4426950408889634
BF = jnp.bfloat16
F32 = jnp.float32
MIB = 1024 * 1024


def swap_perm(axis, bit):
    return [(i, i ^ bit) for i in range(lax.axis_size(axis))]


def px(v):
    return lax.ppermute(v, "tr", swap_perm("tr", 2))


def pc(v):
    return lax.ppermute(v, "tr", swap_perm("tr", 1))


def py(v):
    return lax.ppermute(v, "tc", swap_perm("tc", 1))


def phase(*values):
    return lax.optimization_barrier(values)


def after(v, *earlier):
    return phase(v, *earlier)[0]


def dot(a, b):
    return jnp.dot(a, b, preferred_element_type=F32)


def dot_tn(a, b):
    return lax.dot_general(a, b, (((0,), (0,)), ((), ())), preferred_element_type=F32)


def dot_nt(a, b):
    return lax.dot_general(a, b, (((1,), (1,)), ((), ())), preferred_element_type=F32)


def rows_at(v, first, count):
    return lax.dynamic_slice_in_dim(v, first, count, 0)


def cols_at(v, first, count):
    return lax.dynamic_slice_in_dim(v, first, count, 1)


def dp_swap(v, bit):
    return lax.ppermute(v, "dp", swap_perm("dp", bit))


def line(step, v):
    if lax.axis_size("dp") != 4:
        return v
    return lax.ppermute(v, "dp", ([(0, 1), (3, 2)], [(1, 2), (2, 1)], [(1, 0), (2, 3)])[step])


def line_sum(v, received):
    if lax.axis_size("dp") != 4:
        return v
    return (v.astype(F32) + received.astype(F32)).astype(BF)


def line_end(v, received):
    if lax.axis_size("dp") != 4:
        return lax.psum(v, "dp").astype(F32)
    place = lax.axis_index("dp")
    return jnp.where((place == 1) | (place == 2), v, received).astype(F32)


def dp_step(v, bit):
    return dp_swap(v, bit) if lax.axis_size("dp") == 4 else jnp.zeros_like(v)


def dp_last(v):
    return v if lax.axis_size("dp") == 4 else lax.psum(v, "dp")


VM = pl.BlockSpec(memory_space=pltpu.VMEM)
SM = pl.BlockSpec(memory_space=pltpu.SMEM)


def shape(*dims, dtype=BF):
    return jax.ShapeDtypeStruct(dims, dtype)


ANY = pl.BlockSpec(memory_space=pl.ANY)


def call(body, name, scalars, arrays, outs, us, scratch=(), vmem=14, far=()):
    return pl.pallas_call(
        body,
        out_shape=tuple(outs),
        in_specs=[SM] * len(scalars) + [VM] * len(arrays) + [ANY] * len(far),
        out_specs=tuple([VM] * len(outs)),
        scratch_shapes=list(scratch),
        compiler_params=pltpu.CompilerParams(vmem_limit_bytes=vmem * MIB),
        cost_estimate=pl.CostEstimate(
            flops=int(us * 600e6), bytes_accessed=int(us * 3e6), transcendentals=0
        ),
        name=name,
    )(*scalars, *arrays, *far)


def spots():
    return [(rc, ry, rx) for rc in range(2) for ry in range(2) for rx in range(2)]


def block_of(me, rc, ry, rx):
    return me ^ (rx * 4 + rc * 2 + ry)


def span(block):
    return pl.ds(pl.multiple_of(block * SUB, SUB), SUB)


def head_rows(pos):
    return pl.ds(pl.multiple_of(pos * 2 * DH, 16), 2 * DH)


def row_of(col):
    return jnp.broadcast_to(col, (col.shape[0], 128)).T[0:1]


def column(i, *parts):
    return jnp.concatenate([p[...].T[:, i : i + 1] for p in parts], 0)


def pack_kernel(scal, q, k, v, own, send):
    for i, w in enumerate((q, k, v)):
        there = slice(2 * DH * i, 2 * DH * (i + 1))
        own[there, :] = w[head_rows(scal[0]), :]
        send[there, :] = w[head_rows(1 - scal[0]), :]


def unpack_kernel(own, other, wt, w):
    both = jnp.concatenate((own[...].astype(F32), other[...].astype(F32)), 1)
    gap = jnp.zeros((PITCH - DH, both.shape[1]), F32)
    parts = []
    for i in range(6):
        parts += [both[DH * i : DH * (i + 1)], gap]
    whole = jnp.concatenate(parts, 0).astype(BF)
    wt[...] = whole
    w[...] = whole.T


def norm_qkv_kernel(
    scal, a00, b00, a01, b01, a10, b10, a11, b11, weights, bias, small, small_y,
    h_ref, qkv_ref, kv_ref, res_ref, gain_s, shift_s, bias_s,
):
    ypos, me = scal[0], scal[1]
    half = a00.shape[0]
    gain_s[...] = jnp.broadcast_to(column(0, small, small_y), gain_s.shape)
    shift_s[...] = jnp.broadcast_to(column(1, small, small_y), shift_s.shape)
    bias_s[...] = jnp.broadcast_to(column(0, bias), bias_s.shape)
    sources = {(0, 0): (a00, b00), (1, 0): (a01, b01), (0, 1): (a10, b10), (1, 1): (a11, b11)}
    for p, (rc, ry, rx) in enumerate(spots()):
        here = slice(p * SUB, (p + 1) * SUB)
        there = span(block_of(me, rc, ry, rx))
        cols = span(ypos ^ ry)
        sa, sb = sources[(rc, rx)]
        raw = jnp.concatenate((sa[:, cols], sb[:, cols]), 0)
        if rc == 0 and ry == 0:
            res_ref[:, rx * SUB : (rx + 1) * SUB] = raw
        v = raw.astype(F32)
        mean = jnp.sum(v, axis=0, keepdims=True) / (2 * half)
        square = jnp.sum(v * v, axis=0, keepdims=True) / (2 * half)
        root = lax.rsqrt(square - mean * mean + EPSILON)
        hidden = ((v - mean) * root * gain_s[...] + shift_s[...]).astype(BF)
        h_ref[:, here] = hidden
        qkv = (dot(weights[...], hidden) + bias_s[...]).astype(BF)
        qkv_ref[:, there] = qkv
        for i in range(4):
            kv_ref[there, 128 * i : 128 * i + PITCH] = qkv[PITCH * (2 + i) : PITCH * (3 + i), :].T


def attend_kernel(scal, klo, khi, qkv, kv, lo, hi, o0, o1, lse, s_ref, acc_ref):
    me = scal[1]
    outs = (o0, o1)
    places = lax.broadcasted_iota(jnp.int32, (SUB, SUB), 0)
    lanes = lax.broadcasted_iota(jnp.int32, (1, SUB), 1)
    for rc, ry, rx in sorted(spots(), reverse=True):
        block = block_of(me, rc, ry, rx)
        cols = span(block)
        low, high = lo[:, cols], hi[:, cols]
        own = lanes + block * SUB

        def score(kb, tops):
            base = kb * SUB
            allowed = ((places >= low - base) & (places < high - base)) | (places == own - base)
            new = []
            for h in range(2):
                s = dot(kv[span(kb), 128 * h : 128 * h + PITCH], qkv[PITCH * h : PITCH * (h + 1), cols])
                s = jnp.where(allowed, s, MASKED)
                s_ref[h, span(kb), :] = s
                new.append(jnp.maximum(tops[h], jnp.max(s.reshape(SUB // 8, 8, SUB), axis=0)))
            return tuple(new)

        start = jnp.full((8, SUB), MASKED, F32)
        tops = lax.fori_loop(klo[block], khi[block], score, (start, start))
        tops = [jnp.max(t, axis=0, keepdims=True) * SCALE2 for t in tops]
        acc_ref[...] = jnp.zeros_like(acc_ref)

        def weigh(kb, carry):
            for h in range(2):
                weights = jnp.exp2(s_ref[h, span(kb), :] * SCALE2 - tops[h]).astype(BF)
                acc_ref[h] += dot(qkv[PITCH * (4 + h) : PITCH * (5 + h), span(kb)], weights)
            return carry

        lax.fori_loop(klo[block], khi[block], weigh, 0)
        heads = []
        for h in range(2):
            total = acc_ref[h, DH : DH + 1, :]
            heads.append(acc_ref[h, :DH, :] / total)
            lse[h : h + 1, cols] = tops[h] + jnp.log2(total)
        rows = slice(rc * 2 * DH, (rc + 1) * 2 * DH)
        outs[ry][rows, rx * SUB : (rx + 1) * SUB] = jnp.concatenate(heads, 0).astype(BF)


def attend_back_kernel(
    scal, qlo, qhi, qkv, kv, lo, hi, lse, o0, o1, g0, gx, gy, gxy, s0, sx, sy, sxy,
    out0, out1, gt, delta, dqt, dk, dv,
):
    me = scal[1]
    outs = (o0, o1)
    n2 = 2 * DH
    grads = (g0, gx, gy, gxy, s0, sx, sy, sxy)
    for p, (rc, ry, rx) in enumerate(spots()):
        cols = span(block_of(me, rc, ry, rx))
        rows = slice(rc * n2, (rc + 1) * n2)
        gtile = (grads[p][...] if p in (0, 4) else grads[p][rows, :]).astype(F32)
        both = gtile * outs[ry][rows, rx * SUB : (rx + 1) * SUB].astype(F32)
        for h in range(2):
            part = slice(DH * h, DH * (h + 1))
            padded = jnp.concatenate((gtile[part], jnp.zeros((PITCH - DH, SUB), F32)), 0)
            gt[PITCH * h : PITCH * (h + 1), cols] = padded.astype(BF)
            delta[h : h + 1, cols] = jnp.sum(both[part], axis=0, keepdims=True)
    dqt[...] = jnp.zeros_like(dqt)
    dk[...] = jnp.zeros_like(dk)
    dv[...] = jnp.zeros_like(dv)
    places = lax.broadcasted_iota(jnp.int32, (SUB, SUB), 0)
    lanes = lax.broadcasted_iota(jnp.int32, (1, SUB), 1)

    @pl.loop(0, 8)
    def _(kb):
        keys = span(kb)
        base = kb * SUB

        def body(qb, carry):
            cols = span(qb)
            low, high = lo[:, cols] - base, hi[:, cols] - base
            own = lanes + (qb * SUB - base)
            allowed = ((places >= low) & (places < high)) | (places == own)
            for h in range(2):
                head = slice(PITCH * h, PITCH * (h + 1))
                s = dot(kv[keys, 128 * h : 128 * h + PITCH], qkv[head, cols])
                probs = jnp.where(allowed, jnp.exp2(s * SCALE2 - lse[h : h + 1, cols]), 0.0)
                gprobs = dot(kv[keys, 256 + 128 * h : 256 + 128 * h + PITCH], gt[head, cols])
                gscores = (probs * (gprobs - delta[h : h + 1, cols])).astype(BF)
                dv[h, keys, :] += dot_nt(probs.astype(BF), gt[head, cols])
                dk[h, keys, :] += dot_nt(gscores, qkv[head, cols])
                dqt[head, cols] += dot(qkv[PITCH * (2 + h) : PITCH * (3 + h), keys], gscores)
            return carry

        lax.fori_loop(qlo[kb], qhi[kb], body, 0)

    for p, (rc, ry, rx) in enumerate(spots()):
        out = (out0, out1)[rc]
        here = slice((ry * 2 + rx) * SUB, (ry * 2 + rx + 1) * SUB)
        rows = span(block_of(me, rc, ry, rx))
        out[: 2 * PITCH, here] = (dqt[:, rows] * SCALE).astype(BF)
        for h in range(2):
            out[PITCH * (2 + h) : PITCH * (3 + h), here] = (dk[h, rows, :].T * SCALE).astype(BF)
            out[PITCH * (4 + h) : PITCH * (5 + h), here] = dv[h, rows, :].T.astype(BF)


def own_and_y(ypos, w):
    return [w[head_rows(ypos), :], w[head_rows(1 - ypos), :]]


def out_weights_kernel(scal, own_a, own_b, x_a, x_b, w):
    parts = []
    for a, b in ((own_a, own_b), (x_a, x_b)):
        for wa, wb in zip(own_and_y(scal[0], a), own_and_y(scal[0], b)):
            parts.append(jnp.concatenate((wa, wb), 1))
    w[...] = jnp.concatenate(parts, 0)


def mix_kernel(own, y, x, xy, sib, ysib, xsib, xysib, w, w_sib, res, small, small_y, mixed, h2t, h2):
    n2 = 2 * DH
    gain, shift, bias = [column(i, small, small_y) for i in (2, 3, 4)]
    parts = []
    for rows, group in ((slice(0, n2), (own, y, x, xy)), (slice(n2, 2 * n2), (sib, ysib, xsib, xysib))):
        for i, o in enumerate(group):
            if i < 2:
                parts.append(o[rows, :])
            else:
                parts.append(jnp.concatenate((o[rows, SUB:], o[rows, :SUB]), 1))
    att = jnp.concatenate(parts, 0)
    weights = jnp.concatenate((w[...], w_sib[...]), 0)
    v = res[...].astype(F32) + dot_tn(weights, att) + bias
    mixed[...] = v
    mean = jnp.mean(v, axis=0, keepdims=True)
    root = lax.rsqrt(jnp.mean(v * v, axis=0, keepdims=True) - mean * mean + EPSILON)
    hidden = ((v - mean) * root * gain + shift).astype(BF)
    h2t[...] = hidden
    h2[...] = hidden.T


def turn_kernel(oa, ob, xa, xb, gof, go):
    half = oa.shape[0]
    for rx, (a, b) in enumerate(((oa, ob), (xa, xb))):
        here = slice(rx * SUB, (rx + 1) * SUB)
        gof[:half, here] = a[...]
        gof[half:, here] = b[...]
        go[here, :] = jnp.concatenate((a[...], b[...]), 0).T


def gelu_both(u):
    square = u * u
    tangent = jnp.tanh(GELU_C * (u + GELU_A * square * u))
    plus = 0.5 * (1.0 + tangent)
    slope = plus + 0.5 * u * (1.0 - tangent * tangent) * GELU_C * (1.0 + 3.0 * GELU_A * square)
    return u * plus, slope


def fetch(sources, buffers, sems):
    half = sources[0].shape[0]
    copies = []
    for i, src in enumerate(sources):
        dst = buffers[i // 2].at[pl.ds((i % 2) * half, half), :]
        copies.append(pltpu.make_async_copy(src, dst, sems.at[i]))
        copies[-1].start()
    return copies


def feed_up_kernel(h2, bias, ua, ub, act, slope, u, sems):
    copies = fetch((ua, ub), (u,), sems)
    for c in copies:
        c.wait()
    value, sl = gelu_both(dot(h2[...], u[...]) + bias[...])
    act[...] = value.astype(BF)
    slope[...] = sl.astype(BF)


def feed_grad(go, slope, u, d, copies, gu, sums):
    for c in copies[:2]:
        c.wait()
    rounded = (dot(go[...], d[...]) * slope[...].astype(F32)).astype(BF)
    gu[...] = rounded
    sums[...] = jnp.broadcast_to(jnp.sum(rounded.astype(F32), axis=0, keepdims=True), sums.shape)
    for c in copies[2:]:
        c.wait()
    return dot_nt(u[...], gu[...])


def feed_own_kernel(go, slope, ua, ub, da, db, gu, sums, part, u, d, sems):
    part[...] = feed_grad(go, slope, u, d, fetch((da, db, ua, ub), (d, u), sems), gu, sums)


def feed_sib_kernel(go, slope, part, act, h2t, gof, ua, ub, da, db, gu, sums, send, own, down, up, u, d, sems):
    copies = fetch((da, db, ua, ub), (d, u), sems)
    width, rows = down.shape[1], h2t.shape[0]
    down[...] = padded_units(dot(gof[...], act[...]).astype(BF), width)
    total = feed_grad(go, slope, u, d, copies, gu, sums) + part[...]
    send[...] = total[:, SUB:].astype(BF)
    own[...] = total[:, :SUB]
    up[:rows, :] = padded_units(dot(h2t[...], gu[...]).astype(BF), width)
    up[rows:, :] = padded_units(jnp.concatenate((sums[...], sums[...]), 0).astype(BF), width)


def padded_units(v, width):
    return jnp.concatenate((v, jnp.zeros((v.shape[0], width - v.shape[1]), v.dtype)), 1)


def down_own_kernel(gof, act, recv, keep0, send0, keep_rest, send_rest):
    half, width = recv.shape[0] // 2, recv.shape[1]
    total = padded_units(dot(gof[...], act[...]), width) + recv[...].astype(F32)
    rows = keep0.shape[0]
    keep0[...] = total[:rows]
    keep_rest[...] = total[rows:half]
    send0[...] = total[half : half + rows].astype(BF)
    send_rest[...] = total[half + rows :].astype(BF)


def up_own_kernel(h2t, gu, sums, recv, keep_rest, send_rest, keep1, send1, keep2, send2):
    half = h2t.shape[0] // 2
    width = recv.shape[1]
    total = padded_units(dot(h2t[...], gu[...]), width) + recv[: 2 * half, :].astype(F32)
    more = padded_units(jnp.concatenate((sums[...], sums[...]), 0), width) + recv[2 * half :, :].astype(F32)
    rest = keep_rest.shape[0]
    rows = keep1.shape[0] - rest
    keep1[:rest, :] = keep_rest[...]
    send1[:rest, :] = send_rest[...]
    keep1[rest:, :] = total[:rows]
    send1[rest:, :] = total[half : half + rows].astype(BF)
    keep2[: half - rows, :] = total[rows:half]
    keep2[half - rows :, :] = more
    send2[: half - rows, :] = total[half + rows :].astype(BF)
    send2[half - rows :, :] = more.astype(BF)


def result_kernel(act0, act1, mixed, small, small_y, daa, dba, das, dbs, send, own, d0, d1, sems):
    copies = fetch((daa, dba, das, dbs), (d0, d1), sems)
    for c in copies:
        c.wait()
    part = dot_nt(d0[...], act0[...]) + dot_nt(d1[...], act1[...])
    send[...] = part[:, SUB:].astype(BF)
    own[...] = part[:, :SUB] + mixed[:, :SUB] + column(5, small, small_y)


def result_sum_kernel(own, recv, out_a, out_b):
    half = out_a.shape[0]
    total = (own[...] + recv[: own.shape[0], :].astype(F32)).astype(BF)
    out_a[...] = total[:half]
    out_b[...] = total[half:]


def place_kernel(scal, own, other, out):
    out[:, span(scal[0])] = own[...]
    out[:, span(1 - scal[0])] = other[...]


def norm2_back_kernel(
    own, recv, mixed, goa, gob, small, small_y, w, w_sib, gm, low, low_b, g_own, g_sib, g_y, g_x, g_xy, sums_a, sums_b
):
    e = own[...] + recv[...].astype(F32)
    v = mixed[:, :SUB]
    mean = jnp.mean(v, axis=0, keepdims=True)
    root = lax.rsqrt(jnp.mean(v * v, axis=0, keepdims=True) - mean * mean + EPSILON)
    n = (v - mean) * root
    weighted = e * column(2, small, small_y)
    go = jnp.concatenate((goa[...], gob[...]), 0).astype(F32)
    grad = go + root * (
        weighted
        - jnp.mean(weighted, axis=0, keepdims=True)
        - n * jnp.mean(weighted * n, axis=0, keepdims=True)
    )
    gm[...] = grad
    rounded = grad.astype(BF)
    low[...] = rounded
    low_b[...] = rounded[low_b.shape[0] :]
    n2 = 2 * DH
    mine = dot(w[...], rounded).astype(BF)
    sibs = dot(w_sib[...], rounded).astype(BF)
    g_own[...] = mine[:n2]
    g_sib[...] = sibs[:n2]
    for i, out in enumerate((g_y, g_x, g_xy)):
        rows = slice(n2 * (i + 1), n2 * (i + 2))
        out[:n2, :] = mine[rows]
        out[n2:, :] = sibs[rows]
    for i, q in enumerate((e * n, e, grad, go)):
        col = jnp.sum(q, axis=1, keepdims=True)
        half = low_b.shape[0]
        sums_a[i : i + 1, :] = row_of(col[:half])
        sums_b[i : i + 1, :] = row_of(col[half:])
    sums_a[4:, :] = jnp.zeros_like(sums_a[4:, :])
    sums_b[4:, :] = jnp.zeros_like(sums_b[4:, :])


def heads_outer_kernel(scal, own, y, sib, ysib, low, low_x, keep, send):
    right = jnp.concatenate((low[...], low_x[...]), 1)
    n2 = 2 * DH
    for rows, a, b, out in ((slice(0, n2), own, y, keep), (slice(n2, 2 * n2), sib, ysib, send)):
        out[head_rows(scal[0]), :] = dot_nt(a[rows, :], right).astype(out.dtype)
        out[head_rows(1 - scal[0]), :] = dot_nt(b[rows, :], right).astype(out.dtype)


def gather_kernel(q_own, o_own, o_recv, out):
    n = q_own.shape[0]
    out[:n, :] = q_own[...]
    out[n:, :] = (o_own[...] + o_recv[...].astype(F32)).astype(BF)


def qkv_outer_kernel(dqkv, dqkv_sib, h1, own, send):
    mid = dqkv.shape[1]
    total = dot_nt(dqkv[...], h1[:, :mid]) + dot_nt(dqkv_sib[...], h1[:, mid:])
    half = h1.shape[0] // 2
    lanes = own.shape[1]
    rows = jnp.concatenate([total[PITCH * i : PITCH * i + DH] for i in range(6)], 0)
    n = 6 * DH
    own[:n, :] = padded_units(rows[:, :half].astype(BF), lanes)
    send[...] = padded_units(rows[:, half:].astype(BF), lanes)
    col = jnp.sum(dqkv[...].astype(F32) + dqkv_sib[...].astype(F32), axis=1, keepdims=True)
    cols = [col[PITCH * i : PITCH * i + DH] for i in (0, 1, 4, 5)]
    cols.append(jnp.zeros((lanes - 4 * DH, 1), F32))
    own[n:, :] = jnp.broadcast_to(row_of(jnp.concatenate(cols, 0)), (16, lanes)).astype(BF)


def heads_sum_kernel(keep, recv, own, send):
    half = keep.shape[1] // 2
    total = keep[...] + recv[...].astype(F32)
    own[...] = padded_units(total[:, :half], own.shape[1])
    send[...] = padded_units(total[:, half:].astype(BF), send.shape[1])


def spread_kernel(w, wt_sib, dqkv, from_sib, to_x, keep):
    total = dot(w[...], dqkv[...]) + dot_tn(wt_sib[...], from_sib[...])
    for ry in range(2):
        first = 2 * ry * SUB
        at = slice(ry * SUB, (ry + 1) * SUB)
        keep[:, at] = total[:, first : first + SUB]
        to_x[:, at] = total[:, first + SUB : first + 2 * SUB].astype(BF)


def spread2_kernel(keep, from_x, to_y, own):
    half = own.shape[0]
    total = keep[...] + from_x[...].astype(F32)
    own[...] = total[:half]
    to_y[...] = total[half:].astype(BF)


def norm1_stats_kernel(scal, own, from_y, a, b, small, sums_b, grad, normed, stats, sums):
    ypos = scal[0]
    half = a.shape[0]
    gain = column(0, small)
    cols_sums = [0.0, 0.0]
    stats[...] = jnp.zeros_like(stats)
    for ry in range(2):
        cols = span(ypos ^ ry)
        here = slice(ry * SUB, (ry + 1) * SUB)
        e = own[:, here] + from_y[:, (1 - ry) * SUB : (2 - ry) * SUB].astype(F32)
        va, vb = a[:, cols].astype(F32), b[:, cols].astype(F32)
        mean = (jnp.sum(va, 0, keepdims=True) + jnp.sum(vb, 0, keepdims=True)) / (2 * half)
        square = (jnp.sum(va * va, 0, keepdims=True) + jnp.sum(vb * vb, 0, keepdims=True)) / (2 * half)
        root = lax.rsqrt(square - mean * mean + EPSILON)
        n = (va - mean) * root
        w = e * gain
        grad[:, here] = w
        normed[:, here] = n
        stats[0:1, here] = jnp.sum(w, 0, keepdims=True)
        stats[1:2, here] = jnp.sum(w * n, 0, keepdims=True)
        stats[2:3, here] = root
        cols_sums[0] += jnp.sum(e * n, 1, keepdims=True)
        cols_sums[1] += jnp.sum(e, 1, keepdims=True)
    stats[8:, :half] = sums_b[...]
    for i in range(2):
        sums[i : i + 1, :] = row_of(cols_sums[i])
    sums[2:, :] = jnp.zeros_like(sums[2:, :])


def norm1_back_kernel(scal, grad, normed, stats, recv, gm_own, gm_y, out):
    ypos = scal[0]
    width = 2 * grad.shape[0]
    for ry in range(2):
        here = slice(ry * SUB, (ry + 1) * SUB)
        other = slice((1 - ry) * SUB, (2 - ry) * SUB)
        total = (stats[0:1, here] + recv[0:1, other]) / width
        along = (stats[1:2, here] + recv[1:2, other]) / width
        gm = gm_own[: grad.shape[0], :] if ry == 0 else gm_y[...].astype(F32)
        whole = gm + stats[2:3, here] * (grad[:, here] - total - normed[:, here] * along)
        out[:, span(ypos ^ ry)] = whole.astype(BF)


def local(
    layer_input, picture, token_kept, ln1_gain, ln1_bias, w_query, b_query, w_key, w_value, b_value,
    w_out, b_out, ln2_gain, ln2_bias, w_up, b_up, w_down, b_down, grad_out,
):
    ypos = lax.axis_index("tc").astype(jnp.int32)
    trpos = lax.axis_index("tr").astype(jnp.int32)
    me = trpos * 2 + ypos
    half = layer_input.shape[1]
    width = 2 * half
    seq = picture.shape[0]
    n2 = b_query.shape[0]
    units = w_up.shape[1]
    n_up = b_up.shape[0]
    scal = jnp.stack((ypos, me))
    two = 2 * SUB

    a00 = layer_input.T
    qkv_weights = (w_query.T, w_key.T, w_value.T)
    go_t = grad_out.T
    u_aa, d_aa = w_up, w_down.T
    small = jnp.stack(
        (ln1_gain, ln1_bias, ln2_gain, ln2_bias, b_out, b_down, jnp.pad(b_up, (0, half - n_up)), ln1_gain)
    )
    w_own, w_send = call(pack_kernel, "pack", (scal,), qkv_weights, (shape(3 * n2, half),) * 2, 1)
    b00, a10, a01, small_y, d_as = py(a00), px(a00), pc(a00), py(small), pc(d_aa)
    go_a = cols_at(go_t, ypos * SUB, SUB)
    go_send = cols_at(go_t, (1 - ypos) * SUB, SUB)
    quarter = half // lax.axis_size("dp")
    first = lax.axis_index("dp") * quarter
    u_part, d_part = rows_at(u_aa, first, quarter), rows_at(d_aa, first, quarter)
    qkv_bias = jnp.concatenate((b_query, jnp.zeros_like(b_query), b_value)).reshape(6, DH)
    ones = (jnp.arange(6) >= 4).astype(F32)[:, None]
    qkv_bias = jnp.concatenate((qkv_bias, ones, jnp.zeros((6, PITCH - DH - 1), F32)), 1).reshape(1, -1)
    qkv_bias = jnp.broadcast_to(qkv_bias, (8, 6 * PITCH))

    numbers = jnp.arange(8, dtype=jnp.int32)[:, None]
    hot = (picture[None, :] == numbers).astype(jnp.int32)
    counts = jnp.sum(hot, axis=1)
    kept = jnp.sum(hot * token_kept[None, :], axis=1)
    starts = jnp.cumsum(counts) - counts
    lo = jnp.sum(hot * starts[:, None], axis=0)
    hi = jnp.sum(hot * (starts + kept)[:, None], axis=0)
    end = jnp.sum(hot * (starts + counts)[:, None], axis=0)
    blocks = seq // SUB
    klo = qlo = lo.reshape(blocks, SUB)[:, 0] // SUB
    lasts = jnp.arange(1, blocks + 1, dtype=jnp.int32) * SUB
    khi = (jnp.maximum(lasts, hi.reshape(blocks, SUB)[:, -1]) + SUB - 1) // SUB
    qhi = (jnp.maximum(lasts, end.reshape(blocks, SUB)[:, -1]) + SUB - 1) // SUB
    lo, hi = lo[None, :], hi[None, :]

    b00, a10, a01, small_y, d_as, w_send, u_part = phase(b00, a10, a01, small_y, d_as, w_send, u_part)
    b10, w_other, b01, a11, u_part = px(b00), py(w_send), pc(b00), pc(a10), py(u_part)
    b10, w_other, b01, a11, u_part, w_out1, go_send, go_a, d_part = phase(
        b10, w_other, b01, a11, u_part, w_out, go_send, go_a, d_part
    )
    u_ba = lax.all_gather(u_part, "dp", axis=0, tiled=True)
    b11, w0b, w2a, go_b, d_part = pc(b10), py(w_out1), px(w_out1), py(go_send), py(d_part)
    wt_all, w_all = call(
        unpack_kernel, "unpack", (), (w_own, w_other),
        (shape(6 * PITCH, width), shape(width, 6 * PITCH)), 2,
    )
    h1, qkv, kv, resid = call(
        norm_qkv_kernel, "norm_qkv", (scal,),
        (a00, b00, a01, b01, a10, b10, a11, b11, wt_all, qkv_bias, small, small_y),
        (shape(width, seq), shape(6 * PITCH, seq), shape(seq, 512), shape(width, two)),
        8,
        scratch=[pltpu.VMEM((width, SUB), F32)] * 2 + [pltpu.VMEM((6 * PITCH, SUB), F32)],
    )

    qkv, w2a = phase(qkv, w2a)
    w2b, go_xa = py(w2a), px(after(go_a, w2a))

    o0, o1, lse = call(
        attend_kernel, "attend", (scal, klo, khi), (qkv, kv, lo, hi),
        (shape(2 * n2, two),) * 2 + (shape(2, seq, dtype=F32),), 12,
        scratch=[pltpu.VMEM((2, seq, SUB), F32), pltpu.VMEM((2, PITCH, SUB), F32)],
    )
    o0, o1, w0b, w2b, go_b, go_xa, d_part, u_ba = phase(o0, o1, w0b, w2b, go_b, go_xa, d_part, u_ba)
    d_ba = lax.all_gather(d_part, "dp", axis=0, tiled=True)
    att_y, att_x, att_s = py(o1), px(o0), pc(o0)
    (wo,) = call(out_weights_kernel, "out_weights", (scal,), (w_out, w0b, w2a, w2b), (shape(4 * n2, width),), 1)
    wo_sib = pc(wo)
    up_y = small_y[6, :n_up]
    up_own = jnp.where(ypos == 0, jnp.concatenate((b_up, up_y)), jnp.concatenate((up_y, b_up)))[None, :]
    att_y, att_x, att_s, wo_sib, up_own, u_aa1, go_b1 = phase(att_y, att_x, att_s, wo_sib, up_own, u_aa, go_b)
    att_xy, att_sy, att_sx, up_sib, u_as = px(att_y), pc(att_y), pc(att_x), pc(up_own), pc(u_aa1)
    att_xy, att_sy, att_sx, up_sib, u_as, go_b1, u_ba1 = phase(att_xy, att_sy, att_sx, up_sib, u_as, go_b1, u_ba)
    att_sxy, go_xb = pc(att_xy), px(go_b1)
    mixed, h2t, h2 = call(
        mix_kernel, "mix", (),
        (o0, att_y, att_x, att_xy, att_s, att_sy, att_sx, att_sxy, wo, wo_sib, resid, small, small_y),
        (shape(width, two, dtype=F32), shape(width, two), shape(two, width)), 5,
    )
    u_bs = pc(after(u_ba1, att_sxy))

    held = pltpu.VMEM((width, units), BF)
    four = pltpu.SemaphoreType.DMA((4,))
    u_shape = shape(two, units)
    s_shape = shape(two, units)
    sum_shape = shape(8, units, dtype=F32)
    act0, slope0 = call(
        feed_up_kernel, "feed_up", (), (h2, up_own), (u_shape, s_shape), 3,
        scratch=[held, four], far=(u_aa, u_ba),
    )
    u_bs, go_xb, act0 = phase(u_bs, go_xb, act0)
    act1, slope1 = call(
        feed_up_kernel, "feed_up_sib", (), (h2, up_sib), (u_shape, s_shape), 3,
        scratch=[held, four], far=(u_as, u_bs),
    )
    gof, go = call(
        turn_kernel, "turn", (), (go_a, go_b, go_xa, go_xb), (shape(width, two), shape(two, width)), 2
    )
    d_ba, act1, go = phase(d_ba, act1, go)
    d_bs = pc(d_ba)
    gu0, gu_sums0, gh_part = call(
        feed_own_kernel, "feed_own", (), (go, slope0), (u_shape, sum_shape, shape(width, two, dtype=F32)), 4, vmem=24,
        scratch=[held, held, four], far=(u_aa, u_ba, d_aa, d_ba),
    )
    wide = (units + 127) // 128 * 128
    gu1, gu_sums1, gh_send, gh_own, d_send, u_send = call(
        feed_sib_kernel, "feed_sib", (), (go, slope1, gh_part, act1, h2t, gof),
        (u_shape, sum_shape, shape(width, SUB), shape(width, SUB, dtype=F32), shape(width, wide), shape(width + 16, wide)),
        8, vmem=28, scratch=[held, held, four], far=(u_as, u_bs, d_as, d_bs),
    )
    gh_recv, d_recv, u_recv = px(gh_send), pc(d_send), pc(u_send)
    first = SUB
    rest = half - first
    second = rest + HALF
    keep0, send0, keep_rest, send_rest = call(
        down_own_kernel, "down_own", (), (gof, act0, d_recv),
        (shape(first, wide, dtype=F32), shape(first, wide), shape(rest, wide, dtype=F32), shape(rest, wide)), 2,
    )
    recv0 = py(send0)
    keep1, send1, keep2, send2 = call(
        up_own_kernel, "up_own", (), (h2t, after(gu0, send0), gu_sums0, u_recv, keep_rest, send_rest),
        (
            shape(second, wide, dtype=F32), shape(second, wide),
            shape(half - HALF + 16, wide, dtype=F32), shape(half - HALF + 16, wide),
        ),
        2,
    )
    gh_recv, send1 = phase(gh_recv, send1)
    gm, low, low_b, g_own, g_sib, g_y, g_x, g_xy, sums2_a, sums2_b = call(
        norm2_back_kernel, "norm2_back", (), (gh_own, gh_recv, mixed, go_a, go_b, small, small_y, wo, wo_sib),
        (shape(width, SUB, dtype=F32), shape(width, SUB), shape(half, SUB))
        + (shape(n2, SUB),) * 2
        + (shape(2 * n2, SUB),) * 3
        + (shape(8, half, dtype=F32),) * 2,
        4,
    )

    def total(keep, recv):
        return (keep + recv.astype(F32)).astype(BF)

    g_x, g_xy, g_y = px(g_x), py(g_xy), py(g_y)
    r_send, r_own = call(
        result_kernel, "result", (), (act0, act1, mixed, small, after(small_y, low)),
        (shape(width, SUB), shape(width, SUB, dtype=F32)), 6, vmem=20,
        scratch=[held, held, four], far=(d_aa, d_ba, d_as, d_bs),
    )
    recv0, r_send, send1 = phase(recv0, r_send, send1)
    p0 = total(keep0, recv0)
    p0_in = line(0, p0)
    g_x, g_xy, g_y, g_sib, p0, send1 = phase(g_x, g_xy, g_y, g_sib, p0, send1)
    recv1 = py(send1)
    g_xy, g_sx, g_sy = px(g_xy), pc(g_x), pc(g_y)
    g_xy, g_sx, g_sy, g_sib, wt_all1, recv1, p0_in, low1, r_send, send2 = phase(
        g_xy, g_sx, g_sy, g_sib, wt_all, recv1, p0_in, low, r_send, send2
    )
    g_s, g_sxy, wt_sib = pc(g_sib), pc(g_xy), pc(wt_all1)
    p0, p1 = line_sum(p0, p0_in), total(keep1, recv1)
    heads = phase(qkv, kv, lo, hi, lse, o0, o1, g_own, g_x, g_y, g_xy, g_s, g_sx, g_sy, g_sxy, p0, p1)
    p0, p1 = heads[-2:]
    p0_in, p1_in, recv2, low_x, r_recv = line(1, p0), line(0, p1), py(send2), px(low1), px(r_send)
    dqkv, dqkv_sib = call(
        attend_back_kernel, "attend_back", (scal, qlo, qhi), heads[:-2], (shape(6 * PITCH, 4 * SUB),) * 2, 19,
        scratch=[
            pltpu.VMEM((2 * PITCH, seq), BF), pltpu.VMEM((2, seq), F32), pltpu.VMEM((2 * PITCH, seq), F32),
            pltpu.VMEM((2, seq, PITCH), F32), pltpu.VMEM((2, seq, PITCH), F32),
        ],
    )
    dqkv, dqkv_sib, p0_in, p1_in, recv2, low_x, r_recv = phase(dqkv, dqkv_sib, p0_in, p1_in, recv2, low_x, r_recv)

    from_sib = pc(dqkv_sib)
    p0, p1, p2 = line_sum(p0, p0_in), line_sum(p1, p1_in), total(keep2, recv2)
    p0_in, p1_in, p2_in = line(2, p0), line(1, p1), line(0, p2)
    lanes = (half + 127) // 128 * 128
    q_own, q_send = call(
        qkv_outer_kernel, "qkv_outer", (), (dqkv, dqkv_sib, after(h1, p2)),
        (shape(3 * n2 + 16, lanes), shape(3 * n2, lanes)), 4,
    )
    q_recv = py(q_send)
    to_x, keep = call(
        spread_kernel, "spread", (), (w_all, wt_sib, after(dqkv, q_send), from_sib),
        (shape(width, two), shape(width, two, dtype=F32)), 4,
    )
    keep_o, o_send = call(
        heads_outer_kernel, "heads_outer", (scal,), (o0, att_y, att_s, att_sy, after(low, to_x), low_x),
        (shape(2 * n2, width, dtype=F32), shape(2 * n2, width)), 2,
    )
    o_recv = pc(o_send)
    p0_in, p1_in, p2_in, o_recv, q_recv, to_x = phase(p0_in, p1_in, p2_in, o_recv, q_recv, to_x)
    p1, p2, qa = line_sum(p1, p1_in), line_sum(p2, p2_in), q_own
    p1_in, p2_in, qa_in, from_x = line(2, p1), line(1, p2), line(0, qa), px(to_x)
    o_own, o_send = call(
        heads_sum_kernel, "heads_sum", (), (keep_o, o_recv),
        (shape(2 * n2, lanes, dtype=F32), shape(2 * n2, lanes)), 1,
    )
    o_recv = py(o_send)
    g0 = line_end(p0, p0_in)
    r_a, r_b = call(
        result_sum_kernel, "result_sum", (), (r_own, after(r_recv, o_send)), (shape(half, SUB), shape(half, SUB)), 1
    )
    p1_in, p2_in, qa_in, from_x, o_recv, g0, low_b, r_b = phase(p1_in, p2_in, qa_in, from_x, o_recv, g0, low_b, r_b)
    (qb,) = call(gather_kernel, "gather", (), (q_recv, o_own, o_recv), (shape(5 * n2, lanes),), 1)
    p2, qa = line_sum(p2, p2_in), line_sum(qa, qa_in)
    to_y, own = call(
        spread2_kernel, "spread2", (), (keep, from_x), (shape(half, two), shape(half, two, dtype=F32)), 2,
    )
    p2_in, qa_in, qb_in, from_y, low_y = line(2, p2), line(1, qa), line(0, qb), py(to_y), py(low_b)
    g1 = line_end(p1, p1_in)
    p2_in, qa_in, qb_in, from_y, low_y, g1 = phase(p2_in, qa_in, qb_in, from_y, low_y, g1)
    qa, qb = line_sum(qa, qa_in), line_sum(qb, qb_in)
    grad, normed, stats, sums1 = call(
        norm1_stats_kernel, "norm1_stats", (scal,), (own, from_y, a00, b00, small, sums2_b),
        (shape(half, two, dtype=F32), shape(half, two, dtype=F32), shape(16, lanes, dtype=F32), shape(8, half, dtype=F32)),
        2,
    )
    qa_in, qb_in, stats_y, r_y = line(2, qa), line(1, qb), py(stats), py(r_b)
    g2 = line_end(p2, p2_in)
    stats_y, r_y, g2 = phase(stats_y, r_y, g2)
    sums = jnp.concatenate((sums1[:2], sums2_a[:4] + stats_y[8:12, :half], sums1[6:]), 0)
    sums_c = pc(sums)
    (gin,) = call(
        norm1_back_kernel, "norm1_back", (scal,), (grad, normed, stats, stats_y, gm, low_y), (shape(half, two),), 1,
    )
    sums_c, gin = phase(sums_c, gin)
    sums = sums + sums_c
    sums_x = px(sums)
    (result,) = call(place_kernel, "place", (scal,), (r_a, r_y), (shape(half, two),), 1)
    qa_in, qb_in, sums_x, result = phase(qa_in, qb_in, sums_x, result)
    qb, sums = line_sum(qb, qb_in), sums + sums_x
    qb_in, sums_z = line(2, qb), dp_step(sums, 1)
    ga = line_end(qa, qa_in)
    sums_z, ga = phase(sums_z, ga)
    sums = sums + sums_z
    sums_z = dp_step(sums, 2)
    qb_in, sums_z = phase(qb_in, sums_z)
    sums = dp_last(sums + sums_z)
    dwd, dwu = jnp.concatenate((g0, g1[:rest]), 0), jnp.concatenate((g1[rest:], g2), 0)
    gb = line_end(qb, qb_in)[:, :half]
    dwq_own, dwq_y, dwo = ga[:, :half], gb[: 3 * n2], gb[3 * n2 :]

    bias_q = dwq_own[3 * n2]
    dwq_own = dwq_own[: 3 * n2]
    first = jnp.where(ypos == 0, dwq_own, dwq_y).reshape(3, n2, half)
    second = jnp.where(ypos == 0, dwq_y, dwq_own).reshape(3, n2, half)
    dwq = jnp.concatenate((first, second), 1)
    gbu = lax.dynamic_slice_in_dim(dwu[half], ypos * n_up, n_up, 0)
    return (
        result.T, gin.T, sums[0], sums[1], dwq[0].T, bias_q[:n2], dwq[1].T, dwq[2].T, bias_q[n2 : 2 * n2],
        dwo, sums[4], sums[2], sums[3], dwu[:half, :units], gbu, dwd[:, :units].T, sums[5],
    )


def solution(mesh):
    rows = P(("dp", "tr"), "tc")
    placed = (
        rows, P("dp"), P("dp"), P("tc"), P("tc"), P("tc", "tr"), P(("tr", "tc")), P("tc", "tr"),
        P("tc", "tr"), P(("tr", "tc")), P("tr", "tc"), P("tc"), P("tc"), P("tc"), P("tc", "tr"),
        P(("tr", "tc")), P("tr", "tc"), P("tc"), rows,
    )
    outs = (
        rows, rows, P("tc"), P("tc"), P("tc", "tr"), P(("tr", "tc")), P("tc", "tr"), P("tc", "tr"),
        P(("tr", "tc")), P("tr", "tc"), P("tc"), P("tc"), P("tc"), P("tc", "tr"), P(("tr", "tc")),
        P("tr", "tc"), P("tc"),
    )
    return jax.shard_map(local, mesh=mesh, in_specs=placed, out_specs=outs, check_vma=False)
```

```python
import jax
import jax.numpy as jnp
from jax import lax
from jax.experimental import pallas as pl
from jax.experimental.pallas import tpu as pltpu
from jax.sharding import PartitionSpec as P

DH = 72
PITCH = 80
SUB = 256
HALF = SUB // 2
EPSILON = 1e-06
GELU_C = 0.7978845608028654
GELU_A = 0.044715
MASKED = -1e30
SCALE = DH**-0.5
SCALE2 = SCALE * 1.4426950408889634
BF = jnp.bfloat16
F32 = jnp.float32
MIB = 1024 * 1024


def swap_perm(axis, bit):
    return [(i, i ^ bit) for i in range(lax.axis_size(axis))]


def px(v):
    return lax.ppermute(v, "tr", swap_perm("tr", 2))


def pc(v):
    return lax.ppermute(v, "tr", swap_perm("tr", 1))


def py(v):
    return lax.ppermute(v, "tc", swap_perm("tc", 1))


def phase(*values):
    return lax.optimization_barrier(values)


def after(v, *earlier):
    return phase(v, *earlier)[0]


def dot(a, b):
    return jnp.dot(a, b, preferred_element_type=F32)


def dot_tn(a, b):
    return lax.dot_general(a, b, (((0,), (0,)), ((), ())), preferred_element_type=F32)


def dot_nt(a, b):
    return lax.dot_general(a, b, (((1,), (1,)), ((), ())), preferred_element_type=F32)


def rows_at(v, first, count):
    return lax.dynamic_slice_in_dim(v, first, count, 0)


def cols_at(v, first, count):
    return lax.dynamic_slice_in_dim(v, first, count, 1)


def dp_swap(v, bit):
    return lax.ppermute(v, "dp", swap_perm("dp", bit))


def line(step, v):
    if lax.axis_size("dp") != 4:
        return v
    return lax.ppermute(v, "dp", ([(0, 1), (3, 2)], [(1, 2), (2, 1)], [(1, 0), (2, 3)])[step])


def line_sum(v, received):
    if lax.axis_size("dp") != 4:
        return v
    return (v.astype(F32) + received.astype(F32)).astype(BF)


def line_end(v, received):
    if lax.axis_size("dp") != 4:
        return lax.psum(v, "dp").astype(F32)
    place = lax.axis_index("dp")
    return jnp.where((place == 1) | (place == 2), v, received).astype(F32)


def dp_step(v, bit):
    return dp_swap(v, bit) if lax.axis_size("dp") == 4 else jnp.zeros_like(v)


def dp_last(v):
    return v if lax.axis_size("dp") == 4 else lax.psum(v, "dp")


VM = pl.BlockSpec(memory_space=pltpu.VMEM)
SM = pl.BlockSpec(memory_space=pltpu.SMEM)


def shape(*dims, dtype=BF):
    return jax.ShapeDtypeStruct(dims, dtype)


ANY = pl.BlockSpec(memory_space=pl.ANY)


def call(body, name, scalars, arrays, outs, us, scratch=(), vmem=12, far=()):
    return pl.pallas_call(
        body,
        out_shape=tuple(outs),
        in_specs=[SM] * len(scalars) + [VM] * len(arrays) + [ANY] * len(far),
        out_specs=tuple([VM] * len(outs)),
        scratch_shapes=list(scratch),
        compiler_params=pltpu.CompilerParams(vmem_limit_bytes=vmem * MIB),
        cost_estimate=pl.CostEstimate(
            flops=int(us * 600e6), bytes_accessed=int(us * 3e6), transcendentals=0
        ),
        name=name,
    )(*scalars, *arrays, *far)


def spots():
    return [(rc, ry, rx) for rc in range(2) for ry in range(2) for rx in range(2)]


def block_of(me, rc, ry, rx):
    return me ^ (rx * 4 + rc * 2 + ry)


def span(block):
    return pl.ds(pl.multiple_of(block * SUB, SUB), SUB)


def head_rows(pos):
    return pl.ds(pl.multiple_of(pos * 2 * DH, 16), 2 * DH)


def row_of(col):
    return jnp.broadcast_to(col, (col.shape[0], 128)).T[0:1]


def column(i, *parts):
    return jnp.concatenate([p[...].T[:, i : i + 1] for p in parts], 0)


def pack_kernel(scal, q, k, v, own, send):
    for i, w in enumerate((q, k, v)):
        there = slice(2 * DH * i, 2 * DH * (i + 1))
        own[there, :] = w[head_rows(scal[0]), :]
        send[there, :] = w[head_rows(1 - scal[0]), :]


def unpack_kernel(own, other, wt, w):
    both = jnp.concatenate((own[...].astype(F32), other[...].astype(F32)), 1)
    gap = jnp.zeros((PITCH - DH, both.shape[1]), F32)
    parts = []
    for i in range(6):
        parts += [both[DH * i : DH * (i + 1)], gap]
    whole = jnp.concatenate(parts, 0).astype(BF)
    wt[...] = whole
    w[...] = whole.T


def norm_qkv_kernel(
    scal, a00, b00, a01, b01, a10, b10, a11, b11, weights, bias, small, small_y,
    h_ref, qkv_ref, kv_ref, res_ref, gain_s, shift_s, bias_s,
):
    ypos, me = scal[0], scal[1]
    half = a00.shape[0]
    gain_s[...] = jnp.broadcast_to(column(0, small, small_y), gain_s.shape)
    shift_s[...] = jnp.broadcast_to(column(1, small, small_y), shift_s.shape)
    bias_s[...] = jnp.broadcast_to(column(0, bias), bias_s.shape)
    sources = {(0, 0): (a00, b00), (1, 0): (a01, b01), (0, 1): (a10, b10), (1, 1): (a11, b11)}
    for p, (rc, ry, rx) in enumerate(spots()):
        here = slice(p * SUB, (p + 1) * SUB)
        there = span(block_of(me, rc, ry, rx))
        cols = span(ypos ^ ry)
        sa, sb = sources[(rc, rx)]
        raw = jnp.concatenate((sa[:, cols], sb[:, cols]), 0)
        if rc == 0 and ry == 0:
            res_ref[:, rx * SUB : (rx + 1) * SUB] = raw
        v = raw.astype(F32)
        mean = jnp.sum(v, axis=0, keepdims=True) / (2 * half)
        square = jnp.sum(v * v, axis=0, keepdims=True) / (2 * half)
        root = lax.rsqrt(square - mean * mean + EPSILON)
        hidden = ((v - mean) * root * gain_s[...] + shift_s[...]).astype(BF)
        h_ref[:, here] = hidden
        qkv = (dot(weights[...], hidden) + bias_s[...]).astype(BF)
        qkv_ref[:, there] = qkv
        for i in range(4):
            kv_ref[there, 128 * i : 128 * i + PITCH] = qkv[PITCH * (2 + i) : PITCH * (3 + i), :].T


def attend_kernel(scal, klo, khi, qkv, kv, lo, hi, o0, o1, lse, s_ref, acc_ref):
    me = scal[1]
    outs = (o0, o1)
    places = lax.broadcasted_iota(jnp.int32, (SUB, SUB), 0)
    lanes = lax.broadcasted_iota(jnp.int32, (1, SUB), 1)
    for rc, ry, rx in sorted(spots(), reverse=True):
        block = block_of(me, rc, ry, rx)
        cols = span(block)
        low, high = lo[:, cols], hi[:, cols]
        own = lanes + block * SUB

        def score(kb, tops):
            base = kb * SUB
            allowed = ((places >= low - base) & (places < high - base)) | (places == own - base)
            new = []
            for h in range(2):
                s = dot(kv[span(kb), 128 * h : 128 * h + PITCH], qkv[PITCH * h : PITCH * (h + 1), cols])
                s = jnp.where(allowed, s, MASKED)
                s_ref[h, span(kb), :] = s
                new.append(jnp.maximum(tops[h], jnp.max(s.reshape(SUB // 8, 8, SUB), axis=0)))
            return tuple(new)

        start = jnp.full((8, SUB), MASKED, F32)
        tops = lax.fori_loop(klo[block], khi[block], score, (start, start))
        tops = [jnp.max(t, axis=0, keepdims=True) * SCALE2 for t in tops]
        acc_ref[...] = jnp.zeros_like(acc_ref)

        def weigh(kb, carry):
            for h in range(2):
                weights = jnp.exp2(s_ref[h, span(kb), :] * SCALE2 - tops[h]).astype(BF)
                acc_ref[h] += dot(qkv[PITCH * (4 + h) : PITCH * (5 + h), span(kb)], weights)
            return carry

        lax.fori_loop(klo[block], khi[block], weigh, 0)
        heads = []
        for h in range(2):
            total = acc_ref[h, DH : DH + 1, :]
            heads.append(acc_ref[h, :DH, :] / total)
            lse[h : h + 1, cols] = tops[h] + jnp.log2(total)
        rows = slice(rc * 2 * DH, (rc + 1) * 2 * DH)
        outs[ry][rows, rx * SUB : (rx + 1) * SUB] = jnp.concatenate(heads, 0).astype(BF)


def attend_back_kernel(
    scal, qlo, qhi, qkv, kv, lo, hi, lse, o0, o1, g0, gx, gy, gxy, s0, sx, sy, sxy,
    out0, out1, gt, delta, dqt, dk, dv,
):
    me = scal[1]
    outs = (o0, o1)
    n2 = 2 * DH
    grads = (g0, gx, gy, gxy, s0, sx, sy, sxy)
    for p, (rc, ry, rx) in enumerate(spots()):
        cols = span(block_of(me, rc, ry, rx))
        rows = slice(rc * n2, (rc + 1) * n2)
        gtile = (grads[p][...] if p in (0, 4) else grads[p][rows, :]).astype(F32)
        both = gtile * outs[ry][rows, rx * SUB : (rx + 1) * SUB].astype(F32)
        for h in range(2):
            part = slice(DH * h, DH * (h + 1))
            padded = jnp.concatenate((gtile[part], jnp.zeros((PITCH - DH, SUB), F32)), 0)
            gt[PITCH * h : PITCH * (h + 1), cols] = padded.astype(BF)
            delta[h : h + 1, cols] = jnp.sum(both[part], axis=0, keepdims=True)
    dqt[...] = jnp.zeros_like(dqt)
    dk[...] = jnp.zeros_like(dk)
    dv[...] = jnp.zeros_like(dv)
    places = lax.broadcasted_iota(jnp.int32, (SUB, SUB), 0)
    lanes = lax.broadcasted_iota(jnp.int32, (1, SUB), 1)

    @pl.loop(0, 8)
    def _(kb):
        keys = span(kb)
        base = kb * SUB

        def body(qb, carry):
            cols = span(qb)
            low, high = lo[:, cols] - base, hi[:, cols] - base
            own = lanes + (qb * SUB - base)
            allowed = ((places >= low) & (places < high)) | (places == own)
            for h in range(2):
                head = slice(PITCH * h, PITCH * (h + 1))
                s = dot(kv[keys, 128 * h : 128 * h + PITCH], qkv[head, cols])
                probs = jnp.where(allowed, jnp.exp2(s * SCALE2 - lse[h : h + 1, cols]), 0.0)
                gprobs = dot(kv[keys, 256 + 128 * h : 256 + 128 * h + PITCH], gt[head, cols])
                gscores = (probs * (gprobs - delta[h : h + 1, cols])).astype(BF)
                dv[h, keys, :] += dot_nt(probs.astype(BF), gt[head, cols])
                dk[h, keys, :] += dot_nt(gscores, qkv[head, cols])
                dqt[head, cols] += dot(qkv[PITCH * (2 + h) : PITCH * (3 + h), keys], gscores)
            return carry

        lax.fori_loop(qlo[kb], qhi[kb], body, 0)

    for p, (rc, ry, rx) in enumerate(spots()):
        out = (out0, out1)[rc]
        here = slice((ry * 2 + rx) * SUB, (ry * 2 + rx + 1) * SUB)
        rows = span(block_of(me, rc, ry, rx))
        out[: 2 * PITCH, here] = (dqt[:, rows] * SCALE).astype(BF)
        for h in range(2):
            out[PITCH * (2 + h) : PITCH * (3 + h), here] = (dk[h, rows, :].T * SCALE).astype(BF)
            out[PITCH * (4 + h) : PITCH * (5 + h), here] = dv[h, rows, :].T.astype(BF)


def own_and_y(ypos, w):
    return [w[head_rows(ypos), :], w[head_rows(1 - ypos), :]]


def out_weights_kernel(scal, own_a, own_b, x_a, x_b, w):
    parts = []
    for a, b in ((own_a, own_b), (x_a, x_b)):
        for wa, wb in zip(own_and_y(scal[0], a), own_and_y(scal[0], b)):
            parts.append(jnp.concatenate((wa, wb), 1))
    w[...] = jnp.concatenate(parts, 0)


def mix_kernel(own, y, x, xy, sib, ysib, xsib, xysib, w, w_sib, res, small, small_y, mixed, h2t, h2):
    n2 = 2 * DH
    gain, shift, bias = [column(i, small, small_y) for i in (2, 3, 4)]
    parts = []
    for rows, group in ((slice(0, n2), (own, y, x, xy)), (slice(n2, 2 * n2), (sib, ysib, xsib, xysib))):
        for i, o in enumerate(group):
            if i < 2:
                parts.append(o[rows, :])
            else:
                parts.append(jnp.concatenate((o[rows, SUB:], o[rows, :SUB]), 1))
    att = jnp.concatenate(parts, 0)
    weights = jnp.concatenate((w[...], w_sib[...]), 0)
    v = res[...].astype(F32) + dot_tn(weights, att) + bias
    mixed[...] = v
    mean = jnp.mean(v, axis=0, keepdims=True)
    root = lax.rsqrt(jnp.mean(v * v, axis=0, keepdims=True) - mean * mean + EPSILON)
    hidden = ((v - mean) * root * gain + shift).astype(BF)
    h2t[...] = hidden
    h2[...] = hidden.T


def turn_kernel(oa, ob, xa, xb, gof, go):
    half = oa.shape[0]
    for rx, (a, b) in enumerate(((oa, ob), (xa, xb))):
        here = slice(rx * SUB, (rx + 1) * SUB)
        gof[:half, here] = a[...]
        gof[half:, here] = b[...]
        go[here, :] = jnp.concatenate((a[...], b[...]), 0).T


def gelu_both(u):
    square = u * u
    tangent = jnp.tanh(GELU_C * (u + GELU_A * square * u))
    plus = 0.5 * (1.0 + tangent)
    slope = plus + 0.5 * u * (1.0 - tangent * tangent) * GELU_C * (1.0 + 3.0 * GELU_A * square)
    return u * plus, slope


def fetch(sources, buffers, sems):
    half = sources[0].shape[0]
    copies = []
    for i, src in enumerate(sources):
        dst = buffers[i // 2].at[pl.ds((i % 2) * half, half), :]
        copies.append(pltpu.make_async_copy(src, dst, sems.at[i]))
        copies[-1].start()
    return copies


def feed_up_kernel(h2, bias, ua, ub, act, slope, u, sems):
    copies = fetch((ua, ub), (u,), sems)
    for c in copies:
        c.wait()
    value, sl = gelu_both(dot(h2[...], u[...]) + bias[...])
    act[...] = value.astype(BF)
    slope[...] = sl.astype(BF)


def feed_grad(go, slope, u, d, copies, gu, sums):
    for c in copies[:2]:
        c.wait()
    rounded = (dot(go[...], d[...]) * slope[...].astype(F32)).astype(BF)
    gu[...] = rounded
    sums[...] = jnp.broadcast_to(jnp.sum(rounded.astype(F32), axis=0, keepdims=True), sums.shape)
    for c in copies[2:]:
        c.wait()
    return dot_nt(u[...], gu[...])


def feed_own_kernel(go, slope, ua, ub, da, db, gu, sums, part, u, d, sems):
    part[...] = feed_grad(go, slope, u, d, fetch((da, db, ua, ub), (d, u), sems), gu, sums)


def feed_sib_kernel(go, slope, part, act, h2t, gof, ua, ub, da, db, gu, sums, send, own, down, up, u, d, sems):
    copies = fetch((da, db, ua, ub), (d, u), sems)
    width, rows = down.shape[1], h2t.shape[0]
    down[...] = padded_units(dot(gof[...], act[...]).astype(BF), width)
    total = feed_grad(go, slope, u, d, copies, gu, sums) + part[...]
    send[...] = total[:, SUB:].astype(BF)
    own[...] = total[:, :SUB]
    up[:rows, :] = padded_units(dot(h2t[...], gu[...]).astype(BF), width)
    up[rows:, :] = padded_units(jnp.concatenate((sums[...], sums[...]), 0).astype(BF), width)


def padded_units(v, width):
    return jnp.concatenate((v, jnp.zeros((v.shape[0], width - v.shape[1]), v.dtype)), 1)


def down_own_kernel(gof, act, recv, keep0, send0, keep_rest, send_rest):
    half, width = recv.shape[0] // 2, recv.shape[1]
    total = padded_units(dot(gof[...], act[...]), width) + recv[...].astype(F32)
    rows = keep0.shape[0]
    keep0[...] = total[:rows]
    keep_rest[...] = total[rows:half]
    send0[...] = total[half : half + rows].astype(BF)
    send_rest[...] = total[half + rows :].astype(BF)


def up_own_kernel(h2t, gu, sums, recv, keep_rest, send_rest, keep1, send1, keep2, send2):
    half = h2t.shape[0] // 2
    width = recv.shape[1]
    total = padded_units(dot(h2t[...], gu[...]), width) + recv[: 2 * half, :].astype(F32)
    more = padded_units(jnp.concatenate((sums[...], sums[...]), 0), width) + recv[2 * half :, :].astype(F32)
    rest = keep_rest.shape[0]
    rows = keep1.shape[0] - rest
    keep1[:rest, :] = keep_rest[...]
    send1[:rest, :] = send_rest[...]
    keep1[rest:, :] = total[:rows]
    send1[rest:, :] = total[half : half + rows].astype(BF)
    keep2[: half - rows, :] = total[rows:half]
    keep2[half - rows :, :] = more
    send2[: half - rows, :] = total[half + rows :].astype(BF)
    send2[half - rows :, :] = more.astype(BF)


def result_kernel(act0, act1, mixed, small, small_y, daa, dba, das, dbs, send, own, d0, d1, sems):
    copies = fetch((daa, dba, das, dbs), (d0, d1), sems)
    for c in copies:
        c.wait()
    part = dot_nt(d0[...], act0[...]) + dot_nt(d1[...], act1[...])
    send[...] = part[:, SUB:].astype(BF)
    own[...] = part[:, :SUB] + mixed[:, :SUB] + column(5, small, small_y)


def result_sum_kernel(own, recv, out_a, out_b):
    half = out_a.shape[0]
    total = (own[...] + recv[: own.shape[0], :].astype(F32)).astype(BF)
    out_a[...] = total[:half]
    out_b[...] = total[half:]


def place_kernel(scal, own, other, out):
    out[:, span(scal[0])] = own[...]
    out[:, span(1 - scal[0])] = other[...]


def norm2_back_kernel(
    own, recv, mixed, goa, gob, small, small_y, w, w_sib, gm, low, low_b, g_own, g_sib, g_y, g_x, g_xy, sums_a, sums_b
):
    e = own[...] + recv[...].astype(F32)
    v = mixed[:, :SUB]
    mean = jnp.mean(v, axis=0, keepdims=True)
    root = lax.rsqrt(jnp.mean(v * v, axis=0, keepdims=True) - mean * mean + EPSILON)
    n = (v - mean) * root
    weighted = e * column(2, small, small_y)
    go = jnp.concatenate((goa[...], gob[...]), 0).astype(F32)
    grad = go + root * (
        weighted
        - jnp.mean(weighted, axis=0, keepdims=True)
        - n * jnp.mean(weighted * n, axis=0, keepdims=True)
    )
    gm[...] = grad
    rounded = grad.astype(BF)
    low[...] = rounded
    low_b[...] = rounded[low_b.shape[0] :]
    n2 = 2 * DH
    mine = dot(w[...], rounded).astype(BF)
    sibs = dot(w_sib[...], rounded).astype(BF)
    g_own[...] = mine[:n2]
    g_sib[...] = sibs[:n2]
    for i, out in enumerate((g_y, g_x, g_xy)):
        rows = slice(n2 * (i + 1), n2 * (i + 2))
        out[:n2, :] = mine[rows]
        out[n2:, :] = sibs[rows]
    for i, q in enumerate((e * n, e, grad, go)):
        col = jnp.sum(q, axis=1, keepdims=True)
        half = low_b.shape[0]
        sums_a[i : i + 1, :] = row_of(col[:half])
        sums_b[i : i + 1, :] = row_of(col[half:])
    sums_a[4:, :] = jnp.zeros_like(sums_a[4:, :])
    sums_b[4:, :] = jnp.zeros_like(sums_b[4:, :])


def heads_outer_kernel(scal, own, y, sib, ysib, low, low_x, keep, send):
    right = jnp.concatenate((low[...], low_x[...]), 1)
    n2 = 2 * DH
    for rows, a, b, out in ((slice(0, n2), own, y, keep), (slice(n2, 2 * n2), sib, ysib, send)):
        out[head_rows(scal[0]), :] = dot_nt(a[rows, :], right).astype(out.dtype)
        out[head_rows(1 - scal[0]), :] = dot_nt(b[rows, :], right).astype(out.dtype)


def gather_kernel(q_own, o_own, o_recv, out):
    n = q_own.shape[0]
    out[:n, :] = q_own[...]
    out[n:, :] = (o_own[...] + o_recv[...].astype(F32)).astype(BF)


def qkv_outer_kernel(dqkv, dqkv_sib, h1, own, send):
    mid = dqkv.shape[1]
    total = dot_nt(dqkv[...], h1[:, :mid]) + dot_nt(dqkv_sib[...], h1[:, mid:])
    half = h1.shape[0] // 2
    lanes = own.shape[1]
    rows = jnp.concatenate([total[PITCH * i : PITCH * i + DH] for i in range(6)], 0)
    n = 6 * DH
    own[:n, :] = padded_units(rows[:, :half].astype(BF), lanes)
    send[...] = padded_units(rows[:, half:].astype(BF), lanes)
    col = jnp.sum(dqkv[...].astype(F32) + dqkv_sib[...].astype(F32), axis=1, keepdims=True)
    cols = [col[PITCH * i : PITCH * i + DH] for i in (0, 1, 4, 5)]
    cols.append(jnp.zeros((lanes - 4 * DH, 1), F32))
    own[n:, :] = jnp.broadcast_to(row_of(jnp.concatenate(cols, 0)), (16, lanes)).astype(BF)


def heads_sum_kernel(keep, recv, own, send):
    half = keep.shape[1] // 2
    total = keep[...] + recv[...].astype(F32)
    own[...] = padded_units(total[:, :half], own.shape[1])
    send[...] = padded_units(total[:, half:].astype(BF), send.shape[1])


def spread_kernel(w, wt_sib, dqkv, from_sib, to_x, keep):
    total = dot(w[...], dqkv[...]) + dot_tn(wt_sib[...], from_sib[...])
    for ry in range(2):
        first = 2 * ry * SUB
        at = slice(ry * SUB, (ry + 1) * SUB)
        keep[:, at] = total[:, first : first + SUB]
        to_x[:, at] = total[:, first + SUB : first + 2 * SUB].astype(BF)


def spread2_kernel(keep, from_x, to_y, own):
    half = own.shape[0]
    total = keep[...] + from_x[...].astype(F32)
    own[...] = total[:half]
    to_y[...] = total[half:].astype(BF)


def norm1_stats_kernel(scal, own, from_y, a, b, small, sums_b, grad, normed, stats, sums):
    ypos = scal[0]
    half = a.shape[0]
    gain = column(0, small)
    cols_sums = [0.0, 0.0]
    stats[...] = jnp.zeros_like(stats)
    for ry in range(2):
        cols = span(ypos ^ ry)
        here = slice(ry * SUB, (ry + 1) * SUB)
        e = own[:, here] + from_y[:, (1 - ry) * SUB : (2 - ry) * SUB].astype(F32)
        va, vb = a[:, cols].astype(F32), b[:, cols].astype(F32)
        mean = (jnp.sum(va, 0, keepdims=True) + jnp.sum(vb, 0, keepdims=True)) / (2 * half)
        square = (jnp.sum(va * va, 0, keepdims=True) + jnp.sum(vb * vb, 0, keepdims=True)) / (2 * half)
        root = lax.rsqrt(square - mean * mean + EPSILON)
        n = (va - mean) * root
        w = e * gain
        grad[:, here] = w
        normed[:, here] = n
        stats[0:1, here] = jnp.sum(w, 0, keepdims=True)
        stats[1:2, here] = jnp.sum(w * n, 0, keepdims=True)
        stats[2:3, here] = root
        cols_sums[0] += jnp.sum(e * n, 1, keepdims=True)
        cols_sums[1] += jnp.sum(e, 1, keepdims=True)
    stats[8:, :half] = sums_b[...]
    for i in range(2):
        sums[i : i + 1, :] = row_of(cols_sums[i])
    sums[2:, :] = jnp.zeros_like(sums[2:, :])


def norm1_back_kernel(scal, grad, normed, stats, recv, gm_own, gm_y, out):
    ypos = scal[0]
    width = 2 * grad.shape[0]
    for ry in range(2):
        here = slice(ry * SUB, (ry + 1) * SUB)
        other = slice((1 - ry) * SUB, (2 - ry) * SUB)
        total = (stats[0:1, here] + recv[0:1, other]) / width
        along = (stats[1:2, here] + recv[1:2, other]) / width
        gm = gm_own[: grad.shape[0], :] if ry == 0 else gm_y[...].astype(F32)
        whole = gm + stats[2:3, here] * (grad[:, here] - total - normed[:, here] * along)
        out[:, span(ypos ^ ry)] = whole.astype(BF)


def local(
    layer_input, picture, token_kept, ln1_gain, ln1_bias, w_query, b_query, w_key, w_value, b_value,
    w_out, b_out, ln2_gain, ln2_bias, w_up, b_up, w_down, b_down, grad_out,
):
    ypos = lax.axis_index("tc").astype(jnp.int32)
    trpos = lax.axis_index("tr").astype(jnp.int32)
    me = trpos * 2 + ypos
    half = layer_input.shape[1]
    width = 2 * half
    seq = picture.shape[0]
    n2 = b_query.shape[0]
    units = w_up.shape[1]
    n_up = b_up.shape[0]
    scal = jnp.stack((ypos, me))
    two = 2 * SUB

    a00 = layer_input.T
    qkv_weights = (w_query.T, w_key.T, w_value.T)
    go_t = grad_out.T
    u_aa, d_aa = w_up, w_down.T
    small = jnp.stack(
        (ln1_gain, ln1_bias, ln2_gain, ln2_bias, b_out, b_down, jnp.pad(b_up, (0, half - n_up)), ln1_gain)
    )
    w_own, w_send = call(pack_kernel, "pack", (scal,), qkv_weights, (shape(3 * n2, half),) * 2, 1)
    b00, a10, a01, small_y, d_as = py(a00), px(a00), pc(a00), py(small), pc(d_aa)
    go_a = cols_at(go_t, ypos * SUB, SUB)
    go_send = cols_at(go_t, (1 - ypos) * SUB, SUB)
    quarter = half // lax.axis_size("dp")
    first = lax.axis_index("dp") * quarter
    u_part, d_part = rows_at(u_aa, first, quarter), rows_at(d_aa, first, quarter)
    qkv_bias = jnp.concatenate((b_query, jnp.zeros_like(b_query), b_value)).reshape(6, DH)
    ones = (jnp.arange(6) >= 4).astype(F32)[:, None]
    qkv_bias = jnp.concatenate((qkv_bias, ones, jnp.zeros((6, PITCH - DH - 1), F32)), 1).reshape(1, -1)
    qkv_bias = jnp.broadcast_to(qkv_bias, (8, 6 * PITCH))

    numbers = jnp.arange(8, dtype=jnp.int32)[:, None]
    hot = (picture[None, :] == numbers).astype(jnp.int32)
    counts = jnp.sum(hot, axis=1)
    kept = jnp.sum(hot * token_kept[None, :], axis=1)
    starts = jnp.cumsum(counts) - counts
    lo = jnp.sum(hot * starts[:, None], axis=0)
    hi = jnp.sum(hot * (starts + kept)[:, None], axis=0)
    end = jnp.sum(hot * (starts + counts)[:, None], axis=0)
    blocks = seq // SUB
    klo = qlo = lo.reshape(blocks, SUB)[:, 0] // SUB
    lasts = jnp.arange(1, blocks + 1, dtype=jnp.int32) * SUB
    khi = (jnp.maximum(lasts, hi.reshape(blocks, SUB)[:, -1]) + SUB - 1) // SUB
    qhi = (jnp.maximum(lasts, end.reshape(blocks, SUB)[:, -1]) + SUB - 1) // SUB
    lo, hi = lo[None, :], hi[None, :]

    b00, a10, a01, small_y, d_as, w_send, u_part = phase(b00, a10, a01, small_y, d_as, w_send, u_part)
    b10, w_other, b01, a11, u_part = px(b00), py(w_send), pc(b00), pc(a10), py(u_part)
    b10, w_other, b01, a11, u_part, w_out1, go_send, go_a, d_part = phase(
        b10, w_other, b01, a11, u_part, w_out, go_send, go_a, d_part
    )
    u_ba = lax.all_gather(u_part, "dp", axis=0, tiled=True)
    b11, w0b, w2a, go_b, d_part = pc(b10), py(w_out1), px(w_out1), py(go_send), py(d_part)
    wt_all, w_all = call(
        unpack_kernel, "unpack", (), (w_own, w_other),
        (shape(6 * PITCH, width), shape(width, 6 * PITCH)), 2,
    )
    h1, qkv, kv, resid = call(
        norm_qkv_kernel, "norm_qkv", (scal,),
        (a00, b00, a01, b01, a10, b10, a11, b11, wt_all, qkv_bias, small, small_y),
        (shape(width, seq), shape(6 * PITCH, seq), shape(seq, 512), shape(width, two)),
        8,
        scratch=[pltpu.VMEM((width, SUB), F32)] * 2 + [pltpu.VMEM((6 * PITCH, SUB), F32)],
    )

    qkv, w2a = phase(qkv, w2a)
    w2b, go_xa = py(w2a), px(after(go_a, w2a))

    o0, o1, lse = call(
        attend_kernel, "attend", (scal, klo, khi), (qkv, kv, lo, hi),
        (shape(2 * n2, two),) * 2 + (shape(2, seq, dtype=F32),), 12,
        scratch=[pltpu.VMEM((2, seq, SUB), F32), pltpu.VMEM((2, PITCH, SUB), F32)],
    )
    o0, o1, w0b, w2b, go_b, go_xa, d_part, u_ba = phase(o0, o1, w0b, w2b, go_b, go_xa, d_part, u_ba)
    d_ba = lax.all_gather(d_part, "dp", axis=0, tiled=True)
    att_y, att_x, att_s = py(o1), px(o0), pc(o0)
    (wo,) = call(out_weights_kernel, "out_weights", (scal,), (w_out, w0b, w2a, w2b), (shape(4 * n2, width),), 1)
    wo_sib = pc(wo)
    up_y = small_y[6, :n_up]
    up_own = jnp.where(ypos == 0, jnp.concatenate((b_up, up_y)), jnp.concatenate((up_y, b_up)))[None, :]
    att_y, att_x, att_s, wo_sib, up_own, u_aa1, go_b1 = phase(att_y, att_x, att_s, wo_sib, up_own, u_aa, go_b)
    att_xy, att_sy, att_sx, up_sib, u_as = px(att_y), pc(att_y), pc(att_x), pc(up_own), pc(u_aa1)
    att_xy, att_sy, att_sx, up_sib, u_as, go_b1, u_ba1 = phase(att_xy, att_sy, att_sx, up_sib, u_as, go_b1, u_ba)
    att_sxy, go_xb = pc(att_xy), px(go_b1)
    mixed, h2t, h2 = call(
        mix_kernel, "mix", (),
        (o0, att_y, att_x, att_xy, att_s, att_sy, att_sx, att_sxy, wo, wo_sib, resid, small, small_y),
        (shape(width, two, dtype=F32), shape(width, two), shape(two, width)), 5,
    )
    u_bs = pc(after(u_ba1, att_sxy))

    held = pltpu.VMEM((width, units), BF)
    four = pltpu.SemaphoreType.DMA((4,))
    u_shape = shape(two, units)
    s_shape = shape(two, units)
    sum_shape = shape(8, units, dtype=F32)
    act0, slope0 = call(
        feed_up_kernel, "feed_up", (), (h2, up_own), (u_shape, s_shape), 3,
        scratch=[held, four], far=(u_aa, u_ba),
    )
    u_bs, go_xb, act0 = phase(u_bs, go_xb, act0)
    act1, slope1 = call(
        feed_up_kernel, "feed_up_sib", (), (h2, up_sib), (u_shape, s_shape), 3,
        scratch=[held, four], far=(u_as, u_bs),
    )
    gof, go = call(
        turn_kernel, "turn", (), (go_a, go_b, go_xa, go_xb), (shape(width, two), shape(two, width)), 2
    )
    d_ba, act1, go = phase(d_ba, act1, go)
    d_bs = pc(d_ba)
    gu0, gu_sums0, gh_part = call(
        feed_own_kernel, "feed_own", (), (go, slope0), (u_shape, sum_shape, shape(width, two, dtype=F32)), 4, vmem=16,
        scratch=[held, held, four], far=(u_aa, u_ba, d_aa, d_ba),
    )
    wide = (units + 127) // 128 * 128
    gu1, gu_sums1, gh_send, gh_own, d_send, u_send = call(
        feed_sib_kernel, "feed_sib", (), (go, slope1, gh_part, act1, h2t, gof),
        (u_shape, sum_shape, shape(width, SUB), shape(width, SUB, dtype=F32), shape(width, wide), shape(width + 16, wide)),
        8, vmem=14, scratch=[held, held, four], far=(u_as, u_bs, d_as, d_bs),
    )
    gh_recv, d_recv, u_recv = px(gh_send), pc(d_send), pc(u_send)
    first = SUB
    rest = half - first
    second = rest + HALF
    keep0, send0, keep_rest, send_rest = call(
        down_own_kernel, "down_own", (), (gof, act0, d_recv),
        (shape(first, wide, dtype=F32), shape(first, wide), shape(rest, wide, dtype=F32), shape(rest, wide)), 2,
    )
    recv0 = py(send0)
    keep1, send1, keep2, send2 = call(
        up_own_kernel, "up_own", (), (h2t, after(gu0, send0), gu_sums0, u_recv, keep_rest, send_rest),
        (
            shape(second, wide, dtype=F32), shape(second, wide),
            shape(half - HALF + 16, wide, dtype=F32), shape(half - HALF + 16, wide),
        ),
        2,
    )
    gh_recv, send1 = phase(gh_recv, send1)
    gm, low, low_b, g_own, g_sib, g_y, g_x, g_xy, sums2_a, sums2_b = call(
        norm2_back_kernel, "norm2_back", (), (gh_own, gh_recv, mixed, go_a, go_b, small, small_y, wo, wo_sib),
        (shape(width, SUB, dtype=F32), shape(width, SUB), shape(half, SUB))
        + (shape(n2, SUB),) * 2
        + (shape(2 * n2, SUB),) * 3
        + (shape(8, half, dtype=F32),) * 2,
        4,
    )

    def total(keep, recv):
        return (keep + recv.astype(F32)).astype(BF)

    g_x, g_xy, g_y = px(g_x), py(g_xy), py(g_y)
    r_send, r_own = call(
        result_kernel, "result", (), (act0, act1, mixed, small, after(small_y, low)),
        (shape(width, SUB), shape(width, SUB, dtype=F32)), 6, vmem=14,
        scratch=[held, held, four], far=(d_aa, d_ba, d_as, d_bs),
    )
    recv0, r_send, send1 = phase(recv0, r_send, send1)
    p0 = total(keep0, recv0)
    p0_in = line(0, p0)
    g_x, g_xy, g_y, g_sib, p0, send1 = phase(g_x, g_xy, g_y, g_sib, p0, send1)
    recv1 = py(send1)
    g_xy, g_sx, g_sy = px(g_xy), pc(g_x), pc(g_y)
    g_xy, g_sx, g_sy, g_sib, wt_all1, recv1, p0_in, low1, r_send, send2 = phase(
        g_xy, g_sx, g_sy, g_sib, wt_all, recv1, p0_in, low, r_send, send2
    )
    g_s, g_sxy, wt_sib = pc(g_sib), pc(g_xy), pc(wt_all1)
    p0, p1 = line_sum(p0, p0_in), total(keep1, recv1)
    heads = phase(qkv, kv, lo, hi, lse, o0, o1, g_own, g_x, g_y, g_xy, g_s, g_sx, g_sy, g_sxy, p0, p1)
    p0, p1 = heads[-2:]
    p0_in, p1_in, recv2, low_x, r_recv = line(1, p0), line(0, p1), py(send2), px(low1), px(r_send)
    dqkv, dqkv_sib = call(
        attend_back_kernel, "attend_back", (scal, qlo, qhi), heads[:-2], (shape(6 * PITCH, 4 * SUB),) * 2, 19,
        scratch=[
            pltpu.VMEM((2 * PITCH, seq), BF), pltpu.VMEM((2, seq), F32), pltpu.VMEM((2 * PITCH, seq), F32),
            pltpu.VMEM((2, seq, PITCH), F32), pltpu.VMEM((2, seq, PITCH), F32),
        ],
    )
    dqkv, dqkv_sib, p0_in, p1_in, recv2, low_x, r_recv = phase(dqkv, dqkv_sib, p0_in, p1_in, recv2, low_x, r_recv)

    from_sib = pc(dqkv_sib)
    p0, p1, p2 = line_sum(p0, p0_in), line_sum(p1, p1_in), total(keep2, recv2)
    p0_in, p1_in, p2_in = line(2, p0), line(1, p1), line(0, p2)
    keep_o, o_send = call(
        heads_outer_kernel, "heads_outer", (scal,), (o0, att_y, att_s, att_sy, after(low, p0, p1, p2), low_x),
        (shape(2 * n2, width, dtype=F32), shape(2 * n2, width)), 2,
    )
    o_recv = pc(o_send)
    lanes = (half + 127) // 128 * 128
    q_own, q_send = call(
        qkv_outer_kernel, "qkv_outer", (), (dqkv, dqkv_sib, after(h1, o_send)),
        (shape(3 * n2 + 16, lanes), shape(3 * n2, lanes)), 4,
    )
    o_own, o_send = call(
        heads_sum_kernel, "heads_sum", (), (keep_o, after(o_recv, q_own)),
        (shape(2 * n2, lanes, dtype=F32), shape(2 * n2, lanes)), 1,
    )
    o_recv = py(o_send)
    q_send = after(q_send, o_send)
    to_x, keep = call(
        spread_kernel, "spread", (), (w_all, wt_sib, after(dqkv, q_send), from_sib),
        (shape(width, two), shape(width, two, dtype=F32)), 4,
    )
    p0_in, p1_in, p2_in, o_recv, keep, q_send, to_x = phase(p0_in, p1_in, p2_in, o_recv, keep, q_send, to_x)
    (qa,) = call(gather_kernel, "gather", (), (q_own, o_own, o_recv), (shape(5 * n2 + 16, lanes),), 1)
    p1, p2 = line_sum(p1, p1_in), line_sum(p2, p2_in)
    p1_in, p2_in, qa_in, q_recv, from_x = line(2, p1), line(1, p2), line(0, qa), py(q_send), px(to_x)
    g0 = line_end(p0, p0_in)
    r_a, r_b = call(
        result_sum_kernel, "result_sum", (), (r_own, after(r_recv, qa, p1, p2)), (shape(half, SUB), shape(half, SUB)), 1
    )
    p1_in, p2_in, qa_in, q_recv, g0, low_b, r_b = phase(p1_in, p2_in, qa_in, q_recv, g0, low_b, r_b)
    p2, qa, qb = line_sum(p2, p2_in), line_sum(qa, qa_in), q_recv
    p2_in, qa_in, qb_in = line(2, p2), line(1, qa), line(0, qb)
    from_x = after(from_x, p2, qa)
    to_y, own = call(
        spread2_kernel, "spread2", (), (keep, from_x), (shape(half, two), shape(half, two, dtype=F32)), 2,
    )
    from_y, low_y = py(to_y), py(after(low_b, to_y))
    g1 = line_end(p1, p1_in)
    p2_in, qa_in, qb_in, g1 = phase(p2_in, qa_in, qb_in, g1)
    qa, qb = line_sum(qa, qa_in), line_sum(qb, qb_in)
    grad, normed, stats, sums1 = call(
        norm1_stats_kernel, "norm1_stats", (scal,), (own, after(from_y, qa, qb), a00, b00, small, sums2_b),
        (shape(half, two, dtype=F32), shape(half, two, dtype=F32), shape(16, lanes, dtype=F32), shape(8, half, dtype=F32)),
        2,
    )
    qa_in, qb_in, stats_y, r_y = line(2, qa), line(1, qb), py(stats), py(r_b)
    g2 = line_end(p2, p2_in)
    stats_y, r_y, g2 = phase(stats_y, r_y, g2)
    sums = jnp.concatenate((sums1[:2], sums2_a[:4] + stats_y[8:12, :half], sums1[6:]), 0)
    sums_in = [lax.ppermute(sums, "tr", swap_perm("tr", bit)) for bit in (1, 2, 3)]
    (gin,) = call(
        norm1_back_kernel, "norm1_back", (scal,), (grad, normed, stats, stats_y, gm, low_y), (shape(half, two),), 1,
    )
    (result,) = call(place_kernel, "place", (scal,), (r_a, r_y), (shape(half, two),), 1)
    qa_in, qb_in, gin, result, *sums_in = phase(qa_in, qb_in, gin, result, *sums_in)
    sums = (sums + sums_in[0]) + (sums_in[1] + sums_in[2])
    qb = line_sum(qb, qb_in)
    qb_in, sums_in = line(2, qb), [dp_step(sums, bit) for bit in (1, 2, 3)]
    ga = line_end(qa, qa_in)
    qb_in, ga, *sums_in = phase(qb_in, ga, *sums_in)
    sums = dp_last((sums + sums_in[0]) + (sums_in[1] + sums_in[2]))
    dwd, dwu = jnp.concatenate((g0, g1[:rest]), 0), jnp.concatenate((g1[rest:], g2), 0)
    dwq_own, dwq_y, dwo = ga[: 3 * n2 + 16, :half], line_end(qb, qb_in)[:, :half], ga[3 * n2 + 16 :, :half]

    bias_q = dwq_own[3 * n2]
    dwq_own = dwq_own[: 3 * n2]
    first = jnp.where(ypos == 0, dwq_own, dwq_y).reshape(3, n2, half)
    second = jnp.where(ypos == 0, dwq_y, dwq_own).reshape(3, n2, half)
    dwq = jnp.concatenate((first, second), 1)
    gbu = lax.dynamic_slice_in_dim(dwu[half], ypos * n_up, n_up, 0)
    return (
        result.T, gin.T, sums[0], sums[1], dwq[0].T, bias_q[:n2], dwq[1].T, dwq[2].T, bias_q[n2 : 2 * n2],
        dwo, sums[4], sums[2], sums[3], dwu[:half, :units], gbu, dwd[:, :units].T, sums[5],
    )


def solution(mesh):
    rows = P(("dp", "tr"), "tc")
    placed = (
        rows, P("dp"), P("dp"), P("tc"), P("tc"), P("tc", "tr"), P(("tr", "tc")), P("tc", "tr"),
        P("tc", "tr"), P(("tr", "tc")), P("tr", "tc"), P("tc"), P("tc"), P("tc"), P("tc", "tr"),
        P(("tr", "tc")), P("tr", "tc"), P("tc"), rows,
    )
    outs = (
        rows, rows, P("tc"), P("tc"), P("tc", "tr"), P(("tr", "tc")), P("tc", "tr"), P("tc", "tr"),
        P(("tr", "tc")), P("tr", "tc"), P("tc"), P("tc"), P("tc"), P("tc", "tr"), P(("tr", "tc")),
        P("tr", "tc"), P("tc"),
    )
    return jax.shard_map(local, mesh=mesh, in_specs=placed, out_specs=outs, check_vma=False)
```

```python
import jax
import jax.numpy as jnp
from jax import lax
from jax.experimental import pallas as pl
from jax.experimental.pallas import tpu as pltpu
from jax.sharding import PartitionSpec as P

DH = 72
PITCH = 80
SUB = 256
HALF = SUB // 2
EPSILON = 1e-06
GELU_C = 0.7978845608028654
GELU_A = 0.044715
MASKED = -1e30
SCALE = DH**-0.5
SCALE2 = SCALE * 1.4426950408889634
BF = jnp.bfloat16
F32 = jnp.float32
MIB = 1024 * 1024


def swap_perm(axis, bit):
    return [(i, i ^ bit) for i in range(lax.axis_size(axis))]


def px(v):
    return lax.ppermute(v, "tr", swap_perm("tr", 2))


def pc(v):
    return lax.ppermute(v, "tr", swap_perm("tr", 1))


def py(v):
    return lax.ppermute(v, "tc", swap_perm("tc", 1))


def phase(*values):
    return lax.optimization_barrier(values)


def after(v, *earlier):
    return phase(v, *earlier)[0]


def dot(a, b):
    return jnp.dot(a, b, preferred_element_type=F32)


def dot_tn(a, b):
    return lax.dot_general(a, b, (((0,), (0,)), ((), ())), preferred_element_type=F32)


def dot_nt(a, b):
    return lax.dot_general(a, b, (((1,), (1,)), ((), ())), preferred_element_type=F32)


def rows_at(v, first, count):
    return lax.dynamic_slice_in_dim(v, first, count, 0)


def cols_at(v, first, count):
    return lax.dynamic_slice_in_dim(v, first, count, 1)


def dp_swap(v, bit):
    return lax.ppermute(v, "dp", swap_perm("dp", bit))


def line(step, v):
    if lax.axis_size("dp") != 4:
        return v
    return lax.ppermute(v, "dp", ([(0, 1), (3, 2)], [(1, 2), (2, 1)], [(1, 0), (2, 3)])[step])


def line_sum(v, received):
    if lax.axis_size("dp") != 4:
        return v
    return (v.astype(F32) + received.astype(F32)).astype(BF)


def line_end(v, received):
    if lax.axis_size("dp") != 4:
        return lax.psum(v, "dp").astype(F32)
    place = lax.axis_index("dp")
    return jnp.where((place == 1) | (place == 2), v, received).astype(F32)


def dp_step(v, bit):
    return dp_swap(v, bit) if lax.axis_size("dp") == 4 else jnp.zeros_like(v)


def dp_last(v):
    return v if lax.axis_size("dp") == 4 else lax.psum(v, "dp")


VM = pl.BlockSpec(memory_space=pltpu.VMEM)
SM = pl.BlockSpec(memory_space=pltpu.SMEM)


def shape(*dims, dtype=BF):
    return jax.ShapeDtypeStruct(dims, dtype)


ANY = pl.BlockSpec(memory_space=pl.ANY)


def call(body, name, scalars, arrays, outs, us, scratch=(), vmem=12, far=()):
    return pl.pallas_call(
        body,
        out_shape=tuple(outs),
        in_specs=[SM] * len(scalars) + [VM] * len(arrays) + [ANY] * len(far),
        out_specs=tuple([VM] * len(outs)),
        scratch_shapes=list(scratch),
        compiler_params=pltpu.CompilerParams(vmem_limit_bytes=vmem * MIB),
        cost_estimate=pl.CostEstimate(
            flops=int(us * 600e6), bytes_accessed=int(us * 3e6), transcendentals=0
        ),
        name=name,
    )(*scalars, *arrays, *far)


def spots():
    return [(rc, ry, rx) for rc in range(2) for ry in range(2) for rx in range(2)]


def block_of(me, rc, ry, rx):
    return me ^ (rx * 4 + rc * 2 + ry)


def span(block):
    return pl.ds(pl.multiple_of(block * SUB, SUB), SUB)


def head_rows(pos):
    return pl.ds(pl.multiple_of(pos * 2 * DH, 16), 2 * DH)


def row_of(col):
    return jnp.broadcast_to(col, (col.shape[0], 128)).T[0:1]


def column(i, *parts):
    return jnp.concatenate([p[...].T[:, i : i + 1] for p in parts], 0)


def pack_kernel(scal, q, k, v, own, send):
    for i, w in enumerate((q, k, v)):
        there = slice(2 * DH * i, 2 * DH * (i + 1))
        own[there, :] = w[head_rows(scal[0]), :]
        send[there, :] = w[head_rows(1 - scal[0]), :]


def unpack_kernel(own, other, wt, w):
    both = jnp.concatenate((own[...].astype(F32), other[...].astype(F32)), 1)
    gap = jnp.zeros((PITCH - DH, both.shape[1]), F32)
    parts = []
    for i in range(6):
        parts += [both[DH * i : DH * (i + 1)], gap]
    whole = jnp.concatenate(parts, 0).astype(BF)
    wt[...] = whole
    w[...] = whole.T


def norm_qkv_kernel(
    scal, a00, b00, a01, b01, a10, b10, a11, b11, weights, bias, small, small_y,
    h_ref, qkv_ref, kv_ref, res_ref, gain_s, shift_s, bias_s,
):
    ypos, me = scal[0], scal[1]
    half = a00.shape[0]
    gain_s[...] = jnp.broadcast_to(column(0, small, small_y), gain_s.shape)
    shift_s[...] = jnp.broadcast_to(column(1, small, small_y), shift_s.shape)
    bias_s[...] = jnp.broadcast_to(column(0, bias), bias_s.shape)
    sources = {(0, 0): (a00, b00), (1, 0): (a01, b01), (0, 1): (a10, b10), (1, 1): (a11, b11)}
    for p, (rc, ry, rx) in enumerate(spots()):
        here = slice(p * SUB, (p + 1) * SUB)
        there = span(block_of(me, rc, ry, rx))
        cols = span(ypos ^ ry)
        sa, sb = sources[(rc, rx)]
        raw = jnp.concatenate((sa[:, cols], sb[:, cols]), 0)
        if rc == 0 and ry == 0:
            res_ref[:, rx * SUB : (rx + 1) * SUB] = raw
        v = raw.astype(F32)
        mean = jnp.sum(v, axis=0, keepdims=True) / (2 * half)
        square = jnp.sum(v * v, axis=0, keepdims=True) / (2 * half)
        root = lax.rsqrt(square - mean * mean + EPSILON)
        hidden = ((v - mean) * root * gain_s[...] + shift_s[...]).astype(BF)
        h_ref[:, here] = hidden
        qkv = (dot(weights[...], hidden) + bias_s[...]).astype(BF)
        qkv_ref[:, there] = qkv
        for i in range(4):
            kv_ref[there, 128 * i : 128 * i + PITCH] = qkv[PITCH * (2 + i) : PITCH * (3 + i), :].T


def attend_kernel(scal, klo, khi, qkv, kv, lo, hi, o0, o1, lse, s_ref, acc_ref):
    me = scal[1]
    outs = (o0, o1)
    places = lax.broadcasted_iota(jnp.int32, (SUB, SUB), 0)
    lanes = lax.broadcasted_iota(jnp.int32, (1, SUB), 1)
    for rc, ry, rx in sorted(spots(), reverse=True):
        block = block_of(me, rc, ry, rx)
        cols = span(block)
        low, high = lo[:, cols], hi[:, cols]
        own = lanes + block * SUB

        def score(kb, tops):
            base = kb * SUB
            allowed = ((places >= low - base) & (places < high - base)) | (places == own - base)
            new = []
            for h in range(2):
                s = dot(kv[span(kb), 128 * h : 128 * h + PITCH], qkv[PITCH * h : PITCH * (h + 1), cols])
                s = jnp.where(allowed, s, MASKED)
                s_ref[h, span(kb), :] = s
                new.append(jnp.maximum(tops[h], jnp.max(s.reshape(SUB // 8, 8, SUB), axis=0)))
            return tuple(new)

        start = jnp.full((8, SUB), MASKED, F32)
        tops = lax.fori_loop(klo[block], khi[block], score, (start, start))
        tops = [jnp.max(t, axis=0, keepdims=True) * SCALE2 for t in tops]
        acc_ref[...] = jnp.zeros_like(acc_ref)

        def weigh(kb, carry):
            for h in range(2):
                weights = jnp.exp2(s_ref[h, span(kb), :] * SCALE2 - tops[h]).astype(BF)
                acc_ref[h] += dot(qkv[PITCH * (4 + h) : PITCH * (5 + h), span(kb)], weights)
            return carry

        lax.fori_loop(klo[block], khi[block], weigh, 0)
        heads = []
        for h in range(2):
            total = acc_ref[h, DH : DH + 1, :]
            heads.append(acc_ref[h, :DH, :] / total)
            lse[h : h + 1, cols] = tops[h] + jnp.log2(total)
        rows = slice(rc * 2 * DH, (rc + 1) * 2 * DH)
        outs[ry][rows, rx * SUB : (rx + 1) * SUB] = jnp.concatenate(heads, 0).astype(BF)


def attend_back_kernel(
    scal, qlo, qhi, qkv, kv, lo, hi, lse, o0, o1, g0, gx, gy, gxy, s0, sx, sy, sxy,
    out0, out1, gt, delta, dqt, dk, dv,
):
    me = scal[1]
    outs = (o0, o1)
    n2 = 2 * DH
    grads = (g0, gx, gy, gxy, s0, sx, sy, sxy)
    for p, (rc, ry, rx) in enumerate(spots()):
        cols = span(block_of(me, rc, ry, rx))
        rows = slice(rc * n2, (rc + 1) * n2)
        gtile = (grads[p][...] if p in (0, 4) else grads[p][rows, :]).astype(F32)
        both = gtile * outs[ry][rows, rx * SUB : (rx + 1) * SUB].astype(F32)
        for h in range(2):
            part = slice(DH * h, DH * (h + 1))
            padded = jnp.concatenate((gtile[part], jnp.zeros((PITCH - DH, SUB), F32)), 0)
            gt[PITCH * h : PITCH * (h + 1), cols] = padded.astype(BF)
            delta[h : h + 1, cols] = jnp.sum(both[part], axis=0, keepdims=True)
    dqt[...] = jnp.zeros_like(dqt)
    dk[...] = jnp.zeros_like(dk)
    dv[...] = jnp.zeros_like(dv)
    places = lax.broadcasted_iota(jnp.int32, (SUB, SUB), 0)
    lanes = lax.broadcasted_iota(jnp.int32, (1, SUB), 1)

    @pl.loop(0, 8)
    def _(kb):
        keys = span(kb)
        base = kb * SUB

        def body(qb, carry):
            cols = span(qb)
            low, high = lo[:, cols] - base, hi[:, cols] - base
            own = lanes + (qb * SUB - base)
            allowed = ((places >= low) & (places < high)) | (places == own)
            for h in range(2):
                head = slice(PITCH * h, PITCH * (h + 1))
                s = dot(kv[keys, 128 * h : 128 * h + PITCH], qkv[head, cols])
                probs = jnp.where(allowed, jnp.exp2(s * SCALE2 - lse[h : h + 1, cols]), 0.0)
                gprobs = dot(kv[keys, 256 + 128 * h : 256 + 128 * h + PITCH], gt[head, cols])
                gscores = (probs * (gprobs - delta[h : h + 1, cols])).astype(BF)
                dv[h, keys, :] += dot_nt(probs.astype(BF), gt[head, cols])
                dk[h, keys, :] += dot_nt(gscores, qkv[head, cols])
                dqt[head, cols] += dot(qkv[PITCH * (2 + h) : PITCH * (3 + h), keys], gscores)
            return carry

        lax.fori_loop(qlo[kb], qhi[kb], body, 0)

    for p, (rc, ry, rx) in enumerate(spots()):
        out = (out0, out1)[rc]
        here = slice((ry * 2 + rx) * SUB, (ry * 2 + rx + 1) * SUB)
        rows = span(block_of(me, rc, ry, rx))
        out[: 2 * PITCH, here] = (dqt[:, rows] * SCALE).astype(BF)
        for h in range(2):
            out[PITCH * (2 + h) : PITCH * (3 + h), here] = (dk[h, rows, :].T * SCALE).astype(BF)
            out[PITCH * (4 + h) : PITCH * (5 + h), here] = dv[h, rows, :].T.astype(BF)


def own_and_y(ypos, w):
    return [w[head_rows(ypos), :], w[head_rows(1 - ypos), :]]


def out_weights_kernel(scal, own_a, own_b, x_a, x_b, w):
    parts = []
    for a, b in ((own_a, own_b), (x_a, x_b)):
        for wa, wb in zip(own_and_y(scal[0], a), own_and_y(scal[0], b)):
            parts.append(jnp.concatenate((wa, wb), 1))
    w[...] = jnp.concatenate(parts, 0)


def mix_kernel(own, y, x, xy, sib, ysib, xsib, xysib, w, w_sib, res, small, small_y, mixed, h2t, h2):
    n2 = 2 * DH
    gain, shift, bias = [column(i, small, small_y) for i in (2, 3, 4)]
    parts = []
    for rows, group in ((slice(0, n2), (own, y, x, xy)), (slice(n2, 2 * n2), (sib, ysib, xsib, xysib))):
        for i, o in enumerate(group):
            if i < 2:
                parts.append(o[rows, :])
            else:
                parts.append(jnp.concatenate((o[rows, SUB:], o[rows, :SUB]), 1))
    att = jnp.concatenate(parts, 0)
    weights = jnp.concatenate((w[...], w_sib[...]), 0)
    v = res[...].astype(F32) + dot_tn(weights, att) + bias
    mixed[...] = v
    mean = jnp.mean(v, axis=0, keepdims=True)
    root = lax.rsqrt(jnp.mean(v * v, axis=0, keepdims=True) - mean * mean + EPSILON)
    hidden = ((v - mean) * root * gain + shift).astype(BF)
    h2t[...] = hidden
    h2[...] = hidden.T


def turn_kernel(oa, ob, xa, xb, gof, go):
    half = oa.shape[0]
    for rx, (a, b) in enumerate(((oa, ob), (xa, xb))):
        here = slice(rx * SUB, (rx + 1) * SUB)
        gof[:half, here] = a[...]
        gof[half:, here] = b[...]
        go[here, :] = jnp.concatenate((a[...], b[...]), 0).T


def gelu_both(u):
    square = u * u
    tangent = jnp.tanh(GELU_C * (u + GELU_A * square * u))
    plus = 0.5 * (1.0 + tangent)
    slope = plus + 0.5 * u * (1.0 - tangent * tangent) * GELU_C * (1.0 + 3.0 * GELU_A * square)
    return u * plus, slope


def fetch(sources, buffers, sems):
    half = sources[0].shape[0]
    copies = []
    for i, src in enumerate(sources):
        dst = buffers[i // 2].at[pl.ds((i % 2) * half, half), :]
        copies.append(pltpu.make_async_copy(src, dst, sems.at[i]))
        copies[-1].start()
    return copies


def feed_up_kernel(h2, bias, ua, ub, act, slope, u, sems):
    copies = fetch((ua, ub), (u,), sems)
    for c in copies:
        c.wait()
    value, sl = gelu_both(dot(h2[...], u[...]) + bias[...])
    act[...] = value.astype(BF)
    slope[...] = sl.astype(BF)


def feed_grad(go, slope, u, d, copies, gu, sums):
    for c in copies[:2]:
        c.wait()
    rounded = (dot(go[...], d[...]) * slope[...].astype(F32)).astype(BF)
    gu[...] = rounded
    sums[...] = jnp.broadcast_to(jnp.sum(rounded.astype(F32), axis=0, keepdims=True), sums.shape)
    for c in copies[2:]:
        c.wait()
    return dot_nt(u[...], gu[...])


def feed_own_kernel(go, slope, ua, ub, da, db, gu, sums, part, u, d, sems):
    part[...] = feed_grad(go, slope, u, d, fetch((da, db, ua, ub), (d, u), sems), gu, sums)


def feed_sib_kernel(go, slope, part, act, h2t, gof, ua, ub, da, db, gu, sums, send, own, down, up, u, d, sems):
    copies = fetch((da, db, ua, ub), (d, u), sems)
    width, rows = down.shape[1], h2t.shape[0]
    down[...] = padded_units(dot(gof[...], act[...]).astype(BF), width)
    total = feed_grad(go, slope, u, d, copies, gu, sums) + part[...]
    send[...] = total[:, SUB:].astype(BF)
    own[...] = total[:, :SUB]
    up[:rows, :] = padded_units(dot(h2t[...], gu[...]).astype(BF), width)
    up[rows:, :] = padded_units(jnp.concatenate((sums[...], sums[...]), 0).astype(BF), width)


def padded_units(v, width):
    return jnp.concatenate((v, jnp.zeros((v.shape[0], width - v.shape[1]), v.dtype)), 1)


def down_own_kernel(gof, act, recv, keep0, send0, keep_rest, send_rest):
    half, width = recv.shape[0] // 2, recv.shape[1]
    total = padded_units(dot(gof[...], act[...]), width) + recv[...].astype(F32)
    rows = keep0.shape[0]
    keep0[...] = total[:rows]
    keep_rest[...] = total[rows:half]
    send0[...] = total[half : half + rows].astype(BF)
    send_rest[...] = total[half + rows :].astype(BF)


def up_own_kernel(h2t, gu, sums, recv, keep_rest, send_rest, keep1, send1, keep2, send2):
    half = h2t.shape[0] // 2
    width = recv.shape[1]
    total = padded_units(dot(h2t[...], gu[...]), width) + recv[: 2 * half, :].astype(F32)
    more = padded_units(jnp.concatenate((sums[...], sums[...]), 0), width) + recv[2 * half :, :].astype(F32)
    rest = keep_rest.shape[0]
    rows = keep1.shape[0] - rest
    keep1[:rest, :] = keep_rest[...]
    send1[:rest, :] = send_rest[...]
    keep1[rest:, :] = total[:rows]
    send1[rest:, :] = total[half : half + rows].astype(BF)
    keep2[: half - rows, :] = total[rows:half]
    keep2[half - rows :, :] = more
    send2[: half - rows, :] = total[half + rows :].astype(BF)
    send2[half - rows :, :] = more.astype(BF)


def result_kernel(act0, act1, mixed, small, small_y, daa, dba, das, dbs, send, own, d0, d1, sems):
    copies = fetch((daa, dba, das, dbs), (d0, d1), sems)
    for c in copies:
        c.wait()
    part = dot_nt(d0[...], act0[...]) + dot_nt(d1[...], act1[...])
    send[...] = part[:, SUB:].astype(BF)
    own[...] = part[:, :SUB] + mixed[:, :SUB] + column(5, small, small_y)


def result_sum_kernel(own, recv, out_a, out_b):
    half = out_a.shape[0]
    total = (own[...] + recv[: own.shape[0], :].astype(F32)).astype(BF)
    out_a[...] = total[:half]
    out_b[...] = total[half:]


def place_kernel(scal, own, other, out):
    out[:, span(scal[0])] = own[...]
    out[:, span(1 - scal[0])] = other[...]


def norm2_back_kernel(
    own, recv, mixed, goa, gob, small, small_y, w, w_sib, gm, low, low_b, g_own, g_sib, g_y, g_x, g_xy, sums_a, sums_b
):
    e = own[...] + recv[...].astype(F32)
    v = mixed[:, :SUB]
    mean = jnp.mean(v, axis=0, keepdims=True)
    root = lax.rsqrt(jnp.mean(v * v, axis=0, keepdims=True) - mean * mean + EPSILON)
    n = (v - mean) * root
    weighted = e * column(2, small, small_y)
    go = jnp.concatenate((goa[...], gob[...]), 0).astype(F32)
    grad = go + root * (
        weighted
        - jnp.mean(weighted, axis=0, keepdims=True)
        - n * jnp.mean(weighted * n, axis=0, keepdims=True)
    )
    gm[...] = grad
    rounded = grad.astype(BF)
    low[...] = rounded
    low_b[...] = rounded[low_b.shape[0] :]
    n2 = 2 * DH
    mine = dot(w[...], rounded).astype(BF)
    sibs = dot(w_sib[...], rounded).astype(BF)
    g_own[...] = mine[:n2]
    g_sib[...] = sibs[:n2]
    for i, out in enumerate((g_y, g_x, g_xy)):
        rows = slice(n2 * (i + 1), n2 * (i + 2))
        out[:n2, :] = mine[rows]
        out[n2:, :] = sibs[rows]
    for i, q in enumerate((e * n, e, grad, go)):
        col = jnp.sum(q, axis=1, keepdims=True)
        half = low_b.shape[0]
        sums_a[i : i + 1, :] = row_of(col[:half])
        sums_b[i : i + 1, :] = row_of(col[half:])
    sums_a[4:, :] = jnp.zeros_like(sums_a[4:, :])
    sums_b[4:, :] = jnp.zeros_like(sums_b[4:, :])


def heads_outer_kernel(scal, own, y, sib, ysib, low, low_x, keep, send):
    right = jnp.concatenate((low[...], low_x[...]), 1)
    n2 = 2 * DH
    for rows, a, b, out in ((slice(0, n2), own, y, keep), (slice(n2, 2 * n2), sib, ysib, send)):
        out[head_rows(scal[0]), :] = dot_nt(a[rows, :], right).astype(out.dtype)
        out[head_rows(1 - scal[0]), :] = dot_nt(b[rows, :], right).astype(out.dtype)


def gather_kernel(q_own, o_own, o_recv, out):
    n = q_own.shape[0]
    out[:n, :] = q_own[...]
    out[n:, :] = (o_own[...] + o_recv[...].astype(F32)).astype(BF)


def qkv_outer_kernel(dqkv, dqkv_sib, h1, own, send):
    mid = dqkv.shape[1]
    total = dot_nt(dqkv[...], h1[:, :mid]) + dot_nt(dqkv_sib[...], h1[:, mid:])
    half = h1.shape[0] // 2
    lanes = own.shape[1]
    rows = jnp.concatenate([total[PITCH * i : PITCH * i + DH] for i in range(6)], 0)
    n = 6 * DH
    own[:n, :] = padded_units(rows[:, :half].astype(BF), lanes)
    send[...] = padded_units(rows[:, half:].astype(BF), lanes)
    col = jnp.sum(dqkv[...].astype(F32) + dqkv_sib[...].astype(F32), axis=1, keepdims=True)
    cols = [col[PITCH * i : PITCH * i + DH] for i in (0, 1, 4, 5)]
    cols.append(jnp.zeros((lanes - 4 * DH, 1), F32))
    own[n:, :] = jnp.broadcast_to(row_of(jnp.concatenate(cols, 0)), (16, lanes)).astype(BF)


def heads_sum_kernel(keep, recv, own, send):
    half = keep.shape[1] // 2
    total = keep[...] + recv[...].astype(F32)
    own[...] = padded_units(total[:, :half], own.shape[1])
    send[...] = padded_units(total[:, half:].astype(BF), send.shape[1])


def spread_kernel(w, wt_sib, dqkv, from_sib, to_x, keep):
    total = dot(w[...], dqkv[...]) + dot_tn(wt_sib[...], from_sib[...])
    for ry in range(2):
        first = 2 * ry * SUB
        at = slice(ry * SUB, (ry + 1) * SUB)
        keep[:, at] = total[:, first : first + SUB]
        to_x[:, at] = total[:, first + SUB : first + 2 * SUB].astype(BF)


def spread2_kernel(keep, from_x, to_y, own):
    half = own.shape[0]
    total = keep[...] + from_x[...].astype(F32)
    own[...] = total[:half]
    to_y[...] = total[half:].astype(BF)


def norm1_stats_kernel(scal, own, from_y, a, b, small, sums_b, grad, normed, stats, sums):
    ypos = scal[0]
    half = a.shape[0]
    gain = column(0, small)
    cols_sums = [0.0, 0.0]
    stats[...] = jnp.zeros_like(stats)
    for ry in range(2):
        cols = span(ypos ^ ry)
        here = slice(ry * SUB, (ry + 1) * SUB)
        e = own[:, here] + from_y[:, (1 - ry) * SUB : (2 - ry) * SUB].astype(F32)
        va, vb = a[:, cols].astype(F32), b[:, cols].astype(F32)
        mean = (jnp.sum(va, 0, keepdims=True) + jnp.sum(vb, 0, keepdims=True)) / (2 * half)
        square = (jnp.sum(va * va, 0, keepdims=True) + jnp.sum(vb * vb, 0, keepdims=True)) / (2 * half)
        root = lax.rsqrt(square - mean * mean + EPSILON)
        n = (va - mean) * root
        w = e * gain
        grad[:, here] = w
        normed[:, here] = n
        stats[0:1, here] = jnp.sum(w, 0, keepdims=True)
        stats[1:2, here] = jnp.sum(w * n, 0, keepdims=True)
        stats[2:3, here] = root
        cols_sums[0] += jnp.sum(e * n, 1, keepdims=True)
        cols_sums[1] += jnp.sum(e, 1, keepdims=True)
    stats[8:, :half] = sums_b[...]
    for i in range(2):
        sums[i : i + 1, :] = row_of(cols_sums[i])
    sums[2:, :] = jnp.zeros_like(sums[2:, :])


def norm1_back_kernel(scal, grad, normed, stats, recv, gm_own, gm_y, out):
    ypos = scal[0]
    width = 2 * grad.shape[0]
    for ry in range(2):
        here = slice(ry * SUB, (ry + 1) * SUB)
        other = slice((1 - ry) * SUB, (2 - ry) * SUB)
        total = (stats[0:1, here] + recv[0:1, other]) / width
        along = (stats[1:2, here] + recv[1:2, other]) / width
        gm = gm_own[: grad.shape[0], :] if ry == 0 else gm_y[...].astype(F32)
        whole = gm + stats[2:3, here] * (grad[:, here] - total - normed[:, here] * along)
        out[:, span(ypos ^ ry)] = whole.astype(BF)


def local(
    layer_input, picture, token_kept, ln1_gain, ln1_bias, w_query, b_query, w_key, w_value, b_value,
    w_out, b_out, ln2_gain, ln2_bias, w_up, b_up, w_down, b_down, grad_out,
):
    ypos = lax.axis_index("tc").astype(jnp.int32)
    trpos = lax.axis_index("tr").astype(jnp.int32)
    me = trpos * 2 + ypos
    half = layer_input.shape[1]
    width = 2 * half
    seq = picture.shape[0]
    n2 = b_query.shape[0]
    units = w_up.shape[1]
    n_up = b_up.shape[0]
    scal = jnp.stack((ypos, me))
    two = 2 * SUB

    a00 = layer_input.T
    qkv_weights = (w_query.T, w_key.T, w_value.T)
    go_t = grad_out.T
    u_aa, d_aa = w_up, w_down.T
    small = jnp.stack(
        (ln1_gain, ln1_bias, ln2_gain, ln2_bias, b_out, b_down, jnp.pad(b_up, (0, half - n_up)), ln1_gain)
    )
    w_own, w_send = call(pack_kernel, "pack", (scal,), qkv_weights, (shape(3 * n2, half),) * 2, 1)
    b00, a10, a01, small_y, d_as = py(a00), px(a00), pc(a00), py(small), pc(d_aa)
    go_a = cols_at(go_t, ypos * SUB, SUB)
    go_send = cols_at(go_t, (1 - ypos) * SUB, SUB)
    quarter = half // lax.axis_size("dp")
    first = lax.axis_index("dp") * quarter
    u_part, d_part = rows_at(u_aa, first, quarter), rows_at(d_aa, first, quarter)
    qkv_bias = jnp.concatenate((b_query, jnp.zeros_like(b_query), b_value)).reshape(6, DH)
    ones = (jnp.arange(6) >= 4).astype(F32)[:, None]
    qkv_bias = jnp.concatenate((qkv_bias, ones, jnp.zeros((6, PITCH - DH - 1), F32)), 1).reshape(1, -1)
    qkv_bias = jnp.broadcast_to(qkv_bias, (8, 6 * PITCH))

    numbers = jnp.arange(8, dtype=jnp.int32)[:, None]
    hot = (picture[None, :] == numbers).astype(jnp.int32)
    counts = jnp.sum(hot, axis=1)
    kept = jnp.sum(hot * token_kept[None, :], axis=1)
    starts = jnp.cumsum(counts) - counts
    lo = jnp.sum(hot * starts[:, None], axis=0)
    hi = jnp.sum(hot * (starts + kept)[:, None], axis=0)
    end = jnp.sum(hot * (starts + counts)[:, None], axis=0)
    blocks = seq // SUB
    klo = qlo = lo.reshape(blocks, SUB)[:, 0] // SUB
    lasts = jnp.arange(1, blocks + 1, dtype=jnp.int32) * SUB
    khi = (jnp.maximum(lasts, hi.reshape(blocks, SUB)[:, -1]) + SUB - 1) // SUB
    qhi = (jnp.maximum(lasts, end.reshape(blocks, SUB)[:, -1]) + SUB - 1) // SUB
    lo, hi = lo[None, :], hi[None, :]

    b00, a10, a01, small_y, d_as, w_send, u_part = phase(b00, a10, a01, small_y, d_as, w_send, u_part)
    b10, w_other, b01, a11, u_part = px(b00), py(w_send), pc(b00), pc(a10), py(u_part)
    b10, w_other, b01, a11, u_part, w_out1, go_send, go_a, d_part = phase(
        b10, w_other, b01, a11, u_part, w_out, go_send, go_a, d_part
    )
    u_ba = lax.all_gather(u_part, "dp", axis=0, tiled=True)
    b11, w0b, w2a, go_b, d_part = pc(b10), py(w_out1), px(w_out1), py(go_send), py(d_part)
    wt_all, w_all = call(
        unpack_kernel, "unpack", (), (w_own, w_other),
        (shape(6 * PITCH, width), shape(width, 6 * PITCH)), 2,
    )
    h1, qkv, kv, resid = call(
        norm_qkv_kernel, "norm_qkv", (scal,),
        (a00, b00, a01, b01, a10, b10, a11, b11, wt_all, qkv_bias, small, small_y),
        (shape(width, seq), shape(6 * PITCH, seq), shape(seq, 512), shape(width, two)),
        8,
        scratch=[pltpu.VMEM((width, SUB), F32)] * 2 + [pltpu.VMEM((6 * PITCH, SUB), F32)],
    )

    qkv, w2a = phase(qkv, w2a)
    w2b, go_xa = py(w2a), px(after(go_a, w2a))

    o0, o1, lse = call(
        attend_kernel, "attend", (scal, klo, khi), (qkv, kv, lo, hi),
        (shape(2 * n2, two),) * 2 + (shape(2, seq, dtype=F32),), 12,
        scratch=[pltpu.VMEM((2, seq, SUB), F32), pltpu.VMEM((2, PITCH, SUB), F32)],
    )
    o0, o1, w0b, w2b, go_b, go_xa, d_part, u_ba = phase(o0, o1, w0b, w2b, go_b, go_xa, d_part, u_ba)
    d_ba = lax.all_gather(d_part, "dp", axis=0, tiled=True)
    att_y, att_x, att_s = py(o1), px(o0), pc(o0)
    (wo,) = call(out_weights_kernel, "out_weights", (scal,), (w_out, w0b, w2a, w2b), (shape(4 * n2, width),), 1)
    wo_sib = pc(wo)
    up_y = small_y[6, :n_up]
    up_own = jnp.where(ypos == 0, jnp.concatenate((b_up, up_y)), jnp.concatenate((up_y, b_up)))[None, :]
    att_y, att_x, att_s, wo_sib, up_own, u_aa1, go_b1 = phase(att_y, att_x, att_s, wo_sib, up_own, u_aa, go_b)
    att_xy, att_sy, att_sx, up_sib, u_as = px(att_y), pc(att_y), pc(att_x), pc(up_own), pc(u_aa1)
    att_xy, att_sy, att_sx, up_sib, u_as, go_b1, u_ba1 = phase(att_xy, att_sy, att_sx, up_sib, u_as, go_b1, u_ba)
    att_sxy, go_xb = pc(att_xy), px(go_b1)
    mixed, h2t, h2 = call(
        mix_kernel, "mix", (),
        (o0, att_y, att_x, att_xy, att_s, att_sy, att_sx, att_sxy, wo, wo_sib, resid, small, small_y),
        (shape(width, two, dtype=F32), shape(width, two), shape(two, width)), 5,
    )
    u_bs = pc(after(u_ba1, att_sxy))

    held = pltpu.VMEM((width, units), BF)
    four = pltpu.SemaphoreType.DMA((4,))
    u_shape = shape(two, units)
    s_shape = shape(two, units)
    sum_shape = shape(8, units, dtype=F32)
    act0, slope0 = call(
        feed_up_kernel, "feed_up", (), (h2, up_own), (u_shape, s_shape), 3,
        scratch=[held, four], far=(u_aa, u_ba),
    )
    u_bs, go_xb, act0 = phase(u_bs, go_xb, act0)
    act1, slope1 = call(
        feed_up_kernel, "feed_up_sib", (), (h2, up_sib), (u_shape, s_shape), 3,
        scratch=[held, four], far=(u_as, u_bs),
    )
    gof, go = call(
        turn_kernel, "turn", (), (go_a, go_b, go_xa, go_xb), (shape(width, two), shape(two, width)), 2
    )
    d_ba, act1, go = phase(d_ba, act1, go)
    d_bs = pc(d_ba)
    gu0, gu_sums0, gh_part = call(
        feed_own_kernel, "feed_own", (), (go, slope0), (u_shape, sum_shape, shape(width, two, dtype=F32)), 4, vmem=16,
        scratch=[held, held, four], far=(u_aa, u_ba, d_aa, d_ba),
    )
    wide = (units + 127) // 128 * 128
    gu1, gu_sums1, gh_send, gh_own, d_send, u_send = call(
        feed_sib_kernel, "feed_sib", (), (go, slope1, gh_part, act1, h2t, gof),
        (u_shape, sum_shape, shape(width, SUB), shape(width, SUB, dtype=F32), shape(width, wide), shape(width + 16, wide)),
        8, vmem=14, scratch=[held, held, four], far=(u_as, u_bs, d_as, d_bs),
    )
    gh_recv, d_recv, u_recv = px(gh_send), pc(d_send), pc(u_send)
    first = half // 2
    rest = half - first
    second = rest + HALF
    keep0, send0, keep_rest, send_rest = call(
        down_own_kernel, "down_own", (), (gof, act0, d_recv),
        (shape(first, wide, dtype=F32), shape(first, wide), shape(rest, wide, dtype=F32), shape(rest, wide)), 2,
    )
    recv0 = py(send0)
    keep1, send1, keep2, send2 = call(
        up_own_kernel, "up_own", (), (h2t, after(gu0, send0), gu_sums0, u_recv, keep_rest, send_rest),
        (
            shape(second, wide, dtype=F32), shape(second, wide),
            shape(half - HALF + 16, wide, dtype=F32), shape(half - HALF + 16, wide),
        ),
        2,
    )
    gh_recv, send1 = phase(gh_recv, send1)
    gm, low, low_b, g_own, g_sib, g_y, g_x, g_xy, sums2_a, sums2_b = call(
        norm2_back_kernel, "norm2_back", (), (gh_own, gh_recv, mixed, go_a, go_b, small, small_y, wo, wo_sib),
        (shape(width, SUB, dtype=F32), shape(width, SUB), shape(half, SUB))
        + (shape(n2, SUB),) * 2
        + (shape(2 * n2, SUB),) * 3
        + (shape(8, half, dtype=F32),) * 2,
        4,
    )

    def total(keep, recv):
        return (keep + recv.astype(F32)).astype(BF)

    g_x, g_xy, g_y = px(g_x), py(g_xy), py(g_y)
    r_send, r_own = call(
        result_kernel, "result", (), (act0, act1, mixed, small, after(small_y, low)),
        (shape(width, SUB), shape(width, SUB, dtype=F32)), 6, vmem=14,
        scratch=[held, held, four], far=(d_aa, d_ba, d_as, d_bs),
    )
    recv0, r_send, send1 = phase(recv0, r_send, send1)
    p0 = total(keep0, recv0)
    p0_in = line(0, p0)
    g_x, g_xy, g_y, g_sib, p0, send1 = phase(g_x, g_xy, g_y, g_sib, p0, send1)
    recv1 = py(send1)
    g_xy, g_sx, g_sy = px(g_xy), pc(g_x), pc(g_y)
    g_xy, g_sx, g_sy, g_sib, wt_all1, recv1, p0_in, low1, r_send, send2 = phase(
        g_xy, g_sx, g_sy, g_sib, wt_all, recv1, p0_in, low, r_send, send2
    )
    g_s, g_sxy, wt_sib = pc(g_sib), pc(g_xy), pc(wt_all1)
    p0, p1 = line_sum(p0, p0_in), total(keep1, recv1)
    heads = phase(qkv, kv, lo, hi, lse, o0, o1, g_own, g_x, g_y, g_xy, g_s, g_sx, g_sy, g_sxy, p0, p1)
    p0, p1 = heads[-2:]
    p0_in, p1_in, recv2, low_x, r_recv = line(1, p0), line(0, p1), py(send2), px(low1), px(r_send)
    dqkv, dqkv_sib = call(
        attend_back_kernel, "attend_back", (scal, qlo, qhi), heads[:-2], (shape(6 * PITCH, 4 * SUB),) * 2, 19,
        scratch=[
            pltpu.VMEM((2 * PITCH, seq), BF), pltpu.VMEM((2, seq), F32), pltpu.VMEM((2 * PITCH, seq), F32),
            pltpu.VMEM((2, seq, PITCH), F32), pltpu.VMEM((2, seq, PITCH), F32),
        ],
    )
    dqkv, dqkv_sib, p0_in, p1_in, recv2, low_x, r_recv = phase(dqkv, dqkv_sib, p0_in, p1_in, recv2, low_x, r_recv)

    from_sib = pc(dqkv_sib)
    p0, p1, p2 = line_sum(p0, p0_in), line_sum(p1, p1_in), total(keep2, recv2)
    p0_in, p1_in, p2_in = line(2, p0), line(1, p1), line(0, p2)
    keep_o, o_send = call(
        heads_outer_kernel, "heads_outer", (scal,), (o0, att_y, att_s, att_sy, after(low, p0, p1, p2), low_x),
        (shape(2 * n2, width, dtype=F32), shape(2 * n2, width)), 2,
    )
    o_recv = pc(o_send)
    lanes = (half + 127) // 128 * 128
    q_own, q_send = call(
        qkv_outer_kernel, "qkv_outer", (), (dqkv, dqkv_sib, after(h1, o_send)),
        (shape(3 * n2 + 16, lanes), shape(3 * n2, lanes)), 4,
    )
    o_own, o_send = call(
        heads_sum_kernel, "heads_sum", (), (keep_o, after(o_recv, q_own)),
        (shape(2 * n2, lanes, dtype=F32), shape(2 * n2, lanes)), 1,
    )
    o_recv = py(o_send)
    q_send = after(q_send, o_send)
    to_x, keep = call(
        spread_kernel, "spread", (), (w_all, wt_sib, after(dqkv, q_send), from_sib),
        (shape(width, two), shape(width, two, dtype=F32)), 4,
    )
    p0_in, p1_in, p2_in, o_recv, keep, q_send, to_x = phase(p0_in, p1_in, p2_in, o_recv, keep, q_send, to_x)
    (qa,) = call(gather_kernel, "gather", (), (q_own, o_own, o_recv), (shape(5 * n2 + 16, lanes),), 1)
    p1, p2 = line_sum(p1, p1_in), line_sum(p2, p2_in)
    p1_in, p2_in, qa_in, q_recv, from_x = line(2, p1), line(1, p2), line(0, qa), py(q_send), px(to_x)
    g0 = line_end(p0, p0_in)
    r_a, r_b = call(
        result_sum_kernel, "result_sum", (), (r_own, after(r_recv, qa, p1, p2)), (shape(half, SUB), shape(half, SUB)), 1
    )
    p1_in, p2_in, qa_in, q_recv, g0, low_b, r_b = phase(p1_in, p2_in, qa_in, q_recv, g0, low_b, r_b)
    p2, qa, qb = line_sum(p2, p2_in), line_sum(qa, qa_in), q_recv
    p2_in, qa_in, qb_in = line(2, p2), line(1, qa), line(0, qb)
    from_x = after(from_x, p2, qa)
    to_y, own = call(
        spread2_kernel, "spread2", (), (keep, from_x), (shape(half, two), shape(half, two, dtype=F32)), 2,
    )
    from_y, low_y = py(to_y), py(after(low_b, to_y))
    g1 = line_end(p1, p1_in)
    p2_in, qa_in, qb_in, g1 = phase(p2_in, qa_in, qb_in, g1)
    qa, qb = line_sum(qa, qa_in), line_sum(qb, qb_in)
    grad, normed, stats, sums1 = call(
        norm1_stats_kernel, "norm1_stats", (scal,), (own, after(from_y, qa, qb), a00, b00, small, sums2_b),
        (shape(half, two, dtype=F32), shape(half, two, dtype=F32), shape(16, lanes, dtype=F32), shape(8, half, dtype=F32)),
        2,
    )
    qa_in, qb_in, stats_y, r_y = line(2, qa), line(1, qb), py(stats), py(r_b)
    g2 = line_end(p2, p2_in)
    stats_y, r_y, g2 = phase(stats_y, r_y, g2)
    sums = jnp.concatenate((sums1[:2], sums2_a[:4] + stats_y[8:12, :half], sums1[6:]), 0)
    sums_in = [lax.ppermute(sums, "tr", swap_perm("tr", bit)) for bit in (1, 2, 3)]
    (gin,) = call(
        norm1_back_kernel, "norm1_back", (scal,), (grad, normed, stats, stats_y, gm, low_y), (shape(half, two),), 1,
    )
    (result,) = call(place_kernel, "place", (scal,), (r_a, r_y), (shape(half, two),), 1)
    qa_in, qb_in, gin, result, *sums_in = phase(qa_in, qb_in, gin, result, *sums_in)
    sums = (sums + sums_in[0]) + (sums_in[1] + sums_in[2])
    qb = line_sum(qb, qb_in)
    qb_in, sums_in = line(2, qb), [dp_step(sums, bit) for bit in (1, 2, 3)]
    ga = line_end(qa, qa_in)
    qb_in, ga, *sums_in = phase(qb_in, ga, *sums_in)
    sums = dp_last((sums + sums_in[0]) + (sums_in[1] + sums_in[2]))
    dwd, dwu = jnp.concatenate((g0, g1[:rest]), 0), jnp.concatenate((g1[rest:], g2), 0)
    dwq_own, dwq_y, dwo = ga[: 3 * n2 + 16, :half], line_end(qb, qb_in)[:, :half], ga[3 * n2 + 16 :, :half]

    bias_q = dwq_own[3 * n2]
    dwq_own = dwq_own[: 3 * n2]
    first = jnp.where(ypos == 0, dwq_own, dwq_y).reshape(3, n2, half)
    second = jnp.where(ypos == 0, dwq_y, dwq_own).reshape(3, n2, half)
    dwq = jnp.concatenate((first, second), 1)
    gbu = lax.dynamic_slice_in_dim(dwu[half], ypos * n_up, n_up, 0)
    return (
        result.T, gin.T, sums[0], sums[1], dwq[0].T, bias_q[:n2], dwq[1].T, dwq[2].T, bias_q[n2 : 2 * n2],
        dwo, sums[4], sums[2], sums[3], dwu[:half, :units], gbu, dwd[:, :units].T, sums[5],
    )


def solution(mesh):
    rows = P(("dp", "tr"), "tc")
    placed = (
        rows, P("dp"), P("dp"), P("tc"), P("tc"), P("tc", "tr"), P(("tr", "tc")), P("tc", "tr"),
        P("tc", "tr"), P(("tr", "tc")), P("tr", "tc"), P("tc"), P("tc"), P("tc"), P("tc", "tr"),
        P(("tr", "tc")), P("tr", "tc"), P("tc"), rows,
    )
    outs = (
        rows, rows, P("tc"), P("tc"), P("tc", "tr"), P(("tr", "tc")), P("tc", "tr"), P("tc", "tr"),
        P(("tr", "tc")), P("tr", "tc"), P("tc"), P("tc"), P("tc"), P("tc", "tr"), P(("tr", "tc")),
        P("tr", "tc"), P("tc"),
    )
    return jax.shard_map(local, mesh=mesh, in_specs=placed, out_specs=outs, check_vma=False)
```

```python
import jax
import jax.numpy as jnp
from jax import lax
from jax.experimental import pallas as pl
from jax.experimental.pallas import tpu as pltpu
from jax.sharding import PartitionSpec as P

DH = 72
PITCH = 80
SUB = 256
HALF = SUB // 2
EPSILON = 1e-06
GELU_C = 0.7978845608028654
GELU_A = 0.044715
MASKED = -1e30
SCALE = DH**-0.5
SCALE2 = SCALE * 1.4426950408889634
BF = jnp.bfloat16
F32 = jnp.float32
MIB = 1024 * 1024


def swap_perm(axis, bit):
    return [(i, i ^ bit) for i in range(lax.axis_size(axis))]


def px(v):
    return lax.ppermute(v, "tr", swap_perm("tr", 2))


def pc(v):
    return lax.ppermute(v, "tr", swap_perm("tr", 1))


def py(v):
    return lax.ppermute(v, "tc", swap_perm("tc", 1))


def phase(*values):
    return lax.optimization_barrier(values)


def after(v, *earlier):
    return phase(v, *earlier)[0]


def dot(a, b):
    return jnp.dot(a, b, preferred_element_type=F32)


def dot_tn(a, b):
    return lax.dot_general(a, b, (((0,), (0,)), ((), ())), preferred_element_type=F32)


def dot_nt(a, b):
    return lax.dot_general(a, b, (((1,), (1,)), ((), ())), preferred_element_type=F32)


def rows_at(v, first, count):
    return lax.dynamic_slice_in_dim(v, first, count, 0)


def cols_at(v, first, count):
    return lax.dynamic_slice_in_dim(v, first, count, 1)


def dp_swap(v, bit):
    return lax.ppermute(v, "dp", swap_perm("dp", bit))


def line(step, v):
    if lax.axis_size("dp") != 4:
        return v
    return lax.ppermute(v, "dp", ([(0, 1), (3, 2)], [(1, 2), (2, 1)], [(1, 0), (2, 3)])[step])


def line_sum(v, received):
    if lax.axis_size("dp") != 4:
        return v
    return (v.astype(F32) + received.astype(F32)).astype(BF)


def line_end(v, received):
    if lax.axis_size("dp") != 4:
        return lax.psum(v, "dp").astype(F32)
    place = lax.axis_index("dp")
    return jnp.where((place == 1) | (place == 2), v, received).astype(F32)


def dp_step(v, bit):
    return dp_swap(v, bit) if lax.axis_size("dp") == 4 else jnp.zeros_like(v)


def dp_last(v):
    return v if lax.axis_size("dp") == 4 else lax.psum(v, "dp")


VM = pl.BlockSpec(memory_space=pltpu.VMEM)
SM = pl.BlockSpec(memory_space=pltpu.SMEM)


def shape(*dims, dtype=BF):
    return jax.ShapeDtypeStruct(dims, dtype)


ANY = pl.BlockSpec(memory_space=pl.ANY)


def call(body, name, scalars, arrays, outs, us, scratch=(), vmem=12, far=()):
    return pl.pallas_call(
        body,
        out_shape=tuple(outs),
        in_specs=[SM] * len(scalars) + [VM] * len(arrays) + [ANY] * len(far),
        out_specs=tuple([VM] * len(outs)),
        scratch_shapes=list(scratch),
        compiler_params=pltpu.CompilerParams(vmem_limit_bytes=vmem * MIB),
        cost_estimate=pl.CostEstimate(
            flops=int(us * 600e6), bytes_accessed=int(us * 3e6), transcendentals=0
        ),
        name=name,
    )(*scalars, *arrays, *far)


def spots():
    return [(rc, ry, rx) for rc in range(2) for ry in range(2) for rx in range(2)]


def block_of(me, rc, ry, rx):
    return me ^ (rx * 4 + rc * 2 + ry)


def span(block):
    return pl.ds(pl.multiple_of(block * SUB, SUB), SUB)


def head_rows(pos):
    return pl.ds(pl.multiple_of(pos * 2 * DH, 16), 2 * DH)


def row_of(col):
    return jnp.broadcast_to(col, (col.shape[0], 128)).T[0:1]


def column(i, *parts):
    return jnp.concatenate([p[...].T[:, i : i + 1] for p in parts], 0)


def pack_kernel(scal, q, k, v, own, send):
    for i, w in enumerate((q, k, v)):
        there = slice(2 * DH * i, 2 * DH * (i + 1))
        own[there, :] = w[head_rows(scal[0]), :]
        send[there, :] = w[head_rows(1 - scal[0]), :]


def unpack_kernel(own, other, wt, w):
    both = jnp.concatenate((own[...].astype(F32), other[...].astype(F32)), 1)
    gap = jnp.zeros((PITCH - DH, both.shape[1]), F32)
    parts = []
    for i in range(6):
        parts += [both[DH * i : DH * (i + 1)], gap]
    whole = jnp.concatenate(parts, 0).astype(BF)
    wt[...] = whole
    w[...] = whole.T


def norm_qkv_kernel(
    scal, a00, b00, a01, b01, a10, b10, a11, b11, weights, bias, small, small_y,
    h_ref, qkv_ref, kv_ref, res_ref, gain_s, shift_s, bias_s,
):
    ypos, me = scal[0], scal[1]
    half = a00.shape[0]
    gain_s[...] = jnp.broadcast_to(column(0, small, small_y), gain_s.shape)
    shift_s[...] = jnp.broadcast_to(column(1, small, small_y), shift_s.shape)
    bias_s[...] = jnp.broadcast_to(column(0, bias), bias_s.shape)
    sources = {(0, 0): (a00, b00), (1, 0): (a01, b01), (0, 1): (a10, b10), (1, 1): (a11, b11)}
    for p, (rc, ry, rx) in enumerate(spots()):
        here = slice(p * SUB, (p + 1) * SUB)
        there = span(block_of(me, rc, ry, rx))
        cols = span(ypos ^ ry)
        sa, sb = sources[(rc, rx)]
        raw = jnp.concatenate((sa[:, cols], sb[:, cols]), 0)
        if rc == 0 and ry == 0:
            res_ref[:, rx * SUB : (rx + 1) * SUB] = raw
        v = raw.astype(F32)
        mean = jnp.sum(v, axis=0, keepdims=True) / (2 * half)
        square = jnp.sum(v * v, axis=0, keepdims=True) / (2 * half)
        root = lax.rsqrt(square - mean * mean + EPSILON)
        hidden = ((v - mean) * root * gain_s[...] + shift_s[...]).astype(BF)
        h_ref[:, here] = hidden
        qkv = (dot(weights[...], hidden) + bias_s[...]).astype(BF)
        qkv_ref[:, there] = qkv
        for i in range(4):
            kv_ref[there, 128 * i : 128 * i + PITCH] = qkv[PITCH * (2 + i) : PITCH * (3 + i), :].T


def attend_kernel(scal, klo, khi, qkv, kv, lo, hi, o0, o1, lse, s_ref, acc_ref):
    me = scal[1]
    outs = (o0, o1)
    places = lax.broadcasted_iota(jnp.int32, (SUB, SUB), 0)
    lanes = lax.broadcasted_iota(jnp.int32, (1, SUB), 1)
    for rc, ry, rx in sorted(spots(), reverse=True):
        block = block_of(me, rc, ry, rx)
        cols = span(block)
        low, high = lo[:, cols], hi[:, cols]
        own = lanes + block * SUB

        def score(kb, tops):
            base = kb * SUB
            allowed = ((places >= low - base) & (places < high - base)) | (places == own - base)
            new = []
            for h in range(2):
                s = dot(kv[span(kb), 128 * h : 128 * h + PITCH], qkv[PITCH * h : PITCH * (h + 1), cols])
                s = jnp.where(allowed, s, MASKED)
                s_ref[h, span(kb), :] = s
                new.append(jnp.maximum(tops[h], jnp.max(s.reshape(SUB // 8, 8, SUB), axis=0)))
            return tuple(new)

        start = jnp.full((8, SUB), MASKED, F32)
        tops = lax.fori_loop(klo[block], khi[block], score, (start, start))
        tops = [jnp.max(t, axis=0, keepdims=True) * SCALE2 for t in tops]
        acc_ref[...] = jnp.zeros_like(acc_ref)

        def weigh(kb, carry):
            for h in range(2):
                weights = jnp.exp2(s_ref[h, span(kb), :] * SCALE2 - tops[h]).astype(BF)
                acc_ref[h] += dot(qkv[PITCH * (4 + h) : PITCH * (5 + h), span(kb)], weights)
            return carry

        lax.fori_loop(klo[block], khi[block], weigh, 0)
        heads = []
        for h in range(2):
            total = acc_ref[h, DH : DH + 1, :]
            heads.append(acc_ref[h, :DH, :] / total)
            lse[h : h + 1, cols] = tops[h] + jnp.log2(total)
        rows = slice(rc * 2 * DH, (rc + 1) * 2 * DH)
        outs[ry][rows, rx * SUB : (rx + 1) * SUB] = jnp.concatenate(heads, 0).astype(BF)


def attend_back_kernel(
    scal, qlo, qhi, qkv, kv, lo, hi, lse, o0, o1, g0, gx, gy, gxy, s0, sx, sy, sxy,
    out0, out1, gt, delta, dqt, dk, dv,
):
    me = scal[1]
    outs = (o0, o1)
    n2 = 2 * DH
    grads = (g0, gx, gy, gxy, s0, sx, sy, sxy)
    for p, (rc, ry, rx) in enumerate(spots()):
        cols = span(block_of(me, rc, ry, rx))
        rows = slice(rc * n2, (rc + 1) * n2)
        gtile = (grads[p][...] if p in (0, 4) else grads[p][rows, :]).astype(F32)
        both = gtile * outs[ry][rows, rx * SUB : (rx + 1) * SUB].astype(F32)
        for h in range(2):
            part = slice(DH * h, DH * (h + 1))
            padded = jnp.concatenate((gtile[part], jnp.zeros((PITCH - DH, SUB), F32)), 0)
            gt[PITCH * h : PITCH * (h + 1), cols] = padded.astype(BF)
            delta[h : h + 1, cols] = jnp.sum(both[part], axis=0, keepdims=True)
    dqt[...] = jnp.zeros_like(dqt)
    dk[...] = jnp.zeros_like(dk)
    dv[...] = jnp.zeros_like(dv)
    places = lax.broadcasted_iota(jnp.int32, (SUB, SUB), 0)
    lanes = lax.broadcasted_iota(jnp.int32, (1, SUB), 1)

    @pl.loop(0, 8)
    def _(kb):
        keys = span(kb)
        base = kb * SUB

        def body(qb, carry):
            cols = span(qb)
            low, high = lo[:, cols] - base, hi[:, cols] - base
            own = lanes + (qb * SUB - base)
            allowed = ((places >= low) & (places < high)) | (places == own)
            for h in range(2):
                head = slice(PITCH * h, PITCH * (h + 1))
                s = dot(kv[keys, 128 * h : 128 * h + PITCH], qkv[head, cols])
                probs = jnp.where(allowed, jnp.exp2(s * SCALE2 - lse[h : h + 1, cols]), 0.0)
                gprobs = dot(kv[keys, 256 + 128 * h : 256 + 128 * h + PITCH], gt[head, cols])
                gscores = (probs * (gprobs - delta[h : h + 1, cols])).astype(BF)
                dv[h, keys, :] += dot_nt(probs.astype(BF), gt[head, cols])
                dk[h, keys, :] += dot_nt(gscores, qkv[head, cols])
                dqt[head, cols] += dot(qkv[PITCH * (2 + h) : PITCH * (3 + h), keys], gscores)
            return carry

        lax.fori_loop(qlo[kb], qhi[kb], body, 0)

    for p, (rc, ry, rx) in enumerate(spots()):
        out = (out0, out1)[rc]
        here = slice((ry * 2 + rx) * SUB, (ry * 2 + rx + 1) * SUB)
        rows = span(block_of(me, rc, ry, rx))
        out[: 2 * PITCH, here] = (dqt[:, rows] * SCALE).astype(BF)
        for h in range(2):
            out[PITCH * (2 + h) : PITCH * (3 + h), here] = (dk[h, rows, :].T * SCALE).astype(BF)
            out[PITCH * (4 + h) : PITCH * (5 + h), here] = dv[h, rows, :].T.astype(BF)


def own_and_y(ypos, w):
    return [w[head_rows(ypos), :], w[head_rows(1 - ypos), :]]


def out_weights_kernel(scal, own_a, own_b, x_a, x_b, w):
    parts = []
    for a, b in ((own_a, own_b), (x_a, x_b)):
        for wa, wb in zip(own_and_y(scal[0], a), own_and_y(scal[0], b)):
            parts.append(jnp.concatenate((wa, wb), 1))
    w[...] = jnp.concatenate(parts, 0)


def mix_kernel(own, y, x, xy, sib, ysib, xsib, xysib, w, w_sib, res, small, small_y, mixed, h2t, h2):
    n2 = 2 * DH
    gain, shift, bias = [column(i, small, small_y) for i in (2, 3, 4)]
    parts = []
    for rows, group in ((slice(0, n2), (own, y, x, xy)), (slice(n2, 2 * n2), (sib, ysib, xsib, xysib))):
        for i, o in enumerate(group):
            if i < 2:
                parts.append(o[rows, :])
            else:
                parts.append(jnp.concatenate((o[rows, SUB:], o[rows, :SUB]), 1))
    att = jnp.concatenate(parts, 0)
    weights = jnp.concatenate((w[...], w_sib[...]), 0)
    v = res[...].astype(F32) + dot_tn(weights, att) + bias
    mixed[...] = v
    mean = jnp.mean(v, axis=0, keepdims=True)
    root = lax.rsqrt(jnp.mean(v * v, axis=0, keepdims=True) - mean * mean + EPSILON)
    hidden = ((v - mean) * root * gain + shift).astype(BF)
    h2t[...] = hidden
    h2[...] = hidden.T


def turn_kernel(oa, ob, xa, xb, gof, go):
    half = oa.shape[0]
    for rx, (a, b) in enumerate(((oa, ob), (xa, xb))):
        here = slice(rx * SUB, (rx + 1) * SUB)
        gof[:half, here] = a[...]
        gof[half:, here] = b[...]
        go[here, :] = jnp.concatenate((a[...], b[...]), 0).T


def gelu_both(u):
    square = u * u
    tangent = jnp.tanh(GELU_C * (u + GELU_A * square * u))
    plus = 0.5 * (1.0 + tangent)
    slope = plus + 0.5 * u * (1.0 - tangent * tangent) * GELU_C * (1.0 + 3.0 * GELU_A * square)
    return u * plus, slope


def fetch(sources, buffers, sems):
    half = sources[0].shape[0]
    copies = []
    for i, src in enumerate(sources):
        dst = buffers[i // 2].at[pl.ds((i % 2) * half, half), :]
        copies.append(pltpu.make_async_copy(src, dst, sems.at[i]))
        copies[-1].start()
    return copies


def feed_up_kernel(h2, bias, ua, ub, act, slope, u, sems):
    copies = fetch((ua, ub), (u,), sems)
    for c in copies:
        c.wait()
    value, sl = gelu_both(dot(h2[...], u[...]) + bias[...])
    act[...] = value.astype(BF)
    slope[...] = sl.astype(BF)


def feed_grad(go, slope, u, d, copies, gu, sums):
    for c in copies[:2]:
        c.wait()
    rounded = (dot(go[...], d[...]) * slope[...].astype(F32)).astype(BF)
    gu[...] = rounded
    sums[...] = jnp.broadcast_to(jnp.sum(rounded.astype(F32), axis=0, keepdims=True), sums.shape)
    for c in copies[2:]:
        c.wait()
    return dot_nt(u[...], gu[...])


def feed_own_kernel(go, slope, ua, ub, da, db, gu, sums, part, u, d, sems):
    part[...] = feed_grad(go, slope, u, d, fetch((da, db, ua, ub), (d, u), sems), gu, sums)


def feed_sib_kernel(go, slope, part, act, h2t, gof, ua, ub, da, db, gu, sums, send, own, down, up, u, d, sems):
    copies = fetch((da, db, ua, ub), (d, u), sems)
    width, rows = down.shape[1], h2t.shape[0]
    down[...] = padded_units(dot(gof[...], act[...]).astype(BF), width)
    total = feed_grad(go, slope, u, d, copies, gu, sums) + part[...]
    send[...] = total[:, SUB:].astype(BF)
    own[...] = total[:, :SUB]
    up[:rows, :] = padded_units(dot(h2t[...], gu[...]).astype(BF), width)
    up[rows:, :] = padded_units(jnp.concatenate((sums[...], sums[...]), 0).astype(BF), width)


def padded_units(v, width):
    return jnp.concatenate((v, jnp.zeros((v.shape[0], width - v.shape[1]), v.dtype)), 1)


def down_own_kernel(gof, act, recv, keep0, send0, keep_rest, send_rest):
    half, width = recv.shape[0] // 2, recv.shape[1]
    total = padded_units(dot(gof[...], act[...]), width) + recv[...].astype(F32)
    rows = keep0.shape[0]
    keep0[...] = total[:rows]
    keep_rest[...] = total[rows:half]
    send0[...] = total[half : half + rows].astype(BF)
    send_rest[...] = total[half + rows :].astype(BF)


def up_own_kernel(h2t, gu, sums, recv, keep_rest, send_rest, keep1, send1, keep2, send2):
    half = h2t.shape[0] // 2
    width = recv.shape[1]
    total = padded_units(dot(h2t[...], gu[...]), width) + recv[: 2 * half, :].astype(F32)
    more = padded_units(jnp.concatenate((sums[...], sums[...]), 0), width) + recv[2 * half :, :].astype(F32)
    rest = keep_rest.shape[0]
    rows = keep1.shape[0] - rest
    keep1[:rest, :] = keep_rest[...]
    send1[:rest, :] = send_rest[...]
    keep1[rest:, :] = total[:rows]
    send1[rest:, :] = total[half : half + rows].astype(BF)
    keep2[: half - rows, :] = total[rows:half]
    keep2[half - rows :, :] = more
    send2[: half - rows, :] = total[half + rows :].astype(BF)
    send2[half - rows :, :] = more.astype(BF)


def result_kernel(act0, act1, mixed, small, small_y, daa, dba, das, dbs, send, own, d0, d1, sems):
    copies = fetch((daa, dba, das, dbs), (d0, d1), sems)
    for c in copies:
        c.wait()
    part = dot_nt(d0[...], act0[...]) + dot_nt(d1[...], act1[...])
    send[...] = part[:, SUB:].astype(BF)
    own[...] = part[:, :SUB] + mixed[:, :SUB] + column(5, small, small_y)


def result_sum_kernel(own, recv, out_a, out_b):
    half = out_a.shape[0]
    total = (own[...] + recv[: own.shape[0], :].astype(F32)).astype(BF)
    out_a[...] = total[:half]
    out_b[...] = total[half:]


def place_kernel(scal, own, other, out):
    out[:, span(scal[0])] = own[...]
    out[:, span(1 - scal[0])] = other[...]


def norm2_back_kernel(
    own, recv, mixed, goa, gob, small, small_y, w, w_sib, gm, low, low_b, g_own, g_sib, g_y, g_x, g_xy, sums_a, sums_b
):
    e = own[...] + recv[...].astype(F32)
    v = mixed[:, :SUB]
    mean = jnp.mean(v, axis=0, keepdims=True)
    root = lax.rsqrt(jnp.mean(v * v, axis=0, keepdims=True) - mean * mean + EPSILON)
    n = (v - mean) * root
    weighted = e * column(2, small, small_y)
    go = jnp.concatenate((goa[...], gob[...]), 0).astype(F32)
    grad = go + root * (
        weighted
        - jnp.mean(weighted, axis=0, keepdims=True)
        - n * jnp.mean(weighted * n, axis=0, keepdims=True)
    )
    gm[...] = grad
    rounded = grad.astype(BF)
    low[...] = rounded
    low_b[...] = rounded[low_b.shape[0] :]
    n2 = 2 * DH
    mine = dot(w[...], rounded).astype(BF)
    sibs = dot(w_sib[...], rounded).astype(BF)
    g_own[...] = mine[:n2]
    g_sib[...] = sibs[:n2]
    for i, out in enumerate((g_y, g_x, g_xy)):
        rows = slice(n2 * (i + 1), n2 * (i + 2))
        out[:n2, :] = mine[rows]
        out[n2:, :] = sibs[rows]
    for i, q in enumerate((e * n, e, grad, go)):
        col = jnp.sum(q, axis=1, keepdims=True)
        half = low_b.shape[0]
        sums_a[i : i + 1, :] = row_of(col[:half])
        sums_b[i : i + 1, :] = row_of(col[half:])
    sums_a[4:, :] = jnp.zeros_like(sums_a[4:, :])
    sums_b[4:, :] = jnp.zeros_like(sums_b[4:, :])


def heads_outer_kernel(scal, own, y, sib, ysib, low, low_x, keep, send):
    right = jnp.concatenate((low[...], low_x[...]), 1)
    n2 = 2 * DH
    for rows, a, b, out in ((slice(0, n2), own, y, keep), (slice(n2, 2 * n2), sib, ysib, send)):
        out[head_rows(scal[0]), :] = dot_nt(a[rows, :], right).astype(out.dtype)
        out[head_rows(1 - scal[0]), :] = dot_nt(b[rows, :], right).astype(out.dtype)


def gather_kernel(q_own, o_own, o_recv, out):
    n = q_own.shape[0]
    out[:n, :] = q_own[...]
    out[n:, :] = (o_own[...] + o_recv[...].astype(F32)).astype(BF)


def qkv_outer_kernel(dqkv, dqkv_sib, h1, own, send):
    mid = dqkv.shape[1]
    total = dot_nt(dqkv[...], h1[:, :mid]) + dot_nt(dqkv_sib[...], h1[:, mid:])
    half = h1.shape[0] // 2
    lanes = own.shape[1]
    rows = jnp.concatenate([total[PITCH * i : PITCH * i + DH] for i in range(6)], 0)
    n = 6 * DH
    own[:n, :] = padded_units(rows[:, :half].astype(BF), lanes)
    send[...] = padded_units(rows[:, half:].astype(BF), lanes)
    col = jnp.sum(dqkv[...].astype(F32) + dqkv_sib[...].astype(F32), axis=1, keepdims=True)
    cols = [col[PITCH * i : PITCH * i + DH] for i in (0, 1, 4, 5)]
    cols.append(jnp.zeros((lanes - 4 * DH, 1), F32))
    own[n:, :] = jnp.broadcast_to(row_of(jnp.concatenate(cols, 0)), (16, lanes)).astype(BF)


def heads_sum_kernel(keep, recv, own, send):
    half = keep.shape[1] // 2
    total = keep[...] + recv[...].astype(F32)
    own[...] = padded_units(total[:, :half], own.shape[1])
    send[...] = padded_units(total[:, half:].astype(BF), send.shape[1])


def spread_kernel(w, wt_sib, dqkv, from_sib, to_x, keep):
    total = dot(w[...], dqkv[...]) + dot_tn(wt_sib[...], from_sib[...])
    for ry in range(2):
        first = 2 * ry * SUB
        at = slice(ry * SUB, (ry + 1) * SUB)
        keep[:, at] = total[:, first : first + SUB]
        to_x[:, at] = total[:, first + SUB : first + 2 * SUB].astype(BF)


def spread2_kernel(keep, from_x, to_y, own):
    half = own.shape[0]
    total = keep[...] + from_x[...].astype(F32)
    own[...] = total[:half]
    to_y[...] = total[half:].astype(BF)


def norm1_stats_kernel(scal, own, from_y, a, b, small, sums_b, grad, normed, stats, sums):
    ypos = scal[0]
    half = a.shape[0]
    gain = column(0, small)
    cols_sums = [0.0, 0.0]
    stats[...] = jnp.zeros_like(stats)
    for ry in range(2):
        cols = span(ypos ^ ry)
        here = slice(ry * SUB, (ry + 1) * SUB)
        e = own[:, here] + from_y[:, (1 - ry) * SUB : (2 - ry) * SUB].astype(F32)
        va, vb = a[:, cols].astype(F32), b[:, cols].astype(F32)
        mean = (jnp.sum(va, 0, keepdims=True) + jnp.sum(vb, 0, keepdims=True)) / (2 * half)
        square = (jnp.sum(va * va, 0, keepdims=True) + jnp.sum(vb * vb, 0, keepdims=True)) / (2 * half)
        root = lax.rsqrt(square - mean * mean + EPSILON)
        n = (va - mean) * root
        w = e * gain
        grad[:, here] = w
        normed[:, here] = n
        stats[0:1, here] = jnp.sum(w, 0, keepdims=True)
        stats[1:2, here] = jnp.sum(w * n, 0, keepdims=True)
        stats[2:3, here] = root
        cols_sums[0] += jnp.sum(e * n, 1, keepdims=True)
        cols_sums[1] += jnp.sum(e, 1, keepdims=True)
    stats[8:, :half] = sums_b[...]
    for i in range(2):
        sums[i : i + 1, :] = row_of(cols_sums[i])
    sums[2:, :] = jnp.zeros_like(sums[2:, :])


def norm1_back_kernel(scal, grad, normed, stats, recv, gm_own, gm_y, out):
    ypos = scal[0]
    width = 2 * grad.shape[0]
    for ry in range(2):
        here = slice(ry * SUB, (ry + 1) * SUB)
        other = slice((1 - ry) * SUB, (2 - ry) * SUB)
        total = (stats[0:1, here] + recv[0:1, other]) / width
        along = (stats[1:2, here] + recv[1:2, other]) / width
        gm = gm_own[: grad.shape[0], :] if ry == 0 else gm_y[...].astype(F32)
        whole = gm + stats[2:3, here] * (grad[:, here] - total - normed[:, here] * along)
        out[:, span(ypos ^ ry)] = whole.astype(BF)


def local(
    layer_input, picture, token_kept, ln1_gain, ln1_bias, w_query, b_query, w_key, w_value, b_value,
    w_out, b_out, ln2_gain, ln2_bias, w_up, b_up, w_down, b_down, grad_out,
):
    ypos = lax.axis_index("tc").astype(jnp.int32)
    trpos = lax.axis_index("tr").astype(jnp.int32)
    me = trpos * 2 + ypos
    half = layer_input.shape[1]
    width = 2 * half
    seq = picture.shape[0]
    n2 = b_query.shape[0]
    units = w_up.shape[1]
    n_up = b_up.shape[0]
    scal = jnp.stack((ypos, me))
    two = 2 * SUB

    a00 = layer_input.T
    qkv_weights = (w_query.T, w_key.T, w_value.T)
    go_t = grad_out.T
    u_aa, d_aa = w_up, w_down.T
    small = jnp.stack(
        (ln1_gain, ln1_bias, ln2_gain, ln2_bias, b_out, b_down, jnp.pad(b_up, (0, half - n_up)), ln1_gain)
    )
    w_own, w_send = call(pack_kernel, "pack", (scal,), qkv_weights, (shape(3 * n2, half),) * 2, 1)
    b00, a10, a01, small_y, d_as = py(a00), px(a00), pc(a00), py(small), pc(d_aa)
    go_a = cols_at(go_t, ypos * SUB, SUB)
    go_send = cols_at(go_t, (1 - ypos) * SUB, SUB)
    quarter = half // lax.axis_size("dp")
    first = lax.axis_index("dp") * quarter
    u_part, d_part = rows_at(u_aa, first, quarter), rows_at(d_aa, first, quarter)
    qkv_bias = jnp.concatenate((b_query, jnp.zeros_like(b_query), b_value)).reshape(6, DH)
    ones = (jnp.arange(6) >= 4).astype(F32)[:, None]
    qkv_bias = jnp.concatenate((qkv_bias, ones, jnp.zeros((6, PITCH - DH - 1), F32)), 1).reshape(1, -1)
    qkv_bias = jnp.broadcast_to(qkv_bias, (8, 6 * PITCH))

    numbers = jnp.arange(8, dtype=jnp.int32)[:, None]
    hot = (picture[None, :] == numbers).astype(jnp.int32)
    counts = jnp.sum(hot, axis=1)
    kept = jnp.sum(hot * token_kept[None, :], axis=1)
    starts = jnp.cumsum(counts) - counts
    lo = jnp.sum(hot * starts[:, None], axis=0)
    hi = jnp.sum(hot * (starts + kept)[:, None], axis=0)
    end = jnp.sum(hot * (starts + counts)[:, None], axis=0)
    blocks = seq // SUB
    klo = qlo = lo.reshape(blocks, SUB)[:, 0] // SUB
    lasts = jnp.arange(1, blocks + 1, dtype=jnp.int32) * SUB
    khi = (jnp.maximum(lasts, hi.reshape(blocks, SUB)[:, -1]) + SUB - 1) // SUB
    qhi = (jnp.maximum(lasts, end.reshape(blocks, SUB)[:, -1]) + SUB - 1) // SUB
    lo, hi = lo[None, :], hi[None, :]

    b00, a10, a01, small_y, d_as, w_send, u_part = phase(b00, a10, a01, small_y, d_as, w_send, u_part)
    b10, w_other, b01, a11, u_part = px(b00), py(w_send), pc(b00), pc(a10), py(u_part)
    b10, w_other, b01, a11, u_part, w_out1, go_send, go_a, d_part = phase(
        b10, w_other, b01, a11, u_part, w_out, go_send, go_a, d_part
    )
    u_ba = lax.all_gather(u_part, "dp", axis=0, tiled=True)
    b11, w0b, w2a, go_b, d_part = pc(b10), py(w_out1), px(w_out1), py(go_send), py(d_part)
    wt_all, w_all = call(
        unpack_kernel, "unpack", (), (w_own, w_other),
        (shape(6 * PITCH, width), shape(width, 6 * PITCH)), 2,
    )
    h1, qkv, kv, resid = call(
        norm_qkv_kernel, "norm_qkv", (scal,),
        (a00, b00, a01, b01, a10, b10, a11, b11, wt_all, qkv_bias, small, small_y),
        (shape(width, seq), shape(6 * PITCH, seq), shape(seq, 512), shape(width, two)),
        8,
        scratch=[pltpu.VMEM((width, SUB), F32)] * 2 + [pltpu.VMEM((6 * PITCH, SUB), F32)],
    )

    qkv, w2a = phase(qkv, w2a)
    w2b, go_xa = py(w2a), px(after(go_a, w2a))

    o0, o1, lse = call(
        attend_kernel, "attend", (scal, klo, khi), (qkv, kv, lo, hi),
        (shape(2 * n2, two),) * 2 + (shape(2, seq, dtype=F32),), 12,
        scratch=[pltpu.VMEM((2, seq, SUB), F32), pltpu.VMEM((2, PITCH, SUB), F32)],
    )
    o0, o1, w0b, w2b, go_b, go_xa, d_part, u_ba = phase(o0, o1, w0b, w2b, go_b, go_xa, d_part, u_ba)
    d_ba = lax.all_gather(d_part, "dp", axis=0, tiled=True)
    att_y, att_x, att_s = py(o1), px(o0), pc(o0)
    (wo,) = call(out_weights_kernel, "out_weights", (scal,), (w_out, w0b, w2a, w2b), (shape(4 * n2, width),), 1)
    wo_sib = pc(wo)
    up_y = small_y[6, :n_up]
    up_own = jnp.where(ypos == 0, jnp.concatenate((b_up, up_y)), jnp.concatenate((up_y, b_up)))[None, :]
    att_y, att_x, att_s, wo_sib, up_own, u_aa1, go_b1 = phase(att_y, att_x, att_s, wo_sib, up_own, u_aa, go_b)
    att_xy, att_sy, att_sx, up_sib, u_as = px(att_y), pc(att_y), pc(att_x), pc(up_own), pc(u_aa1)
    att_xy, att_sy, att_sx, up_sib, u_as, go_b1, u_ba1 = phase(att_xy, att_sy, att_sx, up_sib, u_as, go_b1, u_ba)
    att_sxy, go_xb = pc(att_xy), px(go_b1)
    mixed, h2t, h2 = call(
        mix_kernel, "mix", (),
        (o0, att_y, att_x, att_xy, att_s, att_sy, att_sx, att_sxy, wo, wo_sib, resid, small, small_y),
        (shape(width, two, dtype=F32), shape(width, two), shape(two, width)), 5,
    )
    u_bs = pc(after(u_ba1, att_sxy))

    held = pltpu.VMEM((width, units), BF)
    four = pltpu.SemaphoreType.DMA((4,))
    u_shape = shape(two, units)
    s_shape = shape(two, units)
    sum_shape = shape(8, units, dtype=F32)
    act0, slope0 = call(
        feed_up_kernel, "feed_up", (), (h2, up_own), (u_shape, s_shape), 3,
        scratch=[held, four], far=(u_aa, u_ba),
    )
    u_bs, go_xb, act0 = phase(u_bs, go_xb, act0)
    act1, slope1 = call(
        feed_up_kernel, "feed_up_sib", (), (h2, up_sib), (u_shape, s_shape), 3,
        scratch=[held, four], far=(u_as, u_bs),
    )
    gof, go = call(
        turn_kernel, "turn", (), (go_a, go_b, go_xa, go_xb), (shape(width, two), shape(two, width)), 2
    )
    d_ba, act1, go = phase(d_ba, act1, go)
    d_bs = pc(d_ba)
    gu0, gu_sums0, gh_part = call(
        feed_own_kernel, "feed_own", (), (go, slope0), (u_shape, sum_shape, shape(width, two, dtype=F32)), 4, vmem=16,
        scratch=[held, held, four], far=(u_aa, u_ba, d_aa, d_ba),
    )
    wide = (units + 127) // 128 * 128
    gu1, gu_sums1, gh_send, gh_own, d_send, u_send = call(
        feed_sib_kernel, "feed_sib", (), (go, slope1, gh_part, act1, h2t, gof),
        (u_shape, sum_shape, shape(width, SUB), shape(width, SUB, dtype=F32), shape(width, wide), shape(width + 16, wide)),
        8, vmem=14, scratch=[held, held, four], far=(u_as, u_bs, d_as, d_bs),
    )
    gh_recv, d_recv, u_recv = px(gh_send), pc(d_send), pc(u_send)
    first = half // 2
    rest = half - first
    more = HALF + 32
    second = rest + more
    keep0, send0, keep_rest, send_rest = call(
        down_own_kernel, "down_own", (), (gof, act0, d_recv),
        (shape(first, wide, dtype=F32), shape(first, wide), shape(rest, wide, dtype=F32), shape(rest, wide)), 2,
    )
    recv0 = py(send0)
    keep1, send1, keep2, send2 = call(
        up_own_kernel, "up_own", (), (h2t, after(gu0, send0), gu_sums0, u_recv, keep_rest, send_rest),
        (
            shape(second, wide, dtype=F32), shape(second, wide),
            shape(half - more + 16, wide, dtype=F32), shape(half - more + 16, wide),
        ),
        2,
    )
    gh_recv, send1 = phase(gh_recv, send1)
    gm, low, low_b, g_own, g_sib, g_y, g_x, g_xy, sums2_a, sums2_b = call(
        norm2_back_kernel, "norm2_back", (), (gh_own, gh_recv, mixed, go_a, go_b, small, small_y, wo, wo_sib),
        (shape(width, SUB, dtype=F32), shape(width, SUB), shape(half, SUB))
        + (shape(n2, SUB),) * 2
        + (shape(2 * n2, SUB),) * 3
        + (shape(8, half, dtype=F32),) * 2,
        4,
    )

    def total(keep, recv):
        return (keep + recv.astype(F32)).astype(BF)

    g_x, g_xy, g_y = px(g_x), py(g_xy), py(g_y)
    r_send, r_own = call(
        result_kernel, "result", (), (act0, act1, mixed, small, after(small_y, low)),
        (shape(width, SUB), shape(width, SUB, dtype=F32)), 6, vmem=14,
        scratch=[held, held, four], far=(d_aa, d_ba, d_as, d_bs),
    )
    recv0, r_send, send1 = phase(recv0, r_send, send1)
    p0 = total(keep0, recv0)
    p0_in = line(0, p0)
    g_x, g_xy, g_y, g_sib, p0, send1 = phase(g_x, g_xy, g_y, g_sib, p0, send1)
    recv1 = py(send1)
    g_xy, g_sx, g_sy = px(g_xy), pc(g_x), pc(g_y)
    g_xy, g_sx, g_sy, g_sib, wt_all1, recv1, p0_in, low1, r_send, send2 = phase(
        g_xy, g_sx, g_sy, g_sib, wt_all, recv1, p0_in, low, r_send, send2
    )
    g_s, g_sxy, wt_sib = pc(g_sib), pc(g_xy), pc(wt_all1)
    p0, p1 = line_sum(p0, p0_in), total(keep1, recv1)
    heads = phase(qkv, kv, lo, hi, lse, o0, o1, g_own, g_x, g_y, g_xy, g_s, g_sx, g_sy, g_sxy, p0, p1)
    p0, p1 = heads[-2:]
    p0_in, p1_in, recv2, low_x, r_recv = line(1, p0), line(0, p1), py(send2), px(low1), px(r_send)
    dqkv, dqkv_sib = call(
        attend_back_kernel, "attend_back", (scal, qlo, qhi), heads[:-2], (shape(6 * PITCH, 4 * SUB),) * 2, 19,
        scratch=[
            pltpu.VMEM((2 * PITCH, seq), BF), pltpu.VMEM((2, seq), F32), pltpu.VMEM((2 * PITCH, seq), F32),
            pltpu.VMEM((2, seq, PITCH), F32), pltpu.VMEM((2, seq, PITCH), F32),
        ],
    )
    dqkv, dqkv_sib, p0_in, p1_in, recv2, low_x, r_recv = phase(dqkv, dqkv_sib, p0_in, p1_in, recv2, low_x, r_recv)

    from_sib = pc(dqkv_sib)
    p0, p1, p2 = line_sum(p0, p0_in), line_sum(p1, p1_in), total(keep2, recv2)
    p0_in, p1_in, p2_in = line(2, p0), line(1, p1), line(0, p2)
    keep_o, o_send = call(
        heads_outer_kernel, "heads_outer", (scal,), (o0, att_y, att_s, att_sy, after(low, p0, p1, p2), low_x),
        (shape(2 * n2, width, dtype=F32), shape(2 * n2, width)), 2,
    )
    o_recv = pc(o_send)
    lanes = (half + 127) // 128 * 128
    q_own, q_send = call(
        qkv_outer_kernel, "qkv_outer", (), (dqkv, dqkv_sib, after(h1, o_send)),
        (shape(3 * n2 + 16, lanes), shape(3 * n2, lanes)), 4,
    )
    o_own, o_send = call(
        heads_sum_kernel, "heads_sum", (), (keep_o, after(o_recv, q_own)),
        (shape(2 * n2, lanes, dtype=F32), shape(2 * n2, lanes)), 1,
    )
    o_recv = py(o_send)
    q_send = after(q_send, o_send)
    to_x, keep = call(
        spread_kernel, "spread", (), (w_all, wt_sib, after(dqkv, q_send), from_sib),
        (shape(width, two), shape(width, two, dtype=F32)), 4,
    )
    p0_in, p1_in, p2_in, o_recv, keep, q_send, to_x = phase(p0_in, p1_in, p2_in, o_recv, keep, q_send, to_x)
    (qa,) = call(gather_kernel, "gather", (), (q_own, o_own, o_recv), (shape(5 * n2 + 16, lanes),), 1)
    p1, p2 = line_sum(p1, p1_in), line_sum(p2, p2_in)
    p1_in, p2_in, qa_in, q_recv, from_x = line(2, p1), line(1, p2), line(0, qa), py(q_send), px(to_x)
    g0 = line_end(p0, p0_in)
    r_a, r_b = call(
        result_sum_kernel, "result_sum", (), (r_own, after(r_recv, qa, p1, p2)), (shape(half, SUB), shape(half, SUB)), 1
    )
    p1_in, p2_in, qa_in, q_recv, g0, low_b, r_b = phase(p1_in, p2_in, qa_in, q_recv, g0, low_b, r_b)
    p2, qa, qb = line_sum(p2, p2_in), line_sum(qa, qa_in), q_recv
    p2_in, qa_in, qb_in = line(2, p2), line(1, qa), line(0, qb)
    from_x = after(from_x, p2, qa)
    to_y, own = call(
        spread2_kernel, "spread2", (), (keep, from_x), (shape(half, two), shape(half, two, dtype=F32)), 2,
    )
    from_y, low_y = py(to_y), py(after(low_b, to_y))
    g1 = line_end(p1, p1_in)
    p2_in, qa_in, qb_in, g1 = phase(p2_in, qa_in, qb_in, g1)
    qa, qb = line_sum(qa, qa_in), line_sum(qb, qb_in)
    grad, normed, stats, sums1 = call(
        norm1_stats_kernel, "norm1_stats", (scal,), (own, after(from_y, qa, qb), a00, b00, small, sums2_b),
        (shape(half, two, dtype=F32), shape(half, two, dtype=F32), shape(16, lanes, dtype=F32), shape(8, half, dtype=F32)),
        2,
    )
    qa_in, qb_in, stats_y, r_y = line(2, qa), line(1, qb), py(stats), py(r_b)
    g2 = line_end(p2, p2_in)
    stats_y, r_y, g2 = phase(stats_y, r_y, g2)
    sums = jnp.concatenate((sums1[:2], sums2_a[:4] + stats_y[8:12, :half], sums1[6:]), 0)
    sums_in = [lax.ppermute(sums, "tr", swap_perm("tr", bit)) for bit in (1, 2, 3)]
    (gin,) = call(
        norm1_back_kernel, "norm1_back", (scal,), (grad, normed, stats, stats_y, gm, low_y), (shape(half, two),), 1,
    )
    (result,) = call(place_kernel, "place", (scal,), (r_a, r_y), (shape(half, two),), 1)
    qa_in, qb_in, gin, result, *sums_in = phase(qa_in, qb_in, gin, result, *sums_in)
    sums = (sums + sums_in[0]) + (sums_in[1] + sums_in[2])
    qb = line_sum(qb, qb_in)
    qb_in, sums_in = line(2, qb), [dp_step(sums, bit) for bit in (1, 2, 3)]
    ga = line_end(qa, qa_in)
    qb_in, ga, *sums_in = phase(qb_in, ga, *sums_in)
    sums = dp_last((sums + sums_in[0]) + (sums_in[1] + sums_in[2]))
    dwd, dwu = jnp.concatenate((g0, g1[:rest]), 0), jnp.concatenate((g1[rest:], g2), 0)
    dwq_own, dwq_y, dwo = ga[: 3 * n2 + 16, :half], line_end(qb, qb_in)[:, :half], ga[3 * n2 + 16 :, :half]

    bias_q = dwq_own[3 * n2]
    dwq_own = dwq_own[: 3 * n2]
    first = jnp.where(ypos == 0, dwq_own, dwq_y).reshape(3, n2, half)
    second = jnp.where(ypos == 0, dwq_y, dwq_own).reshape(3, n2, half)
    dwq = jnp.concatenate((first, second), 1)
    gbu = lax.dynamic_slice_in_dim(dwu[half], ypos * n_up, n_up, 0)
    return (
        result.T, gin.T, sums[0], sums[1], dwq[0].T, bias_q[:n2], dwq[1].T, dwq[2].T, bias_q[n2 : 2 * n2],
        dwo, sums[4], sums[2], sums[3], dwu[:half, :units], gbu, dwd[:, :units].T, sums[5],
    )


def solution(mesh):
    rows = P(("dp", "tr"), "tc")
    placed = (
        rows, P("dp"), P("dp"), P("tc"), P("tc"), P("tc", "tr"), P(("tr", "tc")), P("tc", "tr"),
        P("tc", "tr"), P(("tr", "tc")), P("tr", "tc"), P("tc"), P("tc"), P("tc"), P("tc", "tr"),
        P(("tr", "tc")), P("tr", "tc"), P("tc"), rows,
    )
    outs = (
        rows, rows, P("tc"), P("tc"), P("tc", "tr"), P(("tr", "tc")), P("tc", "tr"), P("tc", "tr"),
        P(("tr", "tc")), P("tr", "tc"), P("tc"), P("tc"), P("tc"), P("tc", "tr"), P(("tr", "tc")),
        P("tr", "tc"), P("tc"),
    )
    return jax.shard_map(local, mesh=mesh, in_specs=placed, out_specs=outs, check_vma=False)
```
